32 devices in a mesh: ctx: 4 (over z), fsdp: 8 (over y, x, core).
Axes of the slice: x: 2, y: 2, z: 4, core: 2. Of those that a mesh axis runs over, the one named last changes fastest.
Arguments:
- tokens: bfloat16 [8, 512, 1536], P('fsdp', 'ctx'), may hold values from -6 to 6
- positions: int32 [8, 512], P('fsdp', 'ctx'), may hold values from 0 to 511, as said below
- norm1_gain: bfloat16 [1536], P(('ctx', 'fsdp')), may hold values from 0.5 to 1.5
- q_weight: bfloat16 [1536, 1536], P(('ctx', 'fsdp')), may hold values from -0.15625 to 0.15625
- q_bias: bfloat16 [1536], P(('ctx', 'fsdp')), may hold values from -3 to 3
- key_projection: bfloat16 [1536, 256], P(('ctx', 'fsdp')), may hold values from -0.15625 to 0.15625
- key_bias_vector: bfloat16 [256], P(('ctx', 'fsdp')), may hold values from -3 to 3
- value_projection: bfloat16 [1536, 256], P(('ctx', 'fsdp')), may hold values from -0.15625 to 0.15625
- value_bias_vector: bfloat16 [256], P(('ctx', 'fsdp')), may hold values from -0.59765625 to 0.59765625
- o_weight: bfloat16 [1536, 1536], P(('ctx', 'fsdp')), may hold values from -0.625 to 0.625
- norm2_gain: bfloat16 [1536], P(('ctx', 'fsdp')), may hold values from 0.5 to 1.5
- gate_weight: bfloat16 [1536, 8960], P(('ctx', 'fsdp')), may hold values from -0.15625 to 0.15625
- up_weight: bfloat16 [1536, 8960], P(('ctx', 'fsdp')), may hold values from -0.15625 to 0.15625
- down_weight: bfloat16 [8960, 1536], P(None, ('ctx', 'fsdp')), may hold values from -0.0625 to 0.0625
- cotangent: bfloat16 [8, 512, 1536], P('fsdp', 'ctx'), may hold values from -6 to 6
Outputs:
- layer_out: float32 [8, 512, 1536], P('fsdp', 'ctx')
- grad_tokens: float32 [8, 512, 1536], P('fsdp', 'ctx')
- grad_norm1_gain: float32 [1536], P(('ctx', 'fsdp'))
- grad_q_weight: float32 [1536, 1536], P('fsdp', 'ctx')
- grad_q_bias: float32 [1536], P(('ctx', 'fsdp'))
- grad_k_weight: float32 [1536, 256], P('fsdp', 'ctx')
- grad_k_bias: float32 [256], P(('ctx', 'fsdp'))
- grad_v_weight: float32 [1536, 256], P('fsdp', 'ctx')
- grad_v_bias: float32 [256], P(('ctx', 'fsdp'))
- grad_o_weight: float32 [1536, 1536], P('fsdp', 'ctx')
- grad_norm2_gain: float32 [1536], P(('ctx', 'fsdp'))
- grad_gate_weight: float32 [1536, 8960], P('fsdp', 'ctx')
- grad_up_weight: float32 [1536, 8960], P('fsdp', 'ctx')
- grad_down_weight: float32 [8960, 1536], P('ctx', 'fsdp')
The draws below stay inside these ranges and needn't reach their ends.
Inputs may be any that keep to these rules, and one draw needn't show every extreme that they name: `positions`: each row of 512 tokens is split into one to four documents at points drawn at random; a token's position counts from 0 at the first token of its document, so documents never cross rows; in every draw one row is a single document.
All inputs are finite; a program needn't handle non-finite values.
Results may differ from the reference program's by a relative error of at most 0.03.
Values may be sent and summed in bfloat16 or wider, within the bound.
No kernel may reach another device: no remote copies, remote signals or barrier semaphores. Data moves between devices by JAX's collectives and lax.ppermute only.
A program may use at most 256 MiB of HBM per device.

```python
import jax
import jax.numpy as jnp
from jax import lax

MODEL_WIDTH = 1536
QUERY_HEADS = 12
KEY_VALUE_HEADS = 2
HEAD_SIZE = 128
FF = 8960
ROW_TOKENS = 512
BLOCKS = 8


def draw_positions(key, part):
    cut_key = jax.random.fold_in(key, 11)
    pick_key = jax.random.fold_in(key, 12)
    cut_points = jax.random.randint(cut_key, (BLOCKS, 3), 1, ROW_TOKENS)
    single = jax.random.randint(pick_key, (), 0, BLOCKS)
    row_index = jnp.arange(BLOCKS)[:, None]
    cut_points = jnp.where(row_index == single, ROW_TOKENS, cut_points)
    places = jnp.arange(ROW_TOKENS)
    starts = jnp.max(jnp.where(cut_points[:, None, :] <= places[None, :, None], cut_points[:, None, :], 0), axis=-1)
    return (places[None, :] - starts).astype(jnp.int32)


def block_scale(rng, dims, cuts, smallest, top_value):
    level, own = 1.0, jax.random.fold_in(rng, 6)
    for position, shards_of in cuts:
        steps = jnp.exp(jax.random.uniform(jax.random.fold_in(own, position), (shards_of,), jnp.float32, smallest / len(cuts), top_value / len(cuts)))
        level = level * jnp.repeat(steps, dims[position] // shards_of).reshape([-1 if axis == position else 1 for axis in range(len(dims))])
    return level


def scatter_about(stream_key, shape, spread, reach, split=(), kind=jnp.bfloat16):
    drawn = jax.random.normal(stream_key, shape, jnp.float32) * spread
    if len(split) > 0:
        drawn = block_scale(stream_key, shape, split, -0.22, 0.18) * drawn
    return jnp.clip(drawn, min=-reach, max=reach).astype(kind)


def setup_inputs(seed: int = 0) -> dict:
    keys = jax.random.split(jax.random.key(seed), 16)
    tokens = scatter_about(keys[0], (BLOCKS, ROW_TOKENS, MODEL_WIDTH), 1.0, 6.0, ((0, 8), (1, 4)))
    positions = draw_positions(jax.random.fold_in(keys[15], 71), 0)
    norm1_gain = jnp.clip(1.0 + 0.1 * jax.random.normal(keys[2], (MODEL_WIDTH,), jnp.float32), 0.5, 1.5).astype(jnp.bfloat16)
    q_weight = scatter_about(keys[3], (MODEL_WIDTH, QUERY_HEADS * HEAD_SIZE), MODEL_WIDTH ** -0.5, 0.15625, ((0, 32),))
    q_bias = scatter_about(keys[4], (QUERY_HEADS * HEAD_SIZE,), 0.5, 3.0, ((0, 32),))
    key_projection = scatter_about(keys[5], (MODEL_WIDTH, KEY_VALUE_HEADS * HEAD_SIZE), MODEL_WIDTH ** -0.5, 0.15625, ((0, 32),))
    key_bias_vector = scatter_about(keys[6], (KEY_VALUE_HEADS * HEAD_SIZE,), 0.5, 3.0, ((0, 32),))
    value_projection = scatter_about(keys[7], (MODEL_WIDTH, KEY_VALUE_HEADS * HEAD_SIZE), MODEL_WIDTH ** -0.5, 0.15625, ((0, 32),))
    value_bias_vector = scatter_about(keys[8], (KEY_VALUE_HEADS * HEAD_SIZE,), 0.1, 0.59765625, ((0, 32),))
    o_weight = scatter_about(keys[9], (QUERY_HEADS * HEAD_SIZE, MODEL_WIDTH), (QUERY_HEADS * HEAD_SIZE // 16) ** -0.5, 0.625, ((0, 32),))
    norm2_gain = jnp.clip(1.0 + 0.1 * jax.random.normal(keys[10], (MODEL_WIDTH,), jnp.float32), 0.5, 1.5).astype(jnp.bfloat16)
    gate_weight = scatter_about(keys[11], (MODEL_WIDTH, FF), MODEL_WIDTH ** -0.5, 0.15625, ((0, 32),))
    up_weight = scatter_about(keys[12], (MODEL_WIDTH, FF), MODEL_WIDTH ** -0.5, 0.15625, ((0, 32),))
    down_weight = scatter_about(keys[13], (FF, MODEL_WIDTH), FF ** -0.5, 0.0625, ((1, 32),))
    cotangent = scatter_about(keys[14], (BLOCKS, ROW_TOKENS, MODEL_WIDTH), 1.0, 6.0, ((0, 8), (1, 4)))
    return dict(tokens=tokens, positions=positions, norm1_gain=norm1_gain, q_weight=q_weight, q_bias=q_bias, key_projection=key_projection, key_bias_vector=key_bias_vector, value_projection=value_projection, value_bias_vector=value_bias_vector, o_weight=o_weight, norm2_gain=norm2_gain, gate_weight=gate_weight, up_weight=up_weight, down_weight=down_weight, cotangent=cotangent)


@jax.custom_vjp
def low(v):
    return lax.optimization_barrier(v.astype(jnp.bfloat16)).astype(jnp.float32)

@jax.custom_vjp
def low_back(v):
    return v

def low_keep(v):
    return (low(v), None)

def low_pass(kept, grad):
    return (grad,)

def back_keep(v):
    return (v, None)

def back_low(kept, grad):
    return (low(grad),)
low.defvjp(low_keep, low_pass)
low_back.defvjp(back_keep, back_low)
exact_mode = lax.Precision.HIGHEST

def matmul(left_side, right_side):
    return jnp.dot(left_side, right_side, precision=exact_mode)

def rms_scale(matrix):
    return lax.rsqrt(lax.optimization_barrier(jnp.mean(matrix * matrix, axis=-1, keepdims=True)) + 1e-06)

def rotate(matrix, cosine, sine_term):
    row_count = matrix.shape[0]
    per_head = matrix.reshape(row_count, -1, HEAD_SIZE)
    half_size = HEAD_SIZE // 2
    first_half = per_head[..., :half_size]
    second_half = per_head[..., half_size:]
    turned = jnp.concatenate([first_half * cosine - second_half * sine_term, second_half * cosine + first_half * sine_term], axis=-1)
    return turned.reshape(row_count, -1)

def group_layer(params, stream, positions):
    norm1_gain, q_weight, q_bias, key_projection, key_bias_vector, value_projection, value_bias_vector, o_weight, norm2_gain, gate_weight, up_weight, down_weight = params
    normed = low(stream * rms_scale(stream) * norm1_gain)
    step_index = jnp.arange(HEAD_SIZE // 2, dtype=jnp.float32) * 2.0
    frequency = 10000.0 ** (-step_index / HEAD_SIZE)
    angles = positions.astype(jnp.float32)[:, None] * frequency[None, :]
    cosine = jnp.cos(angles)[:, None, :]
    sine_term = jnp.sin(angles)[:, None, :]
    query_rows = low(rotate(low_back(matmul(normed, q_weight) + q_bias), cosine, sine_term))
    key_row_slice = low(rotate(low_back(matmul(normed, key_projection) + key_bias_vector), cosine, sine_term))
    value_rows = low(low_back(matmul(normed, value_projection) + value_bias_vector))
    query_rows = query_rows.reshape(ROW_TOKENS, KEY_VALUE_HEADS, QUERY_HEADS // KEY_VALUE_HEADS, HEAD_SIZE)
    key_row_slice = key_row_slice.reshape(ROW_TOKENS, KEY_VALUE_HEADS, HEAD_SIZE)
    value_rows = value_rows.reshape(ROW_TOKENS, KEY_VALUE_HEADS, HEAD_SIZE)
    scores = jnp.einsum('qkgd,rkd->kgqr', query_rows, key_row_slice, precision=exact_mode) * HEAD_SIZE ** (-0.5)
    scores = low_back(scores)
    token_index = jnp.arange(ROW_TOKENS)
    doc_start = token_index - positions
    allowed = (token_index[None, :] >= doc_start[:, None]) & (token_index[None, :] <= token_index[:, None])
    masked = jnp.where(allowed, scores, -1e+30)
    row_top = lax.optimization_barrier(jnp.max(masked, axis=-1, keepdims=True))
    exp_scores = jnp.where(allowed, jnp.exp(masked - row_top), 0.0)
    weights = low(exp_scores / lax.optimization_barrier(jnp.sum(exp_scores, axis=-1, keepdims=True)))
    attended = jnp.einsum('kgqr,rkd->qkgd', weights, value_rows, precision=exact_mode).reshape(ROW_TOKENS, QUERY_HEADS * HEAD_SIZE)
    attended = low(low_back(attended))
    hidden_one = stream + low_back(matmul(attended, o_weight))
    normed_two = low(hidden_one * rms_scale(hidden_one) * norm2_gain)
    gate_pre = low_back(matmul(normed_two, gate_weight))
    up_pre = low_back(matmul(normed_two, up_weight))
    activated = low(jax.nn.silu(gate_pre) * up_pre)
    return hidden_one + low_back(matmul(activated, down_weight))

def reference(tokens, positions, norm1_gain, q_weight, q_bias, key_projection, key_bias_vector, value_projection, value_bias_vector, o_weight, norm2_gain, gate_weight, up_weight, down_weight, cotangent):
    params = tuple((matrix.astype(jnp.float32) for matrix in (norm1_gain, q_weight, q_bias, key_projection, key_bias_vector, value_projection, value_bias_vector, o_weight, norm2_gain, gate_weight, up_weight, down_weight)))
    stream = tokens.astype(jnp.float32)
    group_step = jax.checkpoint(group_layer)

    def forward(params, stream):
        return lax.map(lambda item_pair: group_step(params, item_pair[0], item_pair[1]), (stream, positions))
    layer_out, pullback = jax.vjp(forward, params, stream)
    grad_params, grad_tokens = pullback(cotangent.astype(jnp.float32))
    grad_norm1_gain, grad_q_weight, grad_q_bias, grad_k_weight, grad_k_bias, grad_v_weight, grad_v_bias, grad_o_weight, grad_norm2_gain, grad_gate_weight, grad_up_weight, grad_down_weight = grad_params
    return (layer_out, grad_tokens, grad_norm1_gain, grad_q_weight, grad_q_bias, grad_k_weight, grad_k_bias, grad_v_weight, grad_v_bias, grad_o_weight, grad_norm2_gain, grad_gate_weight, grad_up_weight, grad_down_weight)
```

```python
import jax
import jax.numpy as jnp
from jax import lax
from jax.sharding import PartitionSpec as P

QUERY_HEADS = 12
KEY_VALUE_HEADS = 2
HEAD_SIZE = 128
GROUP = QUERY_HEADS // KEY_VALUE_HEADS
KV_WIDTH = KEY_VALUE_HEADS * HEAD_SIZE
EPSILON = 1e-06
BOTH = ("ctx", "fsdp")
F32 = jnp.float32
BF16 = jnp.bfloat16


def dot(a, b, dims):
    return lax.dot_general(a, b, ((dims[:1], dims[1:]), ((), ())), preferred_element_type=F32)


def nn(a, b):
    return dot(a, b, (1, 0))


def nt(a, b):
    return dot(a, b, (1, 1))


def tn(a, b):
    return dot(a, b, (0, 0))


def rms_scale(matrix):
    return lax.rsqrt(jnp.mean(matrix * matrix, axis=-1, keepdims=True) + EPSILON)


def angle_tables(positions):
    step_index = jnp.arange(HEAD_SIZE // 2, dtype=F32) * 2.0
    frequency = 10000.0 ** (-step_index / HEAD_SIZE)
    angles = positions.astype(F32)[:, None] * frequency[None, :]
    return jnp.cos(angles)[:, None, :], jnp.sin(angles)[:, None, :]


def rotate(matrix, cosine, sine):
    rows = matrix.shape[0]
    heads = matrix.reshape(rows, -1, HEAD_SIZE)
    a, b = heads[..., : HEAD_SIZE // 2], heads[..., HEAD_SIZE // 2 :]
    turned = jnp.concatenate([a * cosine - b * sine, b * cosine + a * sine], axis=-1)
    return turned.reshape(rows, -1)


def pick(stacked, index):
    return lax.dynamic_index_in_dim(stacked, index, 0, keepdims=False)


class Links:
    def __init__(self, ctx_size, fsdp_size):
        self.ctx_size, self.fsdp_size = ctx_size, fsdp_size
        self.planes = [m for m in (2, 4, 8, 16, 32, 64) if m < fsdp_size]

    def send(self, x, target):
        pairs = []
        for c in range(self.ctx_size):
            for f in range(self.fsdp_size):
                to = target(c, f)
                if to is not None:
                    pairs.append((c * self.fsdp_size + f, to[0] * self.fsdp_size + to[1]))
        return lax.ppermute(x, BOTH, pairs)

    def core(self, x):
        return self.send(x, lambda c, f: (c, f ^ 1))

    def plane(self, x, mask):
        return self.send(x, lambda c, f: (c, f ^ mask))

    def turn(self, x, step):
        return self.send(x, lambda c, f: ((c + step) % self.ctx_size, f))

    def shift(self, x, step):
        return self.send(
            x, lambda c, f: (c + step, f) if 0 <= c + step < self.ctx_size else None
        )


def plane_gather(links, shard):
    first, second, *rest = links.planes
    half = shard.shape[0] // 2
    a = links.plane(shard, first)
    b = links.plane(shard, second)
    low = links.plane(b[:half], first)
    high = links.plane(a[half:], second)
    pieces = {0: shard, first: a, second: b, first | second: jnp.concatenate([low, high])}
    for mask in rest:
        pieces.update({had | mask: links.plane(piece, mask) for had, piece in pieces.items()})
    return pieces


def ff_weight(links, ctx, chip, core, shard):
    ctx_size = links.ctx_size
    rows, hidden = shard.shape
    block = hidden // (2 * ctx_size)
    parts = jnp.transpose(shard.reshape(rows, ctx_size, 2, block), (2, 1, 0, 3))
    mine, other = pick(parts, core), pick(parts, 1 - core)
    got = links.core(other)
    even = core == 0
    pairs = jnp.stack([jnp.where(even, mine, got), jnp.where(even, got, mine)], axis=1)
    by_source = jnp.zeros_like(pairs)
    by_source = lax.dynamic_update_index_in_dim(by_source, pick(pairs, ctx), ctx, 0)
    for step in range(1, ctx_size):
        piece = links.turn(pick(pairs, (ctx + step) % ctx_size), step)
        by_source = lax.dynamic_update_index_in_dim(by_source, piece, (ctx - step) % ctx_size, 0)
    pieces = plane_gather(links, by_source)
    whole = jnp.zeros((ctx_size, links.fsdp_size // 2, 2, rows, block), shard.dtype)
    for mask, piece in pieces.items():
        whole = lax.dynamic_update_index_in_dim(whole, piece, chip ^ (mask // 2), 1)
    return whole.reshape(-1, block)


def spread_tokens(links, x):
    row = jnp.concatenate([x] + [links.turn(x, step) for step in range(1, links.ctx_size)])
    return jnp.concatenate([row, links.core(row)])


def collect_tokens(links, partial):
    rows = partial.shape[0] // 2
    got = links.core(partial[rows:].astype(BF16))
    count = rows // links.ctx_size
    row = (partial[:rows].astype(F32) + got.astype(F32)).reshape(links.ctx_size, count, -1)
    total = row[0]
    for step in range(1, links.ctx_size):
        total = total + links.turn(row[step].astype(BF16), -step).astype(F32)
    return total


def per_device(
    tokens,
    positions,
    norm1_gain,
    q_weight,
    q_bias,
    key_projection,
    key_bias_vector,
    value_projection,
    value_bias_vector,
    o_weight,
    norm2_gain,
    gate_weight,
    up_weight,
    down_weight,
    cotangent,
    *,
    links,
):
    ctx_size, fsdp_size = links.ctx_size, links.fsdp_size
    ctx, row_index = lax.axis_index("ctx"), lax.axis_index("fsdp")
    chip, core = row_index // 2, row_index % 2
    count, width = tokens.shape[1:]
    scale = HEAD_SIZE ** (-0.5)
    even = core == 0

    shard_rows = q_weight.shape[0]

    def column(x):
        return jnp.pad(x, (0, shard_rows - x.shape[0]))[:, None]

    kv_bias_rows = key_bias_vector.shape[0]
    extra = jnp.concatenate(
        [
            column(x)
            for x in (norm1_gain, q_bias, norm2_gain, key_bias_vector, value_bias_vector)
        ],
        axis=1,
    )
    extra = jnp.pad(extra, ((0, 0), (0, 128 - extra.shape[1])))
    packed = jnp.concatenate([q_weight, key_projection, value_projection, extra], axis=1)
    packed = lax.all_gather(packed, BOTH, axis=0, tiled=True)
    weight_o = lax.all_gather(o_weight, BOTH, axis=0, tiled=True)

    weight_gate = ff_weight(links, ctx, chip, core, gate_weight)
    weight_up = ff_weight(links, ctx, chip, core, up_weight)
    weight_down = ff_weight(links, ctx, chip, core, jnp.transpose(down_weight))

    qkv_width = width + 2 * KV_WIDTH
    weight_qkv = packed[:, :qkv_width]
    small = jnp.transpose(packed[:, qkv_width:])[:5].astype(F32)
    gain_one, bias_q, gain_two = small[0:1], small[1:2], small[2:3]

    def bias_of(row):
        return row.reshape(-1, shard_rows)[:, :kv_bias_rows].reshape(1, -1)

    bias_k, bias_v = bias_of(small[3]), bias_of(small[4])
    out_low = cotangent[0]
    group_out = spread_tokens(links, out_low)

    stream = tokens[0].astype(F32)
    scale_one = rms_scale(stream)
    unit_one = stream * scale_one
    normed_one = (unit_one * gain_one).astype(BF16)
    cosine, sine = angle_tables(positions[0])
    linear = nn(normed_one, weight_qkv)
    query = rotate(linear[:, :width] + bias_q, cosine, sine).astype(BF16)
    key = rotate(linear[:, width : width + KV_WIDTH] + bias_k, cosine, sine).astype(BF16)
    value = (linear[:, width + KV_WIDTH :] + bias_v).astype(BF16)
    pairs = jnp.concatenate([key, value], axis=1)
    row_pairs = jnp.concatenate(
        [pairs] + [links.shift(pairs, step) for step in range(1, ctx_size)]
    )
    keys = row_pairs[:, :KV_WIDTH].reshape(-1, KEY_VALUE_HEADS, HEAD_SIZE)
    values = row_pairs[:, KV_WIDTH:].reshape(-1, KEY_VALUE_HEADS, HEAD_SIZE)
    local_index = jnp.arange(count)
    key_index = jnp.concatenate(
        [(ctx - step) * count + local_index for step in range(ctx_size)]
    )
    query_index = ctx * count + local_index
    doc_start = query_index - positions[0]
    allowed = (key_index[None, :] >= doc_start[:, None]) & (
        key_index[None, :] <= query_index[:, None]
    )
    query_heads = query.reshape(count, KEY_VALUE_HEADS, GROUP, HEAD_SIZE)
    scores = jnp.einsum("qkgd,rkd->kgqr", query_heads, keys, preferred_element_type=F32) * scale
    scores = jnp.where(allowed, scores, -1e30)
    top = jnp.max(scores, axis=-1, keepdims=True)
    weights = jnp.where(allowed, jnp.exp(scores - top), 0.0)
    probs = weights / jnp.sum(weights, axis=-1, keepdims=True)
    probs_low = probs.astype(BF16)
    mixed = jnp.einsum("kgqr,rkd->qkgd", probs_low, values, preferred_element_type=F32)
    mixed_low = mixed.reshape(count, -1).astype(BF16)
    hidden_one = stream + nn(mixed_low, weight_o)

    scale_two = rms_scale(hidden_one)
    unit_two = hidden_one * scale_two
    normed_two = (unit_two * gain_two).astype(BF16)
    group_normed = spread_tokens(links, normed_two)
    gate_pre = nn(group_normed, weight_gate)
    up_pre = nn(group_normed, weight_up)
    grad_act = nn(group_out, weight_down)
    sigmoid_gate = jax.nn.sigmoid(gate_pre)
    activated = (gate_pre * sigmoid_gate * up_pre).astype(BF16)
    grad_gate_low = (
        grad_act * up_pre * sigmoid_gate * (1.0 + gate_pre * (1.0 - sigmoid_gate))
    ).astype(BF16)
    grad_up_low = (grad_act * gate_pre * sigmoid_gate).astype(BF16)
    grad_normed_two = collect_tokens(
        links, nt(grad_gate_low, weight_gate) + nt(grad_up_low, weight_up)
    )
    layer_out = hidden_one + collect_tokens(links, nt(activated, weight_down))

    planes = [
        [c * fsdp_size + 2 * p + k for p in range(fsdp_size // 2)]
        for c in range(ctx_size)
        for k in range(2)
    ]

    def ff_grad(left, right):
        term = tn(left, right).astype(BF16)
        part = lax.psum_scatter(
            term, BOTH, scatter_dimension=0, tiled=True, axis_index_groups=planes
        )
        part = part.reshape(2, -1, part.shape[1])
        mine, got = pick(part, core), links.core(pick(part, 1 - core))
        return jnp.concatenate(
            [jnp.where(even, mine, got), jnp.where(even, got, mine)], axis=1
        ).astype(F32)

    grad_gate = ff_grad(group_normed, grad_gate_low)
    grad_up = ff_grad(group_normed, grad_up_low)
    grad_down = jnp.transpose(ff_grad(group_out, activated))

    grad_gain_two = jnp.sum(grad_normed_two * unit_two, axis=0)
    weighted_two = grad_normed_two * gain_two
    grad_hidden = out_low.astype(F32) + scale_two * (
        weighted_two - unit_two * jnp.mean(weighted_two * unit_two, axis=-1, keepdims=True)
    )

    grad_hidden_low = grad_hidden.astype(BF16)
    grad_mixed = nt(grad_hidden_low, weight_o).astype(BF16)
    grad_mixed = grad_mixed.reshape(count, KEY_VALUE_HEADS, GROUP, HEAD_SIZE)
    grad_probs = jnp.einsum("qkgd,rkd->kgqr", grad_mixed, values, preferred_element_type=F32)
    delta = jnp.sum(probs * grad_probs, axis=-1, keepdims=True)
    grad_scores = (probs * (grad_probs - delta)).astype(BF16)
    grad_query = jnp.einsum("kgqr,rkd->qkgd", grad_scores, keys, preferred_element_type=F32)
    grad_key = (
        jnp.einsum("kgqr,qkgd->rkd", grad_scores, query_heads, preferred_element_type=F32) * scale
    )
    grad_value = jnp.einsum("kgqr,qkgd->rkd", probs_low, grad_mixed, preferred_element_type=F32)
    pair_terms = jnp.concatenate(
        [grad_key.reshape(-1, KV_WIDTH), grad_value.reshape(-1, KV_WIDTH)], axis=1
    ).reshape(ctx_size, count, -1)
    pair_grads = pair_terms[0]
    for step in range(1, ctx_size):
        pair_grads = pair_grads + links.shift(pair_terms[step].astype(BF16), -step).astype(F32)
    grad_q_low = rotate(grad_query.reshape(count, -1) * scale, cosine, -sine).astype(BF16)
    grad_k_low = rotate(pair_grads[:, :KV_WIDTH], cosine, -sine).astype(BF16)
    grad_v_low = pair_grads[:, KV_WIDTH:].astype(BF16)
    grad_qkv = jnp.concatenate([grad_q_low, grad_k_low, grad_v_low], axis=1)
    grad_normed_one = nt(grad_qkv, weight_qkv)
    grad_gain_one = jnp.sum(grad_normed_one * unit_one, axis=0)
    weighted_one = grad_normed_one * gain_one
    grad_stream = grad_hidden + scale_one * (
        weighted_one - unit_one * jnp.mean(weighted_one * unit_one, axis=-1, keepdims=True)
    )

    def columns_over_ctx(arrays):
        parts = jnp.concatenate([x.reshape(count, ctx_size, -1) for x in arrays], axis=2)
        parts = jnp.transpose(parts, (1, 0, 2))
        whole = jnp.zeros_like(parts)
        whole = lax.dynamic_update_index_in_dim(whole, pick(parts, ctx), ctx, 0)
        for step in range(1, ctx_size):
            piece = links.turn(pick(parts, (ctx + step) % ctx_size), step)
            whole = lax.dynamic_update_index_in_dim(whole, piece, (ctx - step) % ctx_size, 0)
        return whole.reshape(ctx_size * count, -1)

    def attention_grad(rows, arrays):
        left = lax.all_gather(rows, "ctx", axis=0, tiled=True)
        term = tn(left, columns_over_ctx(arrays)).astype(BF16)
        return lax.psum_scatter(term, "fsdp", scatter_dimension=0, tiled=True).astype(F32)

    grad_o = attention_grad(mixed_low, [grad_hidden_low])
    grad_packed = attention_grad(normed_one, [grad_q_low, grad_k_low, grad_v_low])
    q_columns, kv_columns = width // ctx_size, KV_WIDTH // ctx_size

    sums = jnp.concatenate(
        [grad_gain_one, grad_gain_two, jnp.sum(grad_qkv.astype(F32), axis=0)]
    )
    sums = lax.psum(sums, BOTH)
    device = ctx * fsdp_size + row_index

    def own(start, size):
        part = size // (ctx_size * fsdp_size)
        return lax.dynamic_slice_in_dim(sums, start + device * part, part)

    return (
        layer_out[None],
        grad_stream[None],
        own(0, width),
        grad_packed[:, :q_columns],
        own(2 * width, width),
        grad_packed[:, q_columns : q_columns + kv_columns],
        own(3 * width, KV_WIDTH),
        grad_packed[:, q_columns + kv_columns :],
        own(3 * width + KV_WIDTH, KV_WIDTH),
        grad_o,
        own(width, width),
        grad_gate,
        grad_up,
        grad_down,
    )


def solution(mesh):
    links = Links(mesh.shape["ctx"], mesh.shape["fsdp"])
    vector, matrix, stream = P(BOTH), P(BOTH, None), P("fsdp", "ctx", None)
    grid = P("fsdp", "ctx")
    in_specs = (
        stream,
        grid,
        vector,
        matrix,
        vector,
        matrix,
        vector,
        matrix,
        vector,
        matrix,
        vector,
        matrix,
        matrix,
        P(None, BOTH),
        stream,
    )
    out_specs = (
        stream,
        stream,
        vector,
        grid,
        vector,
        grid,
        vector,
        grid,
        vector,
        grid,
        vector,
        grid,
        grid,
        P("ctx", "fsdp"),
    )

    def run(*arrays):
        return per_device(*arrays, links=links)

    return jax.shard_map(run, mesh=mesh, in_specs=in_specs, out_specs=out_specs, check_vma=False)
```

```python
import jax
import jax.numpy as jnp
from jax import lax
from jax.experimental import pallas as pl
from jax.experimental.pallas import tpu as pltpu
from jax.sharding import PartitionSpec as P

QUERY_HEADS = 12
KEY_VALUE_HEADS = 2
HEAD_SIZE = 128
GROUP = QUERY_HEADS // KEY_VALUE_HEADS
KV_WIDTH = KEY_VALUE_HEADS * HEAD_SIZE
EPSILON = 1e-06
BACK_COST = 8 * 10**9
BOTH = ("ctx", "fsdp")
F32 = jnp.float32
BF16 = jnp.bfloat16


def dot(a, b, dims):
    return lax.dot_general(a, b, ((dims[:1], dims[1:]), ((), ())), preferred_element_type=F32)


def nn(a, b):
    return dot(a, b, (1, 0))


def nt(a, b):
    return dot(a, b, (1, 1))


def tn(a, b):
    return dot(a, b, (0, 0))


def rms_scale(matrix):
    return lax.rsqrt(jnp.mean(matrix * matrix, axis=-1, keepdims=True) + EPSILON)


def angle_tables(positions):
    step_index = jnp.arange(HEAD_SIZE // 2, dtype=F32) * 2.0
    frequency = 10000.0 ** (-step_index / HEAD_SIZE)
    angles = positions.astype(F32)[:, None] * frequency[None, :]
    return jnp.cos(angles)[:, None, :], jnp.sin(angles)[:, None, :]


def rotate(matrix, cosine, sine):
    rows = matrix.shape[0]
    heads = matrix.reshape(rows, -1, HEAD_SIZE)
    a, b = heads[..., : HEAD_SIZE // 2], heads[..., HEAD_SIZE // 2 :]
    turned = jnp.concatenate([a * cosine - b * sine, b * cosine + a * sine], axis=-1)
    return turned.reshape(rows, -1)


def pick(stacked, index):
    return lax.dynamic_index_in_dim(stacked, index, 0, keepdims=False)


class Links:
    def __init__(self, ctx_size, fsdp_size):
        self.ctx_size, self.fsdp_size = ctx_size, fsdp_size
        self.label = "move"
        self.planes = [m for m in (2, 4, 8, 16, 32, 64) if m < fsdp_size]

    def send(self, x, target):
        pairs = []
        for c in range(self.ctx_size):
            for f in range(self.fsdp_size):
                to = target(c, f)
                if to is not None:
                    pairs.append((c * self.fsdp_size + f, to[0] * self.fsdp_size + to[1]))
        with jax.named_scope(self.label):
            return lax.ppermute(x, BOTH, pairs)

    def core(self, x):
        return self.send(x, lambda c, f: (c, f ^ 1))

    def plane(self, x, mask):
        return self.send(x, lambda c, f: (c, f ^ mask))

    def turn(self, x, step):
        return self.send(x, lambda c, f: ((c + step) % self.ctx_size, f))

    def shift(self, x, step):
        return self.send(
            x, lambda c, f: (c + step, f) if 0 <= c + step < self.ctx_size else None
        )


def plane_gather(links, shard):
    first, second, *rest = links.planes
    half = shard.shape[0] // 2
    a = links.plane(shard, first)
    b = links.plane(shard, second)
    low = links.plane(b[:half], first)
    high = links.plane(a[half:], second)
    pieces = {0: shard, first: a, second: b, first | second: jnp.concatenate([low, high])}
    for mask in rest:
        pieces.update({had | mask: links.plane(piece, mask) for had, piece in pieces.items()})
    return pieces


def ff_weight(links, ctx, chip, core, shard):
    ctx_size = links.ctx_size
    rows, hidden = shard.shape
    block = hidden // (2 * ctx_size)
    parts = jnp.transpose(shard.reshape(rows, ctx_size, 2, block), (2, 1, 0, 3))
    mine, other = pick(parts, core), pick(parts, 1 - core)
    got = links.core(other)
    even = core == 0
    pairs = jnp.stack([jnp.where(even, mine, got), jnp.where(even, got, mine)], axis=1)
    by_source = jnp.zeros_like(pairs)
    by_source = lax.dynamic_update_index_in_dim(by_source, pick(pairs, ctx), ctx, 0)
    for step in range(1, ctx_size):
        piece = links.turn(pick(pairs, (ctx + step) % ctx_size), step)
        by_source = lax.dynamic_update_index_in_dim(by_source, piece, (ctx - step) % ctx_size, 0)
    pieces = plane_gather(links, by_source)
    whole = jnp.zeros((ctx_size, links.fsdp_size // 2, 2, rows, block), shard.dtype)
    for mask, piece in pieces.items():
        whole = lax.dynamic_update_index_in_dim(whole, piece, chip ^ (mask // 2), 1)
    return whole.reshape(-1, block)


def spread_tokens(links, x):
    row = jnp.concatenate([x] + [links.turn(x, step) for step in range(1, links.ctx_size)])
    return jnp.concatenate([row, links.core(row)])


def collect_tokens(links, partial):
    rows = partial.shape[0] // 2
    got = links.core(partial[rows:].astype(BF16))
    count = rows // links.ctx_size
    row = (partial[:rows].astype(F32) + got.astype(F32)).reshape(links.ctx_size, count, -1)
    total = row[0]
    for step in range(1, links.ctx_size):
        total = total + links.turn(row[step].astype(BF16), -step).astype(F32)
    return total


def per_device_any_mesh(
    tokens,
    positions,
    norm1_gain,
    q_weight,
    q_bias,
    key_projection,
    key_bias_vector,
    value_projection,
    value_bias_vector,
    o_weight,
    norm2_gain,
    gate_weight,
    up_weight,
    down_weight,
    cotangent,
    *,
    links,
):
    ctx_size, fsdp_size = links.ctx_size, links.fsdp_size
    ctx, row_index = lax.axis_index("ctx"), lax.axis_index("fsdp")
    chip, core = row_index // 2, row_index % 2
    count, width = tokens.shape[1:]
    scale = HEAD_SIZE ** (-0.5)
    even = core == 0

    shard_rows = q_weight.shape[0]

    def column(x):
        return jnp.pad(x, (0, shard_rows - x.shape[0]))[:, None]

    kv_bias_rows = key_bias_vector.shape[0]
    extra = jnp.concatenate(
        [
            column(x)
            for x in (norm1_gain, q_bias, norm2_gain, key_bias_vector, value_bias_vector)
        ],
        axis=1,
    )
    extra = jnp.pad(extra, ((0, 0), (0, 128 - extra.shape[1])))
    packed = jnp.concatenate([q_weight, key_projection, value_projection, extra], axis=1)
    packed = lax.all_gather(packed, BOTH, axis=0, tiled=True)
    weight_o = lax.all_gather(o_weight, BOTH, axis=0, tiled=True)

    weight_gate = ff_weight(links, ctx, chip, core, gate_weight)
    weight_up = ff_weight(links, ctx, chip, core, up_weight)
    weight_down = ff_weight(links, ctx, chip, core, jnp.transpose(down_weight))

    qkv_width = width + 2 * KV_WIDTH
    weight_qkv = packed[:, :qkv_width]
    small = jnp.transpose(packed[:, qkv_width:])[:5].astype(F32)
    gain_one, bias_q, gain_two = small[0:1], small[1:2], small[2:3]

    def bias_of(row):
        return row.reshape(-1, shard_rows)[:, :kv_bias_rows].reshape(1, -1)

    bias_k, bias_v = bias_of(small[3]), bias_of(small[4])
    out_low = cotangent[0]
    group_out = spread_tokens(links, out_low)

    stream = tokens[0].astype(F32)
    scale_one = rms_scale(stream)
    unit_one = stream * scale_one
    normed_one = (unit_one * gain_one).astype(BF16)
    cosine, sine = angle_tables(positions[0])
    linear = nn(normed_one, weight_qkv)
    query = rotate(linear[:, :width] + bias_q, cosine, sine).astype(BF16)
    key = rotate(linear[:, width : width + KV_WIDTH] + bias_k, cosine, sine).astype(BF16)
    value = (linear[:, width + KV_WIDTH :] + bias_v).astype(BF16)
    pairs = jnp.concatenate([key, value], axis=1)
    row_pairs = jnp.concatenate(
        [pairs] + [links.shift(pairs, step) for step in range(1, ctx_size)]
    )
    keys = row_pairs[:, :KV_WIDTH].reshape(-1, KEY_VALUE_HEADS, HEAD_SIZE)
    values = row_pairs[:, KV_WIDTH:].reshape(-1, KEY_VALUE_HEADS, HEAD_SIZE)
    local_index = jnp.arange(count)
    key_index = jnp.concatenate(
        [(ctx - step) * count + local_index for step in range(ctx_size)]
    )
    query_index = ctx * count + local_index
    doc_start = query_index - positions[0]
    allowed = (key_index[None, :] >= doc_start[:, None]) & (
        key_index[None, :] <= query_index[:, None]
    )
    query_heads = query.reshape(count, KEY_VALUE_HEADS, GROUP, HEAD_SIZE)
    scores = jnp.einsum("qkgd,rkd->kgqr", query_heads, keys, preferred_element_type=F32) * scale
    scores = jnp.where(allowed, scores, -1e30)
    top = jnp.max(scores, axis=-1, keepdims=True)
    weights = jnp.where(allowed, jnp.exp(scores - top), 0.0)
    probs = weights / jnp.sum(weights, axis=-1, keepdims=True)
    probs_low = probs.astype(BF16)
    mixed = jnp.einsum("kgqr,rkd->qkgd", probs_low, values, preferred_element_type=F32)
    mixed_low = mixed.reshape(count, -1).astype(BF16)
    hidden_one = stream + nn(mixed_low, weight_o)

    scale_two = rms_scale(hidden_one)
    unit_two = hidden_one * scale_two
    normed_two = (unit_two * gain_two).astype(BF16)
    group_normed = spread_tokens(links, normed_two)
    gate_pre = nn(group_normed, weight_gate)
    up_pre = nn(group_normed, weight_up)
    grad_act = nn(group_out, weight_down)
    sigmoid_gate = jax.nn.sigmoid(gate_pre)
    activated = (gate_pre * sigmoid_gate * up_pre).astype(BF16)
    grad_gate_low = (
        grad_act * up_pre * sigmoid_gate * (1.0 + gate_pre * (1.0 - sigmoid_gate))
    ).astype(BF16)
    grad_up_low = (grad_act * gate_pre * sigmoid_gate).astype(BF16)
    grad_normed_two = collect_tokens(
        links, nt(grad_gate_low, weight_gate) + nt(grad_up_low, weight_up)
    )
    layer_out = hidden_one + collect_tokens(links, nt(activated, weight_down))

    planes = [
        [c * fsdp_size + 2 * p + k for p in range(fsdp_size // 2)]
        for c in range(ctx_size)
        for k in range(2)
    ]

    def ff_grad(left, right):
        term = tn(left, right).astype(BF16)
        part = lax.psum_scatter(
            term, BOTH, scatter_dimension=0, tiled=True, axis_index_groups=planes
        )
        part = part.reshape(2, -1, part.shape[1])
        mine, got = pick(part, core), links.core(pick(part, 1 - core))
        return jnp.concatenate(
            [jnp.where(even, mine, got), jnp.where(even, got, mine)], axis=1
        ).astype(F32)

    grad_gate = ff_grad(group_normed, grad_gate_low)
    grad_up = ff_grad(group_normed, grad_up_low)
    grad_down = jnp.transpose(ff_grad(group_out, activated))

    grad_gain_two = jnp.sum(grad_normed_two * unit_two, axis=0)
    weighted_two = grad_normed_two * gain_two
    grad_hidden = out_low.astype(F32) + scale_two * (
        weighted_two - unit_two * jnp.mean(weighted_two * unit_two, axis=-1, keepdims=True)
    )

    grad_hidden_low = grad_hidden.astype(BF16)
    grad_mixed = nt(grad_hidden_low, weight_o).astype(BF16)
    grad_mixed = grad_mixed.reshape(count, KEY_VALUE_HEADS, GROUP, HEAD_SIZE)
    grad_probs = jnp.einsum("qkgd,rkd->kgqr", grad_mixed, values, preferred_element_type=F32)
    delta = jnp.sum(probs * grad_probs, axis=-1, keepdims=True)
    grad_scores = (probs * (grad_probs - delta)).astype(BF16)
    grad_query = jnp.einsum("kgqr,rkd->qkgd", grad_scores, keys, preferred_element_type=F32)
    grad_key = (
        jnp.einsum("kgqr,qkgd->rkd", grad_scores, query_heads, preferred_element_type=F32) * scale
    )
    grad_value = jnp.einsum("kgqr,qkgd->rkd", probs_low, grad_mixed, preferred_element_type=F32)
    pair_terms = jnp.concatenate(
        [grad_key.reshape(-1, KV_WIDTH), grad_value.reshape(-1, KV_WIDTH)], axis=1
    ).reshape(ctx_size, count, -1)
    pair_grads = pair_terms[0]
    for step in range(1, ctx_size):
        pair_grads = pair_grads + links.shift(pair_terms[step].astype(BF16), -step).astype(F32)
    grad_q_low = rotate(grad_query.reshape(count, -1) * scale, cosine, -sine).astype(BF16)
    grad_k_low = rotate(pair_grads[:, :KV_WIDTH], cosine, -sine).astype(BF16)
    grad_v_low = pair_grads[:, KV_WIDTH:].astype(BF16)
    grad_qkv = jnp.concatenate([grad_q_low, grad_k_low, grad_v_low], axis=1)
    grad_normed_one = nt(grad_qkv, weight_qkv)
    grad_gain_one = jnp.sum(grad_normed_one * unit_one, axis=0)
    weighted_one = grad_normed_one * gain_one
    grad_stream = grad_hidden + scale_one * (
        weighted_one - unit_one * jnp.mean(weighted_one * unit_one, axis=-1, keepdims=True)
    )

    def columns_over_ctx(arrays):
        parts = jnp.concatenate([x.reshape(count, ctx_size, -1) for x in arrays], axis=2)
        parts = jnp.transpose(parts, (1, 0, 2))
        whole = jnp.zeros_like(parts)
        whole = lax.dynamic_update_index_in_dim(whole, pick(parts, ctx), ctx, 0)
        for step in range(1, ctx_size):
            piece = links.turn(pick(parts, (ctx + step) % ctx_size), step)
            whole = lax.dynamic_update_index_in_dim(whole, piece, (ctx - step) % ctx_size, 0)
        return whole.reshape(ctx_size * count, -1)

    def attention_grad(rows, arrays):
        left = lax.all_gather(rows, "ctx", axis=0, tiled=True)
        term = tn(left, columns_over_ctx(arrays)).astype(BF16)
        return lax.psum_scatter(term, "fsdp", scatter_dimension=0, tiled=True).astype(F32)

    grad_o = attention_grad(mixed_low, [grad_hidden_low])
    grad_packed = attention_grad(normed_one, [grad_q_low, grad_k_low, grad_v_low])
    q_columns, kv_columns = width // ctx_size, KV_WIDTH // ctx_size

    sums = jnp.concatenate(
        [grad_gain_one, grad_gain_two, jnp.sum(grad_qkv.astype(F32), axis=0)]
    )
    sums = lax.psum(sums, BOTH)
    device = ctx * fsdp_size + row_index

    def own(start, size):
        part = size // (ctx_size * fsdp_size)
        return lax.dynamic_slice_in_dim(sums, start + device * part, part)

    return (
        layer_out[None],
        grad_stream[None],
        own(0, width),
        grad_packed[:, :q_columns],
        own(2 * width, width),
        grad_packed[:, q_columns : q_columns + kv_columns],
        own(3 * width, KV_WIDTH),
        grad_packed[:, q_columns + kv_columns :],
        own(3 * width + KV_WIDTH, KV_WIDTH),
        grad_o,
        own(width, width),
        grad_gate,
        grad_up,
        grad_down,
    )


def after(x, *others):
    return lax.optimization_barrier((x, *others))[0]


def phase(*groups):
    flat = lax.optimization_barrier(tuple(x for group in groups for x in group))
    out = []
    for group in groups:
        out.append(list(flat[: len(group)]))
        flat = flat[len(group) :]
    return out


def plane_start(links, shard):
    return links.plane(shard, 2), links.plane(shard, 4)


def plane_end(links, shard, a, b):
    half = shard.shape[0] // 2
    return shard, a, b, links.plane(b[:half], 2), links.plane(a[half:], 4)


def laid_out(entries, shard, a, b, low, high):
    half = len(entries) // 2
    return [
        (entries, 0, shard),
        (entries, 1, a),
        (entries, 2, b),
        (entries[:half], 3, low),
        (entries[half:], 3, high),
    ]


def ff_kernel(layout, sizes, place, normed, out_grad, *refs):
    ctx_size, chips, rows = sizes
    pieces, refs = refs[: len(layout)], refs[len(layout) :]
    act_ref, gate_ref, up_ref, down_ref, y_ref, weights, semaphores = refs

    @pl.when(pl.program_id(0) == 0)
    def _():
        ctx, chip = place[0], place[1]
        for which in range(3):
            for (entries, mask, _), piece in zip(layout, pieces):
                for i, (step, core) in enumerate(entries):
                    source = lax.rem(ctx - step + ctx_size, ctx_size)
                    start = ((source * chips + (chip ^ mask)) * 2 + core) * rows
                    pltpu.make_async_copy(
                        piece.at[i, which],
                        weights.at[which, pl.ds(pl.multiple_of(start, rows), rows)],
                        semaphores.at[which],
                    ).start()

    def arrived(which):
        @pl.when(pl.program_id(0) == 0)
        def _():
            pltpu.make_async_copy(
                weights.at[which], weights.at[which], semaphores.at[which]
            ).wait()

    x, gy = normed[...], out_grad[...]
    arrived(0)
    gate = nn(x, weights[0])
    arrived(1)
    up = nn(x, weights[1])
    arrived(2)
    grad = nn(gy, weights[2])
    sigmoid = 1.0 / (1.0 + jnp.exp(-gate))
    silu = gate * sigmoid
    act = (silu * up).astype(BF16)
    grad_gate = (grad * up * sigmoid * (1.0 + gate * (1.0 - sigmoid))).astype(BF16)
    grad_up = (grad * silu).astype(BF16)
    act_ref[...] = act
    gate_ref[...] = grad_gate
    up_ref[...] = grad_up
    down_ref[...] = (nt(grad_gate, weights[0]) + nt(grad_up, weights[1])).astype(BF16)
    y_ref[...] = nt(act, weights[2]).astype(BF16)


def feed_forward(links, layout, place, normed, out_grad):
    tokens, width = normed.shape
    rows, block = layout[0][2].shape[2:]
    tile = 256
    wide = pl.BlockSpec((tile, width), lambda i, place: (i, 0))
    narrow = pl.BlockSpec((tile, block), lambda i, place: (i, 0))
    small = jax.ShapeDtypeStruct((tokens, block), BF16)
    large = jax.ShapeDtypeStruct((tokens, width), BF16)
    sizes = (links.ctx_size, links.fsdp_size // 2, rows)

    def body(*refs):
        ff_kernel(layout, sizes, *refs)

    return pl.pallas_call(
        body,
        grid_spec=pltpu.PrefetchScalarGridSpec(
            num_scalar_prefetch=1,
            grid=(tokens // tile,),
            in_specs=[wide, wide] + [pl.BlockSpec(memory_space=pl.ANY)] * len(layout),
            out_specs=[narrow, narrow, narrow, wide, wide],
            scratch_shapes=[
                pltpu.VMEM((3, width, block), BF16),
                pltpu.SemaphoreType.DMA((3,)),
            ],
        ),
        out_shape=[small, small, small, large, large],
        compiler_params=pltpu.CompilerParams(vmem_limit_bytes=56 * 2**20),
        cost_estimate=pl.CostEstimate(flops=0, bytes_accessed=0, transcendentals=0),
    )(place, normed, out_grad, *[piece for _, _, piece in layout])


def grad_kernel(place, *refs):
    lefts, rights, outs = refs[:4], refs[4:10], refs[10:]
    keep_low, send_low, keep_high, send_high = outs
    j = pl.program_id(0)
    for which in range(3):
        left_a, left_b = lefts[:2] if which < 2 else lefts[2:]
        right_a, right_b = rights[2 * which : 2 * which + 2]
        out = tn(left_a[...], right_a[...]) + tn(left_b[...], right_b[...])
        half = out.shape[0] // 2
        low, high = out[:half].astype(BF16), out[half:].astype(BF16)

        @pl.when(j < 2)
        def _():
            keep_low[0, which] = low

        @pl.when(j >= 2)
        def _():
            send_low[0, which] = low

        @pl.when(j % 2 == 0)
        def _():
            keep_high[0, which] = high

        @pl.when(j % 2 == 1)
        def _():
            send_high[0, which] = high


def ff_grad_terms(place, lefts, rights):
    tokens, width = lefts[0].shape
    block = rights[0].shape[1]
    part = width // 4
    left = pl.BlockSpec((tokens, part), lambda j, place: (0, place[1] ^ j))
    right = pl.BlockSpec((tokens, block), lambda j, place: (0, 0))

    def out(index):
        return pl.BlockSpec((1, 3, part // 2, block), lambda j, place: (index(j), 0, 0, 0))

    return pl.pallas_call(
        grad_kernel,
        grid_spec=pltpu.PrefetchScalarGridSpec(
            num_scalar_prefetch=1,
            grid=(4,),
            in_specs=[left] * 4 + [right] * 6,
            out_specs=[
                out(lambda j: jnp.minimum(j, 1)),
                out(lambda j: jnp.maximum(j - 2, 0)),
                out(lambda j: j // 2),
                out(lambda j: j // 2),
            ],
        ),
        out_shape=[jax.ShapeDtypeStruct((2, 3, part // 2, block), BF16)] * 4,
        compiler_params=pltpu.CompilerParams(vmem_limit_bytes=56 * 2**20),
        cost_estimate=pl.CostEstimate(flops=0, bytes_accessed=0, transcendentals=0),
    )(place, *lefts, *rights)


def added(a, b):
    return (a.astype(F32) + b.astype(F32)).astype(BF16)


def reduce_start(links, terms):
    return links.plane(terms[1], 4), links.plane(terms[3], 2)


def reduce_next(links, terms, first):
    keep_low, _, keep_high, _ = terms
    return (
        links.plane(added(keep_low[1], first[0][1]), 2),
        links.plane(added(keep_high[1], first[1][1]), 4),
    )


def reduce_end(terms, first, second):
    return [
        keep[0].astype(F32) + one[0].astype(F32) + two.astype(F32)
        for keep, one, two in zip(terms[::2], first, second)
    ]


def split_kernel(place, gate, up, down, mine, other):
    block = mine.shape[3]

    def write(core):
        for which, ref in enumerate((gate, up, down)):
            for target in range(mine.shape[0]):
                start = (2 * target + core) * block
                mine[target, which] = ref[:, start : start + block]
                start = (2 * target + 1 - core) * block
                other[target, which] = ref[:, start : start + block]

    @pl.when(place[2] == 0)
    def _():
        write(0)

    @pl.when(place[2] != 0)
    def _():
        write(1)


def split_hidden(links, place, shards):
    rows, hidden = shards[0].shape
    whole = pl.BlockSpec((rows, hidden), lambda i, place: (0, 0))
    shape = (links.ctx_size, 3, rows, hidden // (2 * links.ctx_size))
    out = pl.BlockSpec(shape, lambda i, place: (0, 0, 0, 0))
    return pl.pallas_call(
        split_kernel,
        grid_spec=pltpu.PrefetchScalarGridSpec(
            num_scalar_prefetch=1, grid=(1,), in_specs=[whole] * 3, out_specs=[out] * 2
        ),
        out_shape=[jax.ShapeDtypeStruct(shape, BF16)] * 2,
        compiler_params=pltpu.CompilerParams(vmem_limit_bytes=32 * 2**20),
    )(place, *shards)


class Rows:
    def __init__(self, ctx_size, chips, pieces, layout):
        self.pieces, self.layout = pieces, layout
        self.sizes = (ctx_size, chips)
        self.rows, self.columns = pieces[0].shape[-2:]
        self.shape = (2 * ctx_size * chips * self.rows, self.columns)

    def start(self, place, refs, weight, semaphore):
        chips = self.sizes[1]
        for piece, index, source, mask, turned in self.layout:
            start = ((source * chips + (place[1] ^ mask)) * 2 + (place[2] ^ turned)) * self.rows
            pltpu.make_async_copy(
                refs[piece].at[index],
                weight.at[pl.ds(pl.multiple_of(start, self.rows), self.rows)],
                semaphore,
            ).start()


def by_ctx(links, ctx, got):
    ctx_size, shard = links.ctx_size, got[0]
    whole = jnp.zeros((ctx_size, *shard.shape), shard.dtype)
    for step, piece in enumerate(got):
        whole = lax.dynamic_update_index_in_dim(whole, piece, (ctx - step) % ctx_size, 0)
    return whole


def rows_of_plane(links, mine, a, b, low, high):
    ctx_size = links.ctx_size
    half = ctx_size // 2
    early = links.core(jnp.stack([mine, a, b]))
    late = links.core(jnp.concatenate([low, high]))
    pieces = [mine, a, b, low, high, early, late]
    layout = []
    for c in range(ctx_size):
        layout += [(mask, (c,), c, mask, 0) for mask in range(3)]
        layout.append((3, (c,), c, 3, 0) if c < half else (4, (c - half,), c, 3, 0))
        layout += [(5, (mask, c), c, mask, 1) for mask in range(3)]
        layout.append((6, (c,), c, 3, 1))
    return Rows(ctx_size, links.fsdp_size // 2, pieces, layout)


def wait_all(weight, semaphore):
    pltpu.make_async_copy(weight, weight, semaphore).wait()


def call(body, place, arrays, weight, out_shapes, cost):
    any_spec = pl.BlockSpec(memory_space=pl.ANY)
    vmem = pl.BlockSpec(memory_space=pltpu.VMEM)
    count, pieces = len(arrays), len(weight.pieces)

    def kernel(place, *refs):
        ins, parts, outs = refs[:count], refs[count : count + pieces], refs[count + pieces : -2]
        scratch, semaphore = refs[-2:]
        weight.start(place, parts, scratch, semaphore)
        body(place, ins, outs, scratch, lambda: wait_all(scratch, semaphore))

    return pl.pallas_call(
        kernel,
        in_specs=[pl.BlockSpec(memory_space=pltpu.SMEM)] + [vmem] * count + [any_spec] * pieces,
        out_specs=[vmem] * len(out_shapes),
        out_shape=[jax.ShapeDtypeStruct(shape, dtype) for shape, dtype in out_shapes],
        scratch_shapes=[pltpu.VMEM(weight.shape, BF16), pltpu.SemaphoreType.DMA],
        compiler_params=pltpu.CompilerParams(vmem_limit_bytes=56 * 2**20),
        cost_estimate=pl.CostEstimate(flops=cost, bytes_accessed=0, transcendentals=0),
    )(place, *arrays, *weight.pieces)


def turn_halves(x, cosine, sine):
    return x * cosine + pltpu.roll(x, HEAD_SIZE // 2, 1) * sine


def turned_heads(x, cosine, sine):
    heads = [x[:, i : i + HEAD_SIZE] for i in range(0, x.shape[1], HEAD_SIZE)]
    return jnp.concatenate([turn_halves(x, cosine, sine) for x in heads], axis=1)


def qkv_body(shard_rows, place, ins, outs, weight, wait):
    tokens, cosine, sine = ins
    normed_ref, query_ref, pairs_ref, small_ref = outs
    width = tokens.shape[1]
    qkv_width = width + 2 * KV_WIDTH
    x = tokens[...].astype(F32)
    unit = x * rms_scale(x)
    wait()
    small = jnp.transpose(weight[:, qkv_width:].astype(F32))[:8]
    bias_rows = KV_WIDTH * shard_rows // width
    row = lax.broadcasted_iota(jnp.int32, (width, KV_WIDTH), 0)
    at = lax.broadcasted_iota(jnp.int32, (width, KV_WIDTH), 1)
    chosen = row == (at // bias_rows) * shard_rows + at % bias_rows
    kv_bias = nn(small.astype(BF16), chosen.astype(BF16))
    normed = (unit * small[0:1]).astype(BF16)
    normed_ref[...] = normed
    small_ref[...] = small
    linear = nn(normed, weight[:, :qkv_width])
    query = linear[:, :width] + small[1:2]
    key = linear[:, width : width + KV_WIDTH] + kv_bias[3:4]
    query_ref[...] = turned_heads(query, cosine[...], sine[...]).astype(BF16)
    pairs_ref[:, :KV_WIDTH] = turned_heads(key, cosine[...], sine[...]).astype(BF16)
    pairs_ref[:, KV_WIDTH:] = (linear[:, width + KV_WIDTH :] + kv_bias[4:5]).astype(BF16)


def allowed_keys(ctx, positions, blocks):
    count = positions.shape[0]
    shape = (count, blocks * count)
    column = lax.broadcasted_iota(jnp.int32, shape, 1)
    query = ctx * count + lax.broadcasted_iota(jnp.int32, shape, 0)
    key = (ctx - column // count) * count + column % count
    return (key >= query - positions) & (key <= query)


def heads_of(x, group):
    first = group * GROUP
    return jnp.concatenate(
        [x[:, i * HEAD_SIZE : (i + 1) * HEAD_SIZE] for i in range(first, first + GROUP)], axis=0
    )


def softmax_of(query, keys, allowed):
    scores = nt(query, keys) * HEAD_SIZE ** (-0.5)
    scores = jnp.where(allowed, scores, -1e30)
    weights = jnp.exp(scores - jnp.max(scores, axis=-1, keepdims=True))
    weights = jnp.where(allowed, weights, 0.0)
    return weights / jnp.sum(weights, axis=-1, keepdims=True)


def group_pairs(blocks, group):
    def columns(start):
        return jnp.concatenate([b[:, start : start + HEAD_SIZE] for b in blocks], axis=0)

    return columns(group * HEAD_SIZE), columns(KV_WIDTH + group * HEAD_SIZE)


def mix_body(place, ins, outs, weight, wait):
    tokens, small, positions, query, *blocks = ins
    mixed_ref, hidden_ref, normed_ref = outs
    count = tokens.shape[0]
    allowed = allowed_keys(place[0], positions[...], len(blocks))
    allowed = jnp.concatenate([allowed.astype(F32)] * GROUP, axis=0) > 0
    for group in range(KEY_VALUE_HEADS):
        keys, values = group_pairs(blocks, group)
        probs = softmax_of(heads_of(query, group), keys, allowed)
        mixed = nn(probs.astype(BF16), values).astype(BF16)
        for h in range(GROUP):
            start = (group * GROUP + h) * HEAD_SIZE
            mixed_ref[:, start : start + HEAD_SIZE] = mixed[h * count : (h + 1) * count]
    wait()
    hidden = tokens[...].astype(F32) + nn(mixed_ref[...], weight[...])
    hidden_ref[...] = hidden
    normed_ref[...] = (hidden * rms_scale(hidden) * small[2:3]).astype(BF16)


def norm_back(unit, scale, grad, gain):
    weighted = grad * gain
    return scale * (weighted - unit * jnp.mean(weighted * unit, axis=-1, keepdims=True))


def mix_back_body(steps, place, ins, outs, weight, wait):
    terms, ins = ins[:steps], ins[steps:]
    hidden_ref, small, out_grad, positions, query, cosine, sine, *blocks = ins
    grad_hidden_ref, low_ref, grad_query_ref, gain_ref, *pair_refs = outs
    count = hidden_ref.shape[0]
    hidden = hidden_ref[...]
    scale = rms_scale(hidden)
    unit = hidden * scale
    grad = terms[0][...].astype(F32)
    for term in terms[1:]:
        grad = grad + term[...].astype(F32)
    gain_ref[...] = jnp.sum(grad * unit, axis=0, keepdims=True)
    grad_hidden = out_grad[...].astype(F32) + norm_back(unit, scale, grad, small[2:3])
    grad_hidden_ref[...] = grad_hidden
    low = grad_hidden.astype(BF16)
    low_ref[...] = low
    wait()
    grad_mixed = nt(low, weight[...]).astype(BF16)
    allowed = allowed_keys(place[0], positions[...], len(blocks))
    allowed = jnp.concatenate([allowed.astype(F32)] * GROUP, axis=0) > 0
    score_scale = HEAD_SIZE ** (-0.5)
    for group in range(KEY_VALUE_HEADS):
        keys, values = group_pairs(blocks, group)
        queries, grads = heads_of(query, group), heads_of(grad_mixed, group)
        probs = softmax_of(queries, keys, allowed)
        grad_probs = nt(grads, values)
        delta = jnp.sum(probs * grad_probs, axis=-1, keepdims=True)
        grad_scores = (probs * (grad_probs - delta)).astype(BF16)
        grad_query = nn(grad_scores, keys) * score_scale
        for h in range(GROUP):
            start = (group * GROUP + h) * HEAD_SIZE
            grad_query_ref[:, start : start + HEAD_SIZE] = turn_halves(
                grad_query[h * count : (h + 1) * count], cosine[...], -sine[...]
            ).astype(BF16)
        grad_key = (tn(grad_scores, queries) * score_scale).astype(BF16)
        grad_value = tn(probs.astype(BF16), grads).astype(BF16)
        start = group * HEAD_SIZE
        for block, ref in enumerate(pair_refs):
            rows = slice(block * count, (block + 1) * count)
            ref[:, start : start + HEAD_SIZE] = grad_key[rows]
            ref[:, KV_WIDTH + start : KV_WIDTH + start + HEAD_SIZE] = grad_value[rows]


def qkv_back_body(steps, place, ins, outs, weight, wait):
    terms, ins = ins[:steps], ins[steps:]
    tokens, small, cosine, sine, grad_query, grad_hidden, grad_hidden_low, gain_two = ins
    stream_ref, share_ref = outs
    count, width = tokens.shape
    pairs = terms[0][...].astype(F32)
    for term in terms[1:]:
        pairs = pairs + term[...].astype(F32)
    grad_key = turned_heads(pairs[:, :KV_WIDTH], cosine[...], -sine[...]).astype(BF16)
    grad_value = pairs[:, KV_WIDTH:].astype(BF16)
    wait()
    kv_end = width + KV_WIDTH
    grad = (
        nt(grad_query[...], weight[:, :width])
        + nt(grad_key, weight[:, width:kv_end])
        + nt(grad_value, weight[:, kv_end : kv_end + KV_WIDTH])
    )
    x = tokens[...].astype(F32)
    scale = rms_scale(x)
    unit = x * scale
    stream_ref[...] = grad_hidden[...] + norm_back(unit, scale, grad, small[0:1])
    gains = jnp.concatenate([jnp.sum(grad * unit, axis=0, keepdims=True), gain_two[...]], axis=0)
    gains = jnp.concatenate([gains, jnp.zeros((14, width), F32)], axis=0).astype(BF16)
    targets = share_ref.shape[0]
    q_columns, kv_columns = width // targets, KV_WIDTH // targets
    for target in range(targets):
        q, kv = target * q_columns, target * kv_columns
        share_ref[target, :count, :q_columns] = grad_query[:, q : q + q_columns]
        kv_end = q_columns + 2 * kv_columns
        share_ref[target, :count, q_columns:kv_end] = jnp.concatenate(
            [grad_key[:, kv : kv + kv_columns], grad_value[:, kv : kv + kv_columns]], axis=1
        )
        share_ref[target, :count, kv_end:] = grad_hidden_low[:, q : q + q_columns]
        share_ref[target, count:, :q_columns] = gains[:, q : q + q_columns]
        share_ref[target, count:, q_columns:] = jnp.zeros(
            (16, share_ref.shape[2] - q_columns), BF16
        )


def per_device_plane_of_four(
    tokens,
    positions,
    norm1_gain,
    q_weight,
    q_bias,
    key_projection,
    key_bias_vector,
    value_projection,
    value_bias_vector,
    o_weight,
    norm2_gain,
    gate_weight,
    up_weight,
    down_weight,
    cotangent,
    *,
    links,
):
    ctx_size, fsdp_size = links.ctx_size, links.fsdp_size
    ctx, row_index = lax.axis_index("ctx"), lax.axis_index("fsdp")
    chip, core = row_index // 2, row_index % 2
    place = jnp.stack([ctx, chip, core])
    count, width = tokens.shape[1:]
    shard_rows = q_weight.shape[0]
    even = core == 0
    steps = range(1, ctx_size)

    def column(x):
        return jnp.pad(x, (0, shard_rows - x.shape[0]))[:, None]

    extra = jnp.concatenate(
        [
            column(x)
            for x in (norm1_gain, q_bias, norm2_gain, key_bias_vector, value_bias_vector)
        ],
        axis=1,
    )
    extra = jnp.pad(extra, ((0, 0), (0, 128 - extra.shape[1])))
    packed = jnp.concatenate([q_weight, key_projection, value_projection, extra], axis=1)
    links.label = "qkv_ctx"
    qkv_got = [packed] + [links.turn(packed, step) for step in steps]
    links.label = "o_ctx"
    o_got = [o_weight] + [links.turn(o_weight, step) for step in steps]

    mine, other = split_hidden(
        links, place, (gate_weight, up_weight, jnp.transpose(down_weight))
    )
    links.label = "ff_core"
    qkv_got, o_got, (mine, got) = phase(qkv_got, o_got, (mine, links.core(other)))

    def for_ctx(step):
        target = (ctx + step) % ctx_size
        a, b = pick(mine, target), pick(got, target)
        return jnp.stack([jnp.where(even, a, b), jnp.where(even, b, a)])

    qkv_mine = by_ctx(links, ctx, qkv_got)
    o_mine = by_ctx(links, ctx, o_got)
    own_piece = for_ctx(0)
    links.label = "qkv_plane1"
    qkv_stage = plane_start(links, qkv_mine)
    links.label = "ff_own1"
    own_stage = plane_start(links, own_piece)
    links.label = "ff_ctx_a"
    moved = {step: links.turn(for_ctx(step), step) for step in (1, ctx_size - 1)}
    far = {step: for_ctx(step) for step in range(2, ctx_size - 1)}
    qkv_stage, own_stage, near, far_list, (o_mine,) = phase(
        qkv_stage, own_stage, moved.values(), far.values(), (o_mine,)
    )
    moved = dict(zip(moved, near))
    links.label = "ff_ctx_b"
    for step, piece in zip(far, far_list):
        moved[step] = links.turn(piece, step)
    links.label = "qkv_plane2"
    qkv_parts = plane_end(links, qkv_mine, *qkv_stage)
    links.label = "ff_own2"
    own_parts = plane_end(links, own_piece, *own_stage)
    links.label = "o_plane1"
    o_stage = plane_start(links, o_mine)
    moved_list, qkv_late, own_late, o_stage = phase(
        [moved[step] for step in steps], qkv_parts[3:], own_parts[3:], o_stage
    )
    own_parts = (*own_parts[:3], *own_late)
    links.label = "qkv_core"
    weight_qkv = rows_of_plane(links, *qkv_parts[:3], *qkv_late)
    links.label = "o_plane2"
    o_parts = plane_end(links, o_mine, *o_stage)
    links.label = "o_core"
    weight_o = rows_of_plane(links, *o_parts)
    links.label = "ff_plane1"
    moved_piece = jnp.concatenate(moved_list)
    moved_stage = plane_start(links, moved_piece)

    low_tokens, out_low = tokens[0], cotangent[0]
    cosine, sine = (x[:, 0] for x in angle_tables(positions[0]))
    cosine = jnp.concatenate([cosine, cosine], axis=1)
    sine = jnp.concatenate([-sine, sine], axis=1)
    place_column = positions[0][:, None]
    wide, narrow = (count, width), (count, 2 * KV_WIDTH)

    def qkv(*refs):
        qkv_body(shard_rows, *refs)

    normed_one, query, pairs, small = call(
        qkv,
        place,
        (low_tokens, cosine, sine),
        weight_qkv,
        [(wide, BF16), (wide, BF16), (narrow, BF16), ((8, width), F32)],
        0,
    )
    links.label = "kv"
    blocks = [pairs] + [links.shift(pairs, step) for step in steps]
    mixed_low, hidden_one, normed_two = call(
        mix_body,
        place,
        (low_tokens, small, place_column, query, *blocks),
        weight_o,
        [(wide, BF16), (wide, F32), (wide, BF16)],
        0,
    )

    out_row = lax.all_gather(after(out_low, *moved_list), "ctx", axis=0, tiled=True)
    normed_row = lax.all_gather(normed_two, "ctx", axis=0, tiled=True)
    links.label = "gy_core"
    out_other = links.core(out_row)
    links.label = "ff_plane2"
    moved_parts = plane_end(links, moved_piece, *moved_stage)
    layout = [
        *laid_out([(0, 0), (0, 1)], *own_parts),
        *laid_out([(step, core) for step in steps for core in range(2)], *moved_parts),
    ]
    links.label = "n2_core"
    normed_other = links.core(after(normed_row, *moved_parts[3:]))
    act_a, gate_a, up_a, down_a, y_a = feed_forward(links, layout, place, normed_row, out_row)
    act_b, gate_b, up_b, down_b, y_b = feed_forward(links, layout, place, normed_other, out_other)
    links.label = "gn2_core"
    down_got = links.core(down_b)
    grad_normed_two = lax.psum_scatter(
        added(down_a, down_got), "ctx", scatter_dimension=0, tiled=True
    )

    ff_terms = ff_grad_terms(
        place,
        (after(normed_row, down_got), normed_other, out_row, out_other),
        (gate_a, gate_b, up_a, up_b, act_a, act_b),
    )
    links.label = "ff_sum1"
    ff_first = reduce_start(links, ff_terms)
    grad_normed_two = after(grad_normed_two, ff_terms[0])

    def mix_back(*refs):
        mix_back_body(1, *refs)

    grad_hidden, grad_hidden_low, grad_query, gain_two, *pair_terms = call(
        mix_back,
        place,
        (grad_normed_two, hidden_one, small, out_low, place_column, query, cosine, sine, *blocks),
        weight_o,
        [(wide, F32), (wide, BF16), (wide, BF16), ((1, width), F32)] + [(narrow, BF16)] * ctx_size,
        BACK_COST,
    )
    links.label = "y_core"
    both_rows = lax.all_gather(
        after(jnp.concatenate([normed_one, mixed_low], axis=1), grad_normed_two),
        "ctx",
        axis=0,
        tiled=True,
    )
    y_both = after(added(y_a, links.core(y_b)), both_rows)
    y_sum = lax.psum_scatter(y_both, "ctx", scatter_dimension=0, tiled=True)
    layer_out = hidden_one + y_sum.astype(F32)
    links.label = "gkv"
    pair_terms = [pair_terms[0]] + [links.shift(pair_terms[step], -step) for step in steps]
    def columns_over_ctx(parts):
        whole = jnp.zeros_like(parts)
        whole = lax.dynamic_update_index_in_dim(whole, pick(parts, ctx), ctx, 0)
        for step in steps:
            piece = links.turn(pick(parts, (ctx + step) % ctx_size), step)
            whole = lax.dynamic_update_index_in_dim(whole, piece, (ctx - step) % ctx_size, 0)
        return whole

    def qkv_back(*refs):
        qkv_back_body(ctx_size, *refs)

    columns = (width + 2 * KV_WIDTH) // ctx_size
    grad_stream, parts = call(
        qkv_back,
        place,
        (*pair_terms, low_tokens, small, cosine, sine, grad_query, grad_hidden, grad_hidden_low, gain_two),
        weight_qkv,
        [(wide, F32), ((ctx_size, count + 16, columns + width // ctx_size), BF16)],
        0,
    )


    links.label = "gqkv_ctx"
    share = after(columns_over_ctx(parts), *ff_first)
    links.label = "ff_sum2"
    ff_second = reduce_next(links, ff_terms, ff_first)
    gain_sums = jnp.sum(share[:, count:].astype(F32), axis=0)[:2]
    share = share[:, :count].reshape(ctx_size * count, -1)
    share_o, share = share[:, columns:], share[:, :columns]
    bias_sums = jnp.sum(share.astype(F32), axis=0)
    q_columns, kv_columns = width // ctx_size, KV_WIDTH // ctx_size
    bounds = (0, q_columns, q_columns + kv_columns, columns)
    sums = [gain_sums[0, :q_columns], gain_sums[1, :q_columns]]
    sums += [bias_sums[i:j] for i, j in zip(bounds, bounds[1:])]
    sums = jnp.concatenate([x.reshape(fsdp_size, -1) for x in sums], axis=1)
    sums = jnp.pad(sums, ((0, 0), (0, columns - sums.shape[1])))
    sums = jnp.pad(sums[:, None], ((0, 0), (0, 15), (0, 0)))
    term = tn(both_rows[:, :width], share).reshape(fsdp_size, -1, columns)
    term = jnp.concatenate([term, sums], axis=1).astype(BF16)
    term_o = tn(both_rows[:, width:], share_o).astype(BF16).reshape(fsdp_size, -1, q_columns)
    term_o = jnp.pad(term_o, ((0, 0), (0, 16), (0, 0)))
    term = jnp.concatenate([term, term_o], axis=2)
    term = jnp.transpose(term.reshape(fsdp_size // 2, 2, *term.shape[1:]), (1, 0, 2, 3))
    links.label = "term_core"
    term = added(pick(term, core), links.core(pick(term, 1 - core)))
    links.label = "term_plane"
    total = pick(term, chip).astype(F32)
    for mask in range(1, fsdp_size // 2):
        total = total + links.plane(pick(term, chip ^ mask), 2 * mask).astype(F32)
    grad_packed, grad_o, sums = total[:-16, :columns], total[:-16, columns:], total[-16]
    vectors = []
    start = 0
    for size in (width, width, width, KV_WIDTH, KV_WIDTH):
        part = size // (ctx_size * fsdp_size)
        vectors.append(sums[start : start + part])
        start += part

    links.label = "final_core"
    links.label = "final_core"
    low, high = reduce_end(ff_terms, ff_first, ff_second)
    mine = jnp.where(even, low, high)
    got = links.core(jnp.where(even, high, low).astype(BF16)).astype(F32)
    ff_grads = jnp.concatenate([jnp.where(even, mine, got), jnp.where(even, got, mine)], axis=2)
    grad_gate, grad_up, grad_down = ff_grads[0], ff_grads[1], jnp.transpose(ff_grads[2])

    return (
        layer_out[None],
        grad_stream[None],
        vectors[0],
        grad_packed[:, :q_columns],
        vectors[2],
        grad_packed[:, q_columns : q_columns + kv_columns],
        vectors[3],
        grad_packed[:, q_columns + kv_columns :],
        vectors[4],
        grad_o,
        vectors[1],
        grad_gate,
        grad_up,
        grad_down,
    )


def solution(mesh):
    links = Links(mesh.shape["ctx"], mesh.shape["fsdp"])
    vector, matrix, stream = P(BOTH), P(BOTH, None), P("fsdp", "ctx", None)
    grid = P("fsdp", "ctx")
    in_specs = (
        stream,
        grid,
        vector,
        matrix,
        vector,
        matrix,
        vector,
        matrix,
        vector,
        matrix,
        vector,
        matrix,
        matrix,
        P(None, BOTH),
        stream,
    )
    out_specs = (
        stream,
        stream,
        vector,
        grid,
        vector,
        grid,
        vector,
        grid,
        vector,
        grid,
        vector,
        grid,
        grid,
        P("ctx", "fsdp"),
    )

    def run(*arrays):
        plane_of_four = mesh.shape["fsdp"] == 8 and arrays[3].shape[0] % 16 == 0
        form = per_device_plane_of_four if plane_of_four else per_device_any_mesh
        return form(*arrays, links=links)

    return jax.shard_map(run, mesh=mesh, in_specs=in_specs, out_specs=out_specs, check_vma=False)
```

```python
import jax
import jax.numpy as jnp
from jax import lax
from jax.experimental import pallas as pl
from jax.experimental.pallas import tpu as pltpu
from jax.sharding import PartitionSpec as P

QUERY_HEADS = 12
KEY_VALUE_HEADS = 2
HEAD_SIZE = 128
GROUP = QUERY_HEADS // KEY_VALUE_HEADS
KV_WIDTH = KEY_VALUE_HEADS * HEAD_SIZE
EPSILON = 1e-06
BACK_COST = 8 * 10**9
BOTH = ("ctx", "fsdp")
F32 = jnp.float32
BF16 = jnp.bfloat16


def dot(a, b, dims):
    return lax.dot_general(a, b, ((dims[:1], dims[1:]), ((), ())), preferred_element_type=F32)


def nn(a, b):
    return dot(a, b, (1, 0))


def nt(a, b):
    return dot(a, b, (1, 1))


def tn(a, b):
    return dot(a, b, (0, 0))


def rms_scale(matrix):
    return lax.rsqrt(jnp.mean(matrix * matrix, axis=-1, keepdims=True) + EPSILON)


def angle_tables(positions):
    step_index = jnp.arange(HEAD_SIZE // 2, dtype=F32) * 2.0
    frequency = 10000.0 ** (-step_index / HEAD_SIZE)
    angles = positions.astype(F32)[:, None] * frequency[None, :]
    return jnp.cos(angles)[:, None, :], jnp.sin(angles)[:, None, :]


def rotate(matrix, cosine, sine):
    rows = matrix.shape[0]
    heads = matrix.reshape(rows, -1, HEAD_SIZE)
    a, b = heads[..., : HEAD_SIZE // 2], heads[..., HEAD_SIZE // 2 :]
    turned = jnp.concatenate([a * cosine - b * sine, b * cosine + a * sine], axis=-1)
    return turned.reshape(rows, -1)


def pick(stacked, index):
    return lax.dynamic_index_in_dim(stacked, index, 0, keepdims=False)


class Links:
    def __init__(self, ctx_size, fsdp_size):
        self.ctx_size, self.fsdp_size = ctx_size, fsdp_size
        self.label = "move"
        self.planes = [m for m in (2, 4, 8, 16, 32, 64) if m < fsdp_size]

    def send(self, x, target):
        pairs = []
        for c in range(self.ctx_size):
            for f in range(self.fsdp_size):
                to = target(c, f)
                if to is not None:
                    pairs.append((c * self.fsdp_size + f, to[0] * self.fsdp_size + to[1]))
        with jax.named_scope(self.label):
            return lax.ppermute(x, BOTH, pairs)

    def core(self, x):
        return self.send(x, lambda c, f: (c, f ^ 1))

    def plane(self, x, mask):
        return self.send(x, lambda c, f: (c, f ^ mask))

    def turn(self, x, step):
        return self.send(x, lambda c, f: ((c + step) % self.ctx_size, f))

    def shift(self, x, step):
        return self.send(
            x, lambda c, f: (c + step, f) if 0 <= c + step < self.ctx_size else None
        )


def plane_gather(links, shard):
    first, second, *rest = links.planes
    half = shard.shape[0] // 2
    a = links.plane(shard, first)
    b = links.plane(shard, second)
    low = links.plane(b[:half], first)
    high = links.plane(a[half:], second)
    pieces = {0: shard, first: a, second: b, first | second: jnp.concatenate([low, high])}
    for mask in rest:
        pieces.update({had | mask: links.plane(piece, mask) for had, piece in pieces.items()})
    return pieces


def ff_weight(links, ctx, chip, core, shard):
    ctx_size = links.ctx_size
    rows, hidden = shard.shape
    block = hidden // (2 * ctx_size)
    parts = jnp.transpose(shard.reshape(rows, ctx_size, 2, block), (2, 1, 0, 3))
    mine, other = pick(parts, core), pick(parts, 1 - core)
    got = links.core(other)
    even = core == 0
    pairs = jnp.stack([jnp.where(even, mine, got), jnp.where(even, got, mine)], axis=1)
    by_source = jnp.zeros_like(pairs)
    by_source = lax.dynamic_update_index_in_dim(by_source, pick(pairs, ctx), ctx, 0)
    for step in range(1, ctx_size):
        piece = links.turn(pick(pairs, (ctx + step) % ctx_size), step)
        by_source = lax.dynamic_update_index_in_dim(by_source, piece, (ctx - step) % ctx_size, 0)
    pieces = plane_gather(links, by_source)
    whole = jnp.zeros((ctx_size, links.fsdp_size // 2, 2, rows, block), shard.dtype)
    for mask, piece in pieces.items():
        whole = lax.dynamic_update_index_in_dim(whole, piece, chip ^ (mask // 2), 1)
    return whole.reshape(-1, block)


def spread_tokens(links, x):
    row = jnp.concatenate([x] + [links.turn(x, step) for step in range(1, links.ctx_size)])
    return jnp.concatenate([row, links.core(row)])


def collect_tokens(links, partial):
    rows = partial.shape[0] // 2
    got = links.core(partial[rows:].astype(BF16))
    count = rows // links.ctx_size
    row = (partial[:rows].astype(F32) + got.astype(F32)).reshape(links.ctx_size, count, -1)
    total = row[0]
    for step in range(1, links.ctx_size):
        total = total + links.turn(row[step].astype(BF16), -step).astype(F32)
    return total


def per_device_any_mesh(
    tokens,
    positions,
    norm1_gain,
    q_weight,
    q_bias,
    key_projection,
    key_bias_vector,
    value_projection,
    value_bias_vector,
    o_weight,
    norm2_gain,
    gate_weight,
    up_weight,
    down_weight,
    cotangent,
    *,
    links,
):
    ctx_size, fsdp_size = links.ctx_size, links.fsdp_size
    ctx, row_index = lax.axis_index("ctx"), lax.axis_index("fsdp")
    chip, core = row_index // 2, row_index % 2
    count, width = tokens.shape[1:]
    scale = HEAD_SIZE ** (-0.5)
    even = core == 0

    shard_rows = q_weight.shape[0]

    def column(x):
        return jnp.pad(x, (0, shard_rows - x.shape[0]))[:, None]

    kv_bias_rows = key_bias_vector.shape[0]
    extra = jnp.concatenate(
        [
            column(x)
            for x in (norm1_gain, q_bias, norm2_gain, key_bias_vector, value_bias_vector)
        ],
        axis=1,
    )
    extra = jnp.pad(extra, ((0, 0), (0, 128 - extra.shape[1])))
    packed = jnp.concatenate([q_weight, key_projection, value_projection, extra], axis=1)
    packed = lax.all_gather(packed, BOTH, axis=0, tiled=True)
    weight_o = lax.all_gather(o_weight, BOTH, axis=0, tiled=True)

    weight_gate = ff_weight(links, ctx, chip, core, gate_weight)
    weight_up = ff_weight(links, ctx, chip, core, up_weight)
    weight_down = ff_weight(links, ctx, chip, core, jnp.transpose(down_weight))

    qkv_width = width + 2 * KV_WIDTH
    weight_qkv = packed[:, :qkv_width]
    small = jnp.transpose(packed[:, qkv_width:])[:5].astype(F32)
    gain_one, bias_q, gain_two = small[0:1], small[1:2], small[2:3]

    def bias_of(row):
        return row.reshape(-1, shard_rows)[:, :kv_bias_rows].reshape(1, -1)

    bias_k, bias_v = bias_of(small[3]), bias_of(small[4])
    out_low = cotangent[0]
    group_out = spread_tokens(links, out_low)

    stream = tokens[0].astype(F32)
    scale_one = rms_scale(stream)
    unit_one = stream * scale_one
    normed_one = (unit_one * gain_one).astype(BF16)
    cosine, sine = angle_tables(positions[0])
    linear = nn(normed_one, weight_qkv)
    query = rotate(linear[:, :width] + bias_q, cosine, sine).astype(BF16)
    key = rotate(linear[:, width : width + KV_WIDTH] + bias_k, cosine, sine).astype(BF16)
    value = (linear[:, width + KV_WIDTH :] + bias_v).astype(BF16)
    pairs = jnp.concatenate([key, value], axis=1)
    row_pairs = jnp.concatenate(
        [pairs] + [links.shift(pairs, step) for step in range(1, ctx_size)]
    )
    keys = row_pairs[:, :KV_WIDTH].reshape(-1, KEY_VALUE_HEADS, HEAD_SIZE)
    values = row_pairs[:, KV_WIDTH:].reshape(-1, KEY_VALUE_HEADS, HEAD_SIZE)
    local_index = jnp.arange(count)
    key_index = jnp.concatenate(
        [(ctx - step) * count + local_index for step in range(ctx_size)]
    )
    query_index = ctx * count + local_index
    doc_start = query_index - positions[0]
    allowed = (key_index[None, :] >= doc_start[:, None]) & (
        key_index[None, :] <= query_index[:, None]
    )
    query_heads = query.reshape(count, KEY_VALUE_HEADS, GROUP, HEAD_SIZE)
    scores = jnp.einsum("qkgd,rkd->kgqr", query_heads, keys, preferred_element_type=F32) * scale
    scores = jnp.where(allowed, scores, -1e30)
    top = jnp.max(scores, axis=-1, keepdims=True)
    weights = jnp.where(allowed, jnp.exp(scores - top), 0.0)
    probs = weights / jnp.sum(weights, axis=-1, keepdims=True)
    probs_low = probs.astype(BF16)
    mixed = jnp.einsum("kgqr,rkd->qkgd", probs_low, values, preferred_element_type=F32)
    mixed_low = mixed.reshape(count, -1).astype(BF16)
    hidden_one = stream + nn(mixed_low, weight_o)

    scale_two = rms_scale(hidden_one)
    unit_two = hidden_one * scale_two
    normed_two = (unit_two * gain_two).astype(BF16)
    group_normed = spread_tokens(links, normed_two)
    gate_pre = nn(group_normed, weight_gate)
    up_pre = nn(group_normed, weight_up)
    grad_act = nn(group_out, weight_down)
    sigmoid_gate = jax.nn.sigmoid(gate_pre)
    activated = (gate_pre * sigmoid_gate * up_pre).astype(BF16)
    grad_gate_low = (
        grad_act * up_pre * sigmoid_gate * (1.0 + gate_pre * (1.0 - sigmoid_gate))
    ).astype(BF16)
    grad_up_low = (grad_act * gate_pre * sigmoid_gate).astype(BF16)
    grad_normed_two = collect_tokens(
        links, nt(grad_gate_low, weight_gate) + nt(grad_up_low, weight_up)
    )
    layer_out = hidden_one + collect_tokens(links, nt(activated, weight_down))

    planes = [
        [c * fsdp_size + 2 * p + k for p in range(fsdp_size // 2)]
        for c in range(ctx_size)
        for k in range(2)
    ]

    def ff_grad(left, right):
        term = tn(left, right).astype(BF16)
        part = lax.psum_scatter(
            term, BOTH, scatter_dimension=0, tiled=True, axis_index_groups=planes
        )
        part = part.reshape(2, -1, part.shape[1])
        mine, got = pick(part, core), links.core(pick(part, 1 - core))
        return jnp.concatenate(
            [jnp.where(even, mine, got), jnp.where(even, got, mine)], axis=1
        ).astype(F32)

    grad_gate = ff_grad(group_normed, grad_gate_low)
    grad_up = ff_grad(group_normed, grad_up_low)
    grad_down = jnp.transpose(ff_grad(group_out, activated))

    grad_gain_two = jnp.sum(grad_normed_two * unit_two, axis=0)
    weighted_two = grad_normed_two * gain_two
    grad_hidden = out_low.astype(F32) + scale_two * (
        weighted_two - unit_two * jnp.mean(weighted_two * unit_two, axis=-1, keepdims=True)
    )

    grad_hidden_low = grad_hidden.astype(BF16)
    grad_mixed = nt(grad_hidden_low, weight_o).astype(BF16)
    grad_mixed = grad_mixed.reshape(count, KEY_VALUE_HEADS, GROUP, HEAD_SIZE)
    grad_probs = jnp.einsum("qkgd,rkd->kgqr", grad_mixed, values, preferred_element_type=F32)
    delta = jnp.sum(probs * grad_probs, axis=-1, keepdims=True)
    grad_scores = (probs * (grad_probs - delta)).astype(BF16)
    grad_query = jnp.einsum("kgqr,rkd->qkgd", grad_scores, keys, preferred_element_type=F32)
    grad_key = (
        jnp.einsum("kgqr,qkgd->rkd", grad_scores, query_heads, preferred_element_type=F32) * scale
    )
    grad_value = jnp.einsum("kgqr,qkgd->rkd", probs_low, grad_mixed, preferred_element_type=F32)
    pair_terms = jnp.concatenate(
        [grad_key.reshape(-1, KV_WIDTH), grad_value.reshape(-1, KV_WIDTH)], axis=1
    ).reshape(ctx_size, count, -1)
    pair_grads = pair_terms[0]
    for step in range(1, ctx_size):
        pair_grads = pair_grads + links.shift(pair_terms[step].astype(BF16), -step).astype(F32)
    grad_q_low = rotate(grad_query.reshape(count, -1) * scale, cosine, -sine).astype(BF16)
    grad_k_low = rotate(pair_grads[:, :KV_WIDTH], cosine, -sine).astype(BF16)
    grad_v_low = pair_grads[:, KV_WIDTH:].astype(BF16)
    grad_qkv = jnp.concatenate([grad_q_low, grad_k_low, grad_v_low], axis=1)
    grad_normed_one = nt(grad_qkv, weight_qkv)
    grad_gain_one = jnp.sum(grad_normed_one * unit_one, axis=0)
    weighted_one = grad_normed_one * gain_one
    grad_stream = grad_hidden + scale_one * (
        weighted_one - unit_one * jnp.mean(weighted_one * unit_one, axis=-1, keepdims=True)
    )

    def columns_over_ctx(arrays):
        parts = jnp.concatenate([x.reshape(count, ctx_size, -1) for x in arrays], axis=2)
        parts = jnp.transpose(parts, (1, 0, 2))
        whole = jnp.zeros_like(parts)
        whole = lax.dynamic_update_index_in_dim(whole, pick(parts, ctx), ctx, 0)
        for step in range(1, ctx_size):
            piece = links.turn(pick(parts, (ctx + step) % ctx_size), step)
            whole = lax.dynamic_update_index_in_dim(whole, piece, (ctx - step) % ctx_size, 0)
        return whole.reshape(ctx_size * count, -1)

    def attention_grad(rows, arrays):
        left = lax.all_gather(rows, "ctx", axis=0, tiled=True)
        term = tn(left, columns_over_ctx(arrays)).astype(BF16)
        return lax.psum_scatter(term, "fsdp", scatter_dimension=0, tiled=True).astype(F32)

    grad_o = attention_grad(mixed_low, [grad_hidden_low])
    grad_packed = attention_grad(normed_one, [grad_q_low, grad_k_low, grad_v_low])
    q_columns, kv_columns = width // ctx_size, KV_WIDTH // ctx_size

    sums = jnp.concatenate(
        [grad_gain_one, grad_gain_two, jnp.sum(grad_qkv.astype(F32), axis=0)]
    )
    sums = lax.psum(sums, BOTH)
    device = ctx * fsdp_size + row_index

    def own(start, size):
        part = size // (ctx_size * fsdp_size)
        return lax.dynamic_slice_in_dim(sums, start + device * part, part)

    return (
        layer_out[None],
        grad_stream[None],
        own(0, width),
        grad_packed[:, :q_columns],
        own(2 * width, width),
        grad_packed[:, q_columns : q_columns + kv_columns],
        own(3 * width, KV_WIDTH),
        grad_packed[:, q_columns + kv_columns :],
        own(3 * width + KV_WIDTH, KV_WIDTH),
        grad_o,
        own(width, width),
        grad_gate,
        grad_up,
        grad_down,
    )


def after(x, *others):
    return lax.optimization_barrier((x, *others))[0]


def phase(*groups):
    flat = lax.optimization_barrier(tuple(x for group in groups for x in group))
    out = []
    for group in groups:
        out.append(list(flat[: len(group)]))
        flat = flat[len(group) :]
    return out


def plane_start(links, shard):
    return links.plane(shard, 2), links.plane(shard, 4)


def plane_end(links, shard, a, b):
    half = shard.shape[0] // 2
    return shard, a, b, links.plane(b[:half], 2), links.plane(a[half:], 4)


def ff_kernel(layout, sizes, place, normed, out_grad, *refs):
    ctx_size, chips, rows = sizes
    pieces, refs = refs[: len(layout)], refs[len(layout) :]
    act_ref, gate_ref, up_ref, down_ref, y_ref, weights, semaphores = refs

    @pl.when(pl.program_id(0) == 0)
    def _():
        ctx, chip = place[0], place[1]
        for which in range(3):
            for (entries, mask, _), piece in zip(layout, pieces):
                for i, (step, core) in enumerate(entries):
                    source = lax.rem(ctx - step + ctx_size, ctx_size)
                    start = ((source * chips + (chip ^ mask)) * 2 + core) * rows
                    pltpu.make_async_copy(
                        piece.at[i, which],
                        weights.at[which, pl.ds(pl.multiple_of(start, rows), rows)],
                        semaphores.at[which],
                    ).start()

    def arrived(which):
        @pl.when(pl.program_id(0) == 0)
        def _():
            pltpu.make_async_copy(
                weights.at[which], weights.at[which], semaphores.at[which]
            ).wait()

    x, gy = normed[...], out_grad[...]
    arrived(0)
    gate = nn(x, weights[0])
    arrived(1)
    up = nn(x, weights[1])
    arrived(2)
    grad = nn(gy, weights[2])
    sigmoid = 1.0 / (1.0 + jnp.exp(-gate))
    silu = gate * sigmoid
    act = (silu * up).astype(BF16)
    grad_gate = (grad * up * sigmoid * (1.0 + gate * (1.0 - sigmoid))).astype(BF16)
    grad_up = (grad * silu).astype(BF16)
    act_ref[...] = act
    gate_ref[...] = grad_gate
    up_ref[...] = grad_up
    down_ref[...] = (nt(grad_gate, weights[0]) + nt(grad_up, weights[1])).astype(BF16)
    y_ref[...] = nt(act, weights[2]).astype(BF16)


def feed_forward(links, layout, place, normed, out_grad):
    tokens, width = normed.shape
    rows, block = layout[0][2].shape[2:]
    tile = 256
    wide = pl.BlockSpec((tile, width), lambda i, place: (i, 0))
    narrow = pl.BlockSpec((tile, block), lambda i, place: (i, 0))
    small = jax.ShapeDtypeStruct((tokens, block), BF16)
    large = jax.ShapeDtypeStruct((tokens, width), BF16)
    sizes = (links.ctx_size, links.fsdp_size // 2, rows)

    def body(*refs):
        ff_kernel(layout, sizes, *refs)

    return pl.pallas_call(
        body,
        grid_spec=pltpu.PrefetchScalarGridSpec(
            num_scalar_prefetch=1,
            grid=(tokens // tile,),
            in_specs=[wide, wide] + [pl.BlockSpec(memory_space=pl.ANY)] * len(layout),
            out_specs=[narrow, narrow, narrow, wide, wide],
            scratch_shapes=[
                pltpu.VMEM((3, width, block), BF16),
                pltpu.SemaphoreType.DMA((3,)),
            ],
        ),
        out_shape=[small, small, small, large, large],
        compiler_params=pltpu.CompilerParams(vmem_limit_bytes=56 * 2**20),
        cost_estimate=pl.CostEstimate(flops=0, bytes_accessed=0, transcendentals=0),
    )(place, normed, out_grad, *[piece for _, _, piece in layout])


def grad_kernel(place, *refs):
    lefts, rights, outs = refs[:8], refs[8:14], refs[14:]
    low, high = outs[: len(outs) // 2], outs[len(outs) // 2 :]
    for which in range(3):
        first = 4 * (which // 2)
        for parts, (left_a, left_b), core in (
            (low, lefts[first : first + 2], 0),
            (high, lefts[first + 2 : first + 4], 1),
        ):
            out, at = (parts[0], which) if len(parts) == 1 else (parts[which > 0], max(which - 1, 0))
            half = left_a.shape[1] // 2
            rows = slice(core * half, (core + 1) * half)
            right_a, right_b = rights[2 * which : 2 * which + 2]
            term = tn(left_a[:, rows], right_a[...]) + tn(left_b[:, rows], right_b[...])
            out[0, at] = term.astype(BF16)


def ff_grad_terms(place, lefts, rights, low_at, high_at, parts):
    tokens, width = lefts[0].shape
    block = rights[0].shape[1]
    part = width // 4

    def left(at):
        return pl.BlockSpec((tokens, part), lambda j, place: (0, place[1] ^ at(j)))

    right = pl.BlockSpec((tokens, block), lambda j, place: (0, 0))
    outs = [pl.BlockSpec((1, n, part // 2, block), lambda j, place: (j, 0, 0, 0)) for n in parts]
    low, high = left(low_at), left(high_at)
    x_a, x_b, y_a, y_b = lefts
    return pl.pallas_call(
        grad_kernel,
        grid_spec=pltpu.PrefetchScalarGridSpec(
            num_scalar_prefetch=1,
            grid=(2,),
            in_specs=[low, low, high, high] * 2 + [right] * 6,
            out_specs=outs * 2,
        ),
        out_shape=[jax.ShapeDtypeStruct((2, n, part // 2, block), BF16) for n in parts] * 2,
        compiler_params=pltpu.CompilerParams(vmem_limit_bytes=56 * 2**20),
        cost_estimate=pl.CostEstimate(flops=0, bytes_accessed=0, transcendentals=0),
    )(place, x_a, x_b, x_a, x_b, y_a, y_b, y_a, y_b, *rights)


def added(a, b):
    return (a.astype(F32) + b.astype(F32)).astype(BF16)


def reduce_start(links, terms):
    return [links.plane(x, mask) for x, mask in zip(terms, (4, 4, 2, 2))]


def add_pairs_kernel(*refs):
    for i, out in enumerate(refs[6:]):
        keep, one, rest = refs[3 * i : 3 * i + 3]
        out[:1] = (keep[0, :1].astype(F32) + one[0].astype(F32)).astype(BF16)
        out[1:] = (keep[0, 1:].astype(F32) + rest[0].astype(F32)).astype(BF16)


def first_specs(index):
    def spec(x):
        return pl.BlockSpec((1, *x.shape[1:]), lambda i, *place: (index, 0, 0, 0))

    return spec


def reduce_next(links, terms, first):
    shape = terms[0].shape
    arrays = (terms[0], first[0], first[1], terms[1], first[2], first[3])
    spec = first_specs(1)
    whole = pl.BlockSpec(shape[1:], lambda i: (0, 0, 0))
    low, high = pl.pallas_call(
        add_pairs_kernel,
        grid=(1,),
        in_specs=[spec(x) for x in arrays],
        out_specs=[whole] * 2,
        out_shape=[jax.ShapeDtypeStruct(shape[1:], BF16)] * 2,
        compiler_params=pltpu.CompilerParams(vmem_limit_bytes=56 * 2**20),
        cost_estimate=pl.CostEstimate(flops=0, bytes_accessed=0, transcendentals=0),
    )(*arrays)
    return links.plane(low, 2), links.plane(high, 4)


def reduce_end_kernel(place, *refs):
    low, high, (mine, send) = refs[:4], refs[4:8], refs[8:]

    def write(ref, parts):
        keep, one, rest, last = parts
        total = keep[0, :1].astype(F32) + one[0].astype(F32) + last[:1].astype(F32)
        ref[:1] = total.astype(ref.dtype)
        total = keep[0, 1:].astype(F32) + rest[0].astype(F32) + last[1:].astype(F32)
        ref[1:] = total.astype(ref.dtype)

    @pl.when(place[2] == 0)
    def _():
        write(mine, low)
        write(send, high)

    @pl.when(place[2] != 0)
    def _():
        write(mine, high)
        write(send, low)


def reduce_end(place, terms, first, second):
    shape = terms[0].shape[1:]
    spec = first_specs(0)
    whole = pl.BlockSpec(shape, lambda i, place: (0, 0, 0))
    low = (terms[0], first[0], first[1])
    high = (terms[1], first[2], first[3])
    return pl.pallas_call(
        reduce_end_kernel,
        grid_spec=pltpu.PrefetchScalarGridSpec(
            num_scalar_prefetch=1,
            grid=(1,),
            in_specs=[*map(spec, low), whole, *map(spec, high), whole],
            out_specs=[whole] * 2,
        ),
        out_shape=[jax.ShapeDtypeStruct(shape, F32), jax.ShapeDtypeStruct(shape, BF16)],
        compiler_params=pltpu.CompilerParams(vmem_limit_bytes=56 * 2**20),
        cost_estimate=pl.CostEstimate(flops=12 * 10**9, bytes_accessed=0, transcendentals=0),
    )(place, *low, second[0], *high, second[1])


def join_cores_kernel(place, mine, got, gate, up, down):
    block = mine.shape[2]

    def write(even, odd):
        for which, ref in enumerate((gate, up)):
            ref[...] = jnp.concatenate([even(which), odd(which)], axis=1)
        down[:block] = jnp.transpose(even(2))
        down[block:] = jnp.transpose(odd(2))

    def own(which):
        return mine[which]

    def others(which):
        return got[which].astype(F32)

    @pl.when(place[2] == 0)
    def _():
        write(own, others)

    @pl.when(place[2] != 0)
    def _():
        write(others, own)


def split_kernel(place, gate, up, down, mine, other):
    block = mine.shape[3]

    def write(core):
        for which, ref in enumerate((gate, up, down)):
            for target in range(mine.shape[0]):
                start = (2 * target + core) * block
                mine[target, which] = ref[:, start : start + block]
                start = (2 * target + 1 - core) * block
                other[target, which] = ref[:, start : start + block]

    @pl.when(place[2] == 0)
    def _():
        write(0)

    @pl.when(place[2] != 0)
    def _():
        write(1)


def split_hidden(links, place, shards):
    rows, hidden = shards[0].shape
    whole = pl.BlockSpec((rows, hidden), lambda i, place: (0, 0))
    shape = (links.ctx_size, 3, rows, hidden // (2 * links.ctx_size))
    out = pl.BlockSpec(shape, lambda i, place: (0, 0, 0, 0))
    return pl.pallas_call(
        split_kernel,
        grid_spec=pltpu.PrefetchScalarGridSpec(
            num_scalar_prefetch=1, grid=(1,), in_specs=[whole] * 3, out_specs=[out] * 2
        ),
        out_shape=[jax.ShapeDtypeStruct(shape, BF16)] * 2,
        compiler_params=pltpu.CompilerParams(vmem_limit_bytes=32 * 2**20),
    )(place, *shards)


class Rows:
    def __init__(self, sizes, pieces, layout, first, columns):
        self.sizes, self.pieces, self.layout = sizes, pieces, layout
        self.first, self.columns = first, columns
        self.rows = pieces[0].shape[-2]
        self.shape = (2 * sizes[0] * sizes[1] * self.rows, columns)

    def start(self, place, refs, weight, semaphore):
        ctx_size, chips = self.sizes
        for piece, index, step, mask, turned in self.layout:
            source = lax.rem(place[0] - step + ctx_size, ctx_size)
            start = ((source * chips + (place[1] ^ mask)) * 2 + (place[2] ^ turned)) * self.rows
            pltpu.make_async_copy(
                refs[piece].at[(*index, slice(None), pl.ds(self.first, self.columns))],
                weight.at[pl.ds(pl.multiple_of(start, self.rows), self.rows)],
                semaphore,
            ).start()


def rows_layout(ctx_size):
    half = ctx_size // 2
    layout = []
    for step in range(ctx_size):
        layout += [(mask, (step,), step, mask, 0) for mask in range(3)]
        layout.append((3, (step,), step, 3, 0) if step < half else (4, (step - half,), step, 3, 0))
        layout.append((5, (step,), step, 0, 1))
        layout += [(6, (i * ctx_size + step,), step, i + 1, 1) for i in range(3)]
    return layout


def wait_all(weight, semaphore):
    pltpu.make_async_copy(weight, weight, semaphore).wait()


def call(body, place, arrays, weight, out_shapes, cost, scratch=()):
    any_spec = pl.BlockSpec(memory_space=pl.ANY)
    vmem = pl.BlockSpec(memory_space=pltpu.VMEM)
    count, pieces = len(arrays), len(weight.pieces)

    def kernel(place, *refs):
        ins, parts, outs = refs[:count], refs[count : count + pieces], refs[count + pieces : -2]
        whole, semaphore = refs[-2:]
        weight.start(place, parts, whole, semaphore)
        body(place, ins, outs, whole, lambda: wait_all(whole, semaphore))

    return pl.pallas_call(
        kernel,
        in_specs=[pl.BlockSpec(memory_space=pltpu.SMEM)] + [vmem] * count + [any_spec] * pieces,
        out_specs=[vmem] * len(out_shapes),
        out_shape=[jax.ShapeDtypeStruct(shape, dtype) for shape, dtype in out_shapes],
        scratch_shapes=[*scratch, pltpu.VMEM(weight.shape, BF16), pltpu.SemaphoreType.DMA],
        compiler_params=pltpu.CompilerParams(vmem_limit_bytes=56 * 2**20),
        cost_estimate=pl.CostEstimate(flops=cost, bytes_accessed=0, transcendentals=0),
    )(place, *arrays, *weight.pieces)


def turn_halves(x, cosine, sine):
    return x * cosine + pltpu.roll(x, HEAD_SIZE // 2, 1) * sine


def turned_heads(x, cosine, sine):
    heads = [x[:, i : i + HEAD_SIZE] for i in range(0, x.shape[1], HEAD_SIZE)]
    return jnp.concatenate([turn_halves(x, cosine, sine) for x in heads], axis=1)


def qkv_body(shard_rows, place, ins, outs, weight, wait):
    tokens, cosine, sine = ins
    normed_ref, query_ref, pairs_ref, small_ref = outs
    width = tokens.shape[1]
    qkv_width = width + 2 * KV_WIDTH
    x = tokens[...].astype(F32)
    unit = x * rms_scale(x)
    wait()
    small = jnp.transpose(weight[:, qkv_width:].astype(F32))[:8]
    bias_rows = KV_WIDTH * shard_rows // width
    row = lax.broadcasted_iota(jnp.int32, (width, KV_WIDTH), 0)
    at = lax.broadcasted_iota(jnp.int32, (width, KV_WIDTH), 1)
    chosen = row == (at // bias_rows) * shard_rows + at % bias_rows
    kv_bias = nn(small.astype(BF16), chosen.astype(BF16))
    normed = (unit * small[0:1]).astype(BF16)
    normed_ref[...] = normed
    small_ref[...] = small
    linear = nn(normed, weight[:, :qkv_width])
    query = linear[:, :width] + small[1:2]
    key = linear[:, width : width + KV_WIDTH] + kv_bias[3:4]
    query_ref[...] = turned_heads(query, cosine[...], sine[...]).astype(BF16)
    pairs_ref[:, :KV_WIDTH] = turned_heads(key, cosine[...], sine[...]).astype(BF16)
    pairs_ref[:, KV_WIDTH:] = (linear[:, width + KV_WIDTH :] + kv_bias[4:5]).astype(BF16)


def allowed_keys(ctx, positions, blocks):
    count = positions.shape[0]
    shape = (count, blocks * count)
    column = lax.broadcasted_iota(jnp.int32, shape, 1)
    query = ctx * count + lax.broadcasted_iota(jnp.int32, shape, 0)
    key = (ctx - column // count) * count + column % count
    return (key >= query - positions) & (key <= query)


def heads_of(x, group):
    first = group * GROUP
    return jnp.concatenate(
        [x[:, i * HEAD_SIZE : (i + 1) * HEAD_SIZE] for i in range(first, first + GROUP)], axis=0
    )


def softmax_of(query, keys, allowed):
    scores = nt(query, keys) * HEAD_SIZE ** (-0.5)
    scores = jnp.where(allowed, scores, -1e30)
    weights = jnp.exp(scores - jnp.max(scores, axis=-1, keepdims=True))
    weights = jnp.where(allowed, weights, 0.0)
    return weights / jnp.sum(weights, axis=-1, keepdims=True)


def group_pairs(blocks, group):
    def columns(start):
        return jnp.concatenate([b[:, start : start + HEAD_SIZE] for b in blocks], axis=0)

    return columns(group * HEAD_SIZE), columns(KV_WIDTH + group * HEAD_SIZE)


def mix_body(place, ins, outs, weight, wait):
    tokens, small, positions, query, *blocks = ins
    mixed_ref, hidden_ref, normed_ref = outs
    count = tokens.shape[0]
    allowed = allowed_keys(place[0], positions[...], len(blocks))
    allowed = jnp.concatenate([allowed.astype(F32)] * GROUP, axis=0) > 0
    for group in range(KEY_VALUE_HEADS):
        keys, values = group_pairs(blocks, group)
        probs = softmax_of(heads_of(query, group), keys, allowed)
        mixed = nn(probs.astype(BF16), values).astype(BF16)
        for h in range(GROUP):
            start = (group * GROUP + h) * HEAD_SIZE
            mixed_ref[:, start : start + HEAD_SIZE] = mixed[h * count : (h + 1) * count]
    wait()
    hidden = tokens[...].astype(F32) + nn(mixed_ref[...], weight[...])
    hidden_ref[...] = hidden
    normed_ref[...] = (hidden * rms_scale(hidden) * small[2:3]).astype(BF16)


def norm_back(unit, scale, grad, gain):
    weighted = grad * gain
    return scale * (weighted - unit * jnp.mean(weighted * unit, axis=-1, keepdims=True))


def mix_back_body(steps, place, ins, outs, weight, wait):
    terms, ins = ins[:steps], ins[steps:]
    hidden_ref, small, out_grad, positions, query, cosine, sine, *blocks = ins
    grad_hidden_ref, low_ref, grad_query_ref, gain_ref, *pair_refs = outs
    count = hidden_ref.shape[0]
    hidden = hidden_ref[...]
    scale = rms_scale(hidden)
    unit = hidden * scale
    grad = terms[0][...].astype(F32)
    for term in terms[1:]:
        grad = grad + term[...].astype(F32)
    gain_ref[...] = jnp.sum(grad * unit, axis=0, keepdims=True)
    grad_hidden = out_grad[...].astype(F32) + norm_back(unit, scale, grad, small[2:3])
    grad_hidden_ref[...] = grad_hidden
    low = grad_hidden.astype(BF16)
    low_ref[...] = low
    wait()
    grad_mixed = nt(low, weight[...]).astype(BF16)
    allowed = allowed_keys(place[0], positions[...], len(blocks))
    allowed = jnp.concatenate([allowed.astype(F32)] * GROUP, axis=0) > 0
    score_scale = HEAD_SIZE ** (-0.5)
    for group in range(KEY_VALUE_HEADS):
        keys, values = group_pairs(blocks, group)
        queries, grads = heads_of(query, group), heads_of(grad_mixed, group)
        probs = softmax_of(queries, keys, allowed)
        grad_probs = nt(grads, values)
        delta = jnp.sum(probs * grad_probs, axis=-1, keepdims=True)
        grad_scores = (probs * (grad_probs - delta)).astype(BF16)
        grad_query = nn(grad_scores, keys) * score_scale
        for h in range(GROUP):
            start = (group * GROUP + h) * HEAD_SIZE
            grad_query_ref[:, start : start + HEAD_SIZE] = turn_halves(
                grad_query[h * count : (h + 1) * count], cosine[...], -sine[...]
            ).astype(BF16)
        grad_key = (tn(grad_scores, queries) * score_scale).astype(BF16)
        grad_value = tn(probs.astype(BF16), grads).astype(BF16)
        start = group * HEAD_SIZE
        for block, ref in enumerate(pair_refs):
            rows = slice(block * count, (block + 1) * count)
            ref[:, start : start + HEAD_SIZE] = grad_key[rows]
            ref[:, KV_WIDTH + start : KV_WIDTH + start + HEAD_SIZE] = grad_value[rows]


def qkv_back_body(steps, place, ins, outs, weight, wait):
    terms, ins = ins[:steps], ins[steps:]
    tokens, small, cosine, sine, grad_query, grad_hidden, grad_hidden_low, gain_two = ins
    stream_ref, *share_refs, share_ref = outs
    count, width = tokens.shape
    pairs = terms[0][...].astype(F32)
    for term in terms[1:]:
        pairs = pairs + term[...].astype(F32)
    grad_key = turned_heads(pairs[:, :KV_WIDTH], cosine[...], -sine[...]).astype(BF16)
    grad_value = pairs[:, KV_WIDTH:].astype(BF16)
    wait()
    kv_end = width + KV_WIDTH
    grad = (
        nt(grad_query[...], weight[:, :width])
        + nt(grad_key, weight[:, width:kv_end])
        + nt(grad_value, weight[:, kv_end : kv_end + KV_WIDTH])
    )
    x = tokens[...].astype(F32)
    scale = rms_scale(x)
    unit = x * scale
    stream_ref[...] = grad_hidden[...] + norm_back(unit, scale, grad, small[0:1])
    gains = jnp.concatenate([jnp.sum(grad * unit, axis=0, keepdims=True), gain_two[...]], axis=0)
    gains = jnp.concatenate([gains, jnp.zeros((14, width), F32)], axis=0).astype(BF16)
    targets = share_ref.shape[0]
    q_columns, kv_columns = width // targets, KV_WIDTH // targets
    for target in range(targets):
        q, kv = target * q_columns, target * kv_columns
        share_ref[target, :count, :q_columns] = grad_query[:, q : q + q_columns]
        kv_end = q_columns + 2 * kv_columns
        share_ref[target, :count, q_columns:kv_end] = jnp.concatenate(
            [grad_key[:, kv : kv + kv_columns], grad_value[:, kv : kv + kv_columns]], axis=1
        )
        share_ref[target, :count, kv_end:] = grad_hidden_low[:, q : q + q_columns]
        share_ref[target, count:, :q_columns] = gains[:, q : q + q_columns]
        share_ref[target, count:, q_columns:] = jnp.zeros(
            (16, share_ref.shape[2] - q_columns), BF16
        )
    for step, ref in enumerate(share_refs):
        ref[...] = share_ref[lax.rem(place[0] + step, targets)]


def term_kernel(place, *refs):
    *shares, normed_rows, mixed_rows, mine, other, share, terms, vectors = refs
    ctx_size, width = len(shares), normed_rows.shape[1]
    count = normed_rows.shape[0] // ctx_size
    chips, height = mine.shape[0], mine.shape[1] - 16
    devices = 2 * chips
    q_columns, kv_columns = width // ctx_size, KV_WIDTH // ctx_size
    kv_end = q_columns + 2 * kv_columns
    gains = jnp.zeros((16, q_columns), F32)
    for step, ref in enumerate(shares):
        source = lax.rem(place[0] - step + ctx_size, ctx_size)
        share[pl.ds(pl.multiple_of(source * count, count), count)] = ref[:count]
        gains = gains + ref[count:, :q_columns].astype(F32)
    terms[:, :kv_end] = tn(normed_rows[...], share[:, :kv_end])
    terms[:, kv_end:] = tn(mixed_rows[...], share[:, kv_end:])
    biases = jnp.sum(share[:, :kv_end].astype(F32), axis=0, keepdims=True)
    vectors[...] = jnp.zeros_like(vectors)
    parts = (gains[0:1], gains[1:2], biases[:, :q_columns])
    parts += (biases[:, q_columns : q_columns + kv_columns], biases[:, q_columns + kv_columns :])
    for f in range(devices):
        start = 0
        for part in parts:
            size = part.shape[1] // devices
            vectors[f : f + 1, start : start + size] = part[:, f * size : (f + 1) * size]
            start += size
    first = lax.broadcasted_iota(jnp.int32, (16, terms.shape[1]), 0) == 0
    for ref, core in ((mine, place[2]), (other, 1 - place[2])):
        for mask in range(chips):
            f = (place[1] ^ mask) * 2 + core
            start = pl.multiple_of(f * height, 64)
            ref[mask, :height] = terms[pl.ds(start, height)].astype(BF16)
            row = jnp.broadcast_to(vectors[pl.ds(f, 1)], first.shape)
            ref[mask, height:] = jnp.where(first, row, 0.0).astype(BF16)


def sum_cores_kernel(mine, got, keep, *sends):
    keep[...] = mine[0].astype(F32) + got[0].astype(F32)
    for mask, ref in enumerate(sends, 1):
        ref[...] = (mine[mask].astype(F32) + got[mask].astype(F32)).astype(BF16)


def sum_plane_kernel(keep, *refs):
    got, outs = refs[:3], refs[3:]
    total = keep[...] + got[0][...].astype(F32) + got[1][...].astype(F32) + got[2][...].astype(F32)
    height = total.shape[0] - 16
    start = 0
    for ref in outs[:4]:
        ref[...] = total[:height, start : start + ref.shape[1]]
        start += ref.shape[1]
    start = 0
    for ref in outs[4:]:
        ref[...] = total[height : height + 1, start : start + ref.shape[1]]
        start += ref.shape[1]


def small_call(body, arrays, out_shapes, scratch=(), place=None, cost=0):
    vmem = pl.BlockSpec(memory_space=pltpu.VMEM)
    smem = [] if place is None else [place]
    return pl.pallas_call(
        body,
        in_specs=[pl.BlockSpec(memory_space=pltpu.SMEM)] * len(smem) + [vmem] * len(arrays),
        out_specs=[vmem] * len(out_shapes),
        out_shape=[jax.ShapeDtypeStruct(shape, dtype) for shape, dtype in out_shapes],
        scratch_shapes=list(scratch),
        compiler_params=pltpu.CompilerParams(vmem_limit_bytes=56 * 2**20),
        cost_estimate=pl.CostEstimate(flops=cost, bytes_accessed=0, transcendentals=0),
    )(*smem, *arrays)


def per_device_plane_of_four(
    tokens,
    positions,
    norm1_gain,
    q_weight,
    q_bias,
    key_projection,
    key_bias_vector,
    value_projection,
    value_bias_vector,
    o_weight,
    norm2_gain,
    gate_weight,
    up_weight,
    down_weight,
    cotangent,
    *,
    links,
):
    ctx_size, fsdp_size = links.ctx_size, links.fsdp_size
    ctx, row_index = lax.axis_index("ctx"), lax.axis_index("fsdp")
    chip, core = row_index // 2, row_index % 2
    place = jnp.stack([ctx, chip, core])
    count, width = tokens.shape[1:]
    shard_rows = q_weight.shape[0]
    even = core == 0
    steps = range(1, ctx_size)

    def column(x):
        return jnp.pad(x, (0, shard_rows - x.shape[0]))[:, None]

    extra = jnp.concatenate(
        [
            column(x)
            for x in (norm1_gain, q_bias, norm2_gain, key_bias_vector, value_bias_vector)
        ],
        axis=1,
    )
    extra = jnp.pad(extra, ((0, 0), (0, 128 - extra.shape[1])))
    packed = jnp.concatenate([q_weight, key_projection, value_projection, extra, o_weight], axis=1)
    links.label = "qkvo_ctx"
    packed_got = [links.turn(packed, step) for step in steps]

    mine, other = split_hidden(
        links, place, (gate_weight, up_weight, jnp.transpose(down_weight))
    )
    links.label = "ff_core"
    got = links.core(other)

    def for_ctx(step):
        target = (ctx + step) % ctx_size
        a, b = pick(mine, target), pick(got, target)
        return jnp.stack([jnp.where(even, a, b), jnp.where(even, b, a)])

    packed_got, (mine, got) = phase(packed_got, (mine, got))
    packed_mine = jnp.stack([packed] + packed_got)
    links.label = "qkvo_plane1"
    packed_stage = plane_start(links, packed_mine)
    links.label = "ff_ctx_a"
    near_steps, far_steps = (1, ctx_size - 1), tuple(range(2, ctx_size - 1))
    near = [links.turn(for_ctx(step), step) for step in near_steps]
    far = [for_ctx(step) for step in far_steps]
    links.label = "qkvo_core"
    packed_stage, near, far, (own_piece, early) = phase(
        packed_stage, near, far, (for_ctx(0), links.core(packed_mine))
    )
    links.label = "ff_ctx_b"
    far = [links.turn(piece, step) for step, piece in zip(far_steps, far)]
    links.label = "qkvo_plane2"
    packed_parts = plane_end(links, packed_mine, *packed_stage)
    links.label = "ff_own1"
    own_stage = plane_start(links, own_piece)
    near, far, late, own_stage = phase(near, far, packed_parts[3:], own_stage)
    links.label = "qkvo_core"
    pieces = [*packed_parts[:3], *late, early]
    pieces.append(links.core(jnp.concatenate([*packed_parts[1:3], *late])))
    sizes, qkv_columns = (ctx_size, fsdp_size // 2), packed.shape[1] - width
    weight_qkv = Rows(sizes, pieces, rows_layout(ctx_size), 0, qkv_columns)
    weight_o = Rows(sizes, pieces, rows_layout(ctx_size), qkv_columns, width)
    links.label = "ff_plane1"
    moved = dict(zip(near_steps + far_steps, near + far))
    moved_piece = jnp.concatenate([moved[step] for step in steps])
    moved_stage = plane_start(links, moved_piece)

    low_tokens, out_low = tokens[0], cotangent[0]
    cosine, sine = (x[:, 0] for x in angle_tables(positions[0]))
    cosine = jnp.concatenate([cosine, cosine], axis=1)
    sine = jnp.concatenate([-sine, sine], axis=1)
    place_column = positions[0][:, None]
    wide, narrow = (count, width), (count, 2 * KV_WIDTH)

    def qkv(*refs):
        qkv_body(shard_rows, *refs)

    normed_one, query, pairs, small = call(
        qkv,
        place,
        (low_tokens, cosine, sine),
        weight_qkv,
        [(wide, BF16), (wide, BF16), (narrow, BF16), ((8, width), F32)],
        0,
    )
    links.label = "kv"
    blocks = [pairs] + [links.shift(pairs, step) for step in steps]
    mixed_low, hidden_one, normed_two = call(
        mix_body,
        place,
        (low_tokens, small, place_column, query, *blocks),
        weight_o,
        [(wide, BF16), (wide, F32), (wide, BF16)],
        0,
    )

    out_row = lax.all_gather(after(out_low, *far), "ctx", axis=0, tiled=True)
    normed_row = lax.all_gather(normed_two, "ctx", axis=0, tiled=True)
    links.label = "gy_core"
    out_other = links.core(out_row)
    links.label = "ff_plane2"
    half = ctx_size - 1
    last = [
        links.plane(jnp.concatenate([moved_stage[1][:half], own_stage[1][:1]]), 2),
        links.plane(jnp.concatenate([moved_stage[0][half:], own_stage[0][1:]]), 4),
    ]
    own_entries = [(0, 0), (0, 1)]
    entries = [(step, core) for step in steps for core in range(2)]
    layout = [(own_entries, mask, x) for mask, x in enumerate((own_piece, *own_stage))]
    layout += [(entries, mask, x) for mask, x in enumerate((moved_piece, *moved_stage))]
    layout += [
        (entries[:half] + own_entries[:1], 3, last[0]),
        (entries[half:] + own_entries[1:], 3, last[1]),
    ]
    links.label = "n2_core"
    normed_other = links.core(after(normed_row, *last, out_other))
    act_a, gate_a, up_a, down_a, y_a = feed_forward(links, layout, place, normed_row, out_row)
    normed_other = after(normed_other, act_a)
    act_b, gate_b, up_b, down_b, y_b = feed_forward(links, layout, place, normed_other, out_other)
    links.label = "gn2_core"
    down_got = links.core(down_b)
    normed_rows = lax.all_gather(after(normed_one, normed_row), "ctx", axis=0, tiled=True)
    grad_normed_two = lax.psum_scatter(
        after(added(down_a, down_got), normed_rows), "ctx", scatter_dimension=0, tiled=True
    )

    rights = (gate_a, gate_b, up_a, up_b, act_a, act_b)
    lefts = (after(normed_row, down_got), normed_other, out_row, out_other)
    send_terms = ff_grad_terms(place, lefts, rights, lambda j: 2 + j, lambda j: 1 + 2 * j, (1, 2))
    links.label = "ff_sum1"
    ff_first = reduce_start(links, send_terms)
    lefts = (after(normed_row, *send_terms), *lefts[1:])
    ff_terms = ff_grad_terms(place, lefts, rights, lambda j: j, lambda j: 2 * j, (3,))
    links.label = "y_core"
    y_got = links.core(after(y_b, down_got))
    grad_normed_two = after(grad_normed_two, ff_terms[0], y_got, *ff_first[::2])

    def mix_back(*refs):
        mix_back_body(1, *refs)

    grad_hidden, grad_hidden_low, grad_query, gain_two, *pair_terms = call(
        mix_back,
        place,
        (grad_normed_two, hidden_one, small, out_low, place_column, query, cosine, sine, *blocks),
        weight_o,
        [(wide, F32), (wide, BF16), (wide, BF16), ((1, width), F32)] + [(narrow, BF16)] * ctx_size,
        BACK_COST,
    )
    links.label = "y_core"
    mixed_rows = lax.all_gather(
        after(mixed_low, grad_normed_two), "ctx", axis=0, tiled=True
    )
    links.label = "gkv"
    pair_terms = [pair_terms[0]] + [links.shift(pair_terms[step], -step) for step in steps]
    def columns_over_ctx(parts):
        whole = jnp.zeros_like(parts)
        whole = lax.dynamic_update_index_in_dim(whole, pick(parts, ctx), ctx, 0)
        for step in steps:
            piece = links.turn(pick(parts, (ctx + step) % ctx_size), step)
            whole = lax.dynamic_update_index_in_dim(whole, piece, (ctx - step) % ctx_size, 0)
        return whole

    def qkv_back(*refs):
        qkv_back_body(ctx_size, *refs)

    columns = (width + 2 * KV_WIDTH) // ctx_size
    share_shape = (count + 16, columns + width // ctx_size)
    grad_stream, *shares = call(
        qkv_back,
        place,
        (*pair_terms, low_tokens, small, cosine, sine, grad_query, grad_hidden, grad_hidden_low, gain_two),
        weight_qkv,
        [(wide, F32)] + [(share_shape, BF16)] * ctx_size,
        0,
        [pltpu.VMEM((ctx_size, *share_shape), BF16)],
    )

    links.label = "gqkv_ctx"
    first_share = shares[0]
    shares = [first_share] + [links.turn(shares[step], step) for step in steps]
    shares[0] = after(shares[0], *ff_first)
    y_both = after(added(y_a, y_got), *shares[1:])
    y_sum = lax.psum_scatter(y_both, "ctx", scatter_dimension=0, tiled=True)
    layer_out = hidden_one + y_sum.astype(F32)
    links.label = "ff_sum2"
    ff_second = reduce_next(links, ff_terms, phase(ff_first, (first_share,))[0])
    chips = fsdp_size // 2
    term_shape = (chips, width // fsdp_size + 16, share_shape[1])
    term_mine, term_other = small_call(
        term_kernel,
        (*shares, normed_rows, mixed_rows),
        [(term_shape, BF16)] * 2,
        [
            pltpu.VMEM((ctx_size * count, share_shape[1]), BF16),
            pltpu.VMEM((width, share_shape[1]), F32),
            pltpu.VMEM((fsdp_size, share_shape[1]), F32),
        ],
        place,
    )
    links.label = "term_core"
    ff_mine, ff_send = reduce_end(place, ff_terms, ff_first, ff_second)
    term_mine = after(term_mine, ff_send)
    keep, *sends = small_call(
        sum_cores_kernel,
        (term_mine, links.core(term_other)),
        [(term_shape[1:], F32)] + [(term_shape[1:], BF16)] * (chips - 1),
    )
    links.label = "term_plane"
    q_columns, kv_columns = width // ctx_size, KV_WIDTH // ctx_size
    height, devices = width // fsdp_size, ctx_size * fsdp_size
    plane_got = [links.plane(x, 2 * mask) for mask, x in enumerate(sends, 1)]
    grad_q, grad_k, grad_v, grad_o, *vectors = small_call(
        sum_plane_kernel,
        (keep, *plane_got),
        [((height, x), F32) for x in (q_columns, kv_columns, kv_columns, q_columns)]
        + [((1, x // devices), F32) for x in (width, width, width, KV_WIDTH, KV_WIDTH)],
    )
    vectors = [x[0] for x in vectors]

    links.label = "final_core"
    hidden = 2 * ff_mine.shape[2]
    grad_gate, grad_up, grad_down = small_call(
        join_cores_kernel,
        (ff_mine, after(links.core(ff_send), *sends)),
        [((height, hidden), F32), ((height, hidden), F32), ((hidden, height), F32)],
        place=place,
        cost=2*10**9,
    )

    return (
        layer_out[None],
        grad_stream[None],
        vectors[0],
        grad_q,
        vectors[2],
        grad_k,
        vectors[3],
        grad_v,
        vectors[4],
        grad_o,
        vectors[1],
        grad_gate,
        grad_up,
        grad_down,
    )


def solution(mesh):
    links = Links(mesh.shape["ctx"], mesh.shape["fsdp"])
    vector, matrix, stream = P(BOTH), P(BOTH, None), P("fsdp", "ctx", None)
    grid = P("fsdp", "ctx")
    in_specs = (
        stream,
        grid,
        vector,
        matrix,
        vector,
        matrix,
        vector,
        matrix,
        vector,
        matrix,
        vector,
        matrix,
        matrix,
        P(None, BOTH),
        stream,
    )
    out_specs = (
        stream,
        stream,
        vector,
        grid,
        vector,
        grid,
        vector,
        grid,
        vector,
        grid,
        vector,
        grid,
        grid,
        P("ctx", "fsdp"),
    )

    def run(*arrays):
        plane_of_four = mesh.shape["fsdp"] == 8 and arrays[3].shape[0] % 16 == 0
        form = per_device_plane_of_four if plane_of_four else per_device_any_mesh
        return form(*arrays, links=links)

    return jax.shard_map(run, mesh=mesh, in_specs=in_specs, out_specs=out_specs, check_vma=False)
```

```python
import jax
import jax.numpy as jnp
from jax import lax
from jax.experimental import pallas as pl
from jax.experimental.pallas import tpu as pltpu
from jax.sharding import PartitionSpec as P

QUERY_HEADS = 12
KEY_VALUE_HEADS = 2
HEAD_SIZE = 128
GROUP = QUERY_HEADS // KEY_VALUE_HEADS
KV_WIDTH = KEY_VALUE_HEADS * HEAD_SIZE
EPSILON = 1e-06
BACK_COST = 8 * 10**9
BOTH = ("ctx", "fsdp")
F32 = jnp.float32
BF16 = jnp.bfloat16


def dot(a, b, dims):
    return lax.dot_general(a, b, ((dims[:1], dims[1:]), ((), ())), preferred_element_type=F32)


def nn(a, b):
    return dot(a, b, (1, 0))


def nt(a, b):
    return dot(a, b, (1, 1))


def tn(a, b):
    return dot(a, b, (0, 0))


def rms_scale(matrix):
    return lax.rsqrt(jnp.mean(matrix * matrix, axis=-1, keepdims=True) + EPSILON)


def angle_tables(positions):
    step_index = jnp.arange(HEAD_SIZE // 2, dtype=F32) * 2.0
    frequency = 10000.0 ** (-step_index / HEAD_SIZE)
    angles = positions.astype(F32)[:, None] * frequency[None, :]
    return jnp.cos(angles)[:, None, :], jnp.sin(angles)[:, None, :]


def rotate(matrix, cosine, sine):
    rows = matrix.shape[0]
    heads = matrix.reshape(rows, -1, HEAD_SIZE)
    a, b = heads[..., : HEAD_SIZE // 2], heads[..., HEAD_SIZE // 2 :]
    turned = jnp.concatenate([a * cosine - b * sine, b * cosine + a * sine], axis=-1)
    return turned.reshape(rows, -1)


def pick(stacked, index):
    return lax.dynamic_index_in_dim(stacked, index, 0, keepdims=False)


class Links:
    def __init__(self, ctx_size, fsdp_size):
        self.ctx_size, self.fsdp_size = ctx_size, fsdp_size
        self.label = "move"
        self.planes = [m for m in (2, 4, 8, 16, 32, 64) if m < fsdp_size]

    def send(self, x, target):
        pairs = []
        for c in range(self.ctx_size):
            for f in range(self.fsdp_size):
                to = target(c, f)
                if to is not None:
                    pairs.append((c * self.fsdp_size + f, to[0] * self.fsdp_size + to[1]))
        with jax.named_scope(self.label):
            return lax.ppermute(x, BOTH, pairs)

    def core(self, x):
        return self.send(x, lambda c, f: (c, f ^ 1))

    def plane(self, x, mask):
        return self.send(x, lambda c, f: (c, f ^ mask))

    def turn(self, x, step):
        return self.send(x, lambda c, f: ((c + step) % self.ctx_size, f))

    def shift(self, x, step):
        return self.send(
            x, lambda c, f: (c + step, f) if 0 <= c + step < self.ctx_size else None
        )


def plane_gather(links, shard):
    first, second, *rest = links.planes
    half = shard.shape[0] // 2
    a = links.plane(shard, first)
    b = links.plane(shard, second)
    low = links.plane(b[:half], first)
    high = links.plane(a[half:], second)
    pieces = {0: shard, first: a, second: b, first | second: jnp.concatenate([low, high])}
    for mask in rest:
        pieces.update({had | mask: links.plane(piece, mask) for had, piece in pieces.items()})
    return pieces


def ff_weight(links, ctx, chip, core, shard):
    ctx_size = links.ctx_size
    rows, hidden = shard.shape
    block = hidden // (2 * ctx_size)
    parts = jnp.transpose(shard.reshape(rows, ctx_size, 2, block), (2, 1, 0, 3))
    mine, other = pick(parts, core), pick(parts, 1 - core)
    got = links.core(other)
    even = core == 0
    pairs = jnp.stack([jnp.where(even, mine, got), jnp.where(even, got, mine)], axis=1)
    by_source = jnp.zeros_like(pairs)
    by_source = lax.dynamic_update_index_in_dim(by_source, pick(pairs, ctx), ctx, 0)
    for step in range(1, ctx_size):
        piece = links.turn(pick(pairs, (ctx + step) % ctx_size), step)
        by_source = lax.dynamic_update_index_in_dim(by_source, piece, (ctx - step) % ctx_size, 0)
    pieces = plane_gather(links, by_source)
    whole = jnp.zeros((ctx_size, links.fsdp_size // 2, 2, rows, block), shard.dtype)
    for mask, piece in pieces.items():
        whole = lax.dynamic_update_index_in_dim(whole, piece, chip ^ (mask // 2), 1)
    return whole.reshape(-1, block)


def spread_tokens(links, x):
    row = jnp.concatenate([x] + [links.turn(x, step) for step in range(1, links.ctx_size)])
    return jnp.concatenate([row, links.core(row)])


def collect_tokens(links, partial):
    rows = partial.shape[0] // 2
    got = links.core(partial[rows:].astype(BF16))
    count = rows // links.ctx_size
    row = (partial[:rows].astype(F32) + got.astype(F32)).reshape(links.ctx_size, count, -1)
    total = row[0]
    for step in range(1, links.ctx_size):
        total = total + links.turn(row[step].astype(BF16), -step).astype(F32)
    return total


def per_device_any_mesh(
    tokens,
    positions,
    norm1_gain,
    q_weight,
    q_bias,
    key_projection,
    key_bias_vector,
    value_projection,
    value_bias_vector,
    o_weight,
    norm2_gain,
    gate_weight,
    up_weight,
    down_weight,
    cotangent,
    *,
    links,
):
    ctx_size, fsdp_size = links.ctx_size, links.fsdp_size
    ctx, row_index = lax.axis_index("ctx"), lax.axis_index("fsdp")
    chip, core = row_index // 2, row_index % 2
    count, width = tokens.shape[1:]
    scale = HEAD_SIZE ** (-0.5)
    even = core == 0

    shard_rows = q_weight.shape[0]

    def column(x):
        return jnp.pad(x, (0, shard_rows - x.shape[0]))[:, None]

    kv_bias_rows = key_bias_vector.shape[0]
    extra = jnp.concatenate(
        [
            column(x)
            for x in (norm1_gain, q_bias, norm2_gain, key_bias_vector, value_bias_vector)
        ],
        axis=1,
    )
    extra = jnp.pad(extra, ((0, 0), (0, 128 - extra.shape[1])))
    packed = jnp.concatenate([q_weight, key_projection, value_projection, extra], axis=1)
    packed = lax.all_gather(packed, BOTH, axis=0, tiled=True)
    weight_o = lax.all_gather(o_weight, BOTH, axis=0, tiled=True)

    weight_gate = ff_weight(links, ctx, chip, core, gate_weight)
    weight_up = ff_weight(links, ctx, chip, core, up_weight)
    weight_down = ff_weight(links, ctx, chip, core, jnp.transpose(down_weight))

    qkv_width = width + 2 * KV_WIDTH
    weight_qkv = packed[:, :qkv_width]
    small = jnp.transpose(packed[:, qkv_width:])[:5].astype(F32)
    gain_one, bias_q, gain_two = small[0:1], small[1:2], small[2:3]

    def bias_of(row):
        return row.reshape(-1, shard_rows)[:, :kv_bias_rows].reshape(1, -1)

    bias_k, bias_v = bias_of(small[3]), bias_of(small[4])
    out_low = cotangent[0]
    group_out = spread_tokens(links, out_low)

    stream = tokens[0].astype(F32)
    scale_one = rms_scale(stream)
    unit_one = stream * scale_one
    normed_one = (unit_one * gain_one).astype(BF16)
    cosine, sine = angle_tables(positions[0])
    linear = nn(normed_one, weight_qkv)
    query = rotate(linear[:, :width] + bias_q, cosine, sine).astype(BF16)
    key = rotate(linear[:, width : width + KV_WIDTH] + bias_k, cosine, sine).astype(BF16)
    value = (linear[:, width + KV_WIDTH :] + bias_v).astype(BF16)
    pairs = jnp.concatenate([key, value], axis=1)
    row_pairs = jnp.concatenate(
        [pairs] + [links.shift(pairs, step) for step in range(1, ctx_size)]
    )
    keys = row_pairs[:, :KV_WIDTH].reshape(-1, KEY_VALUE_HEADS, HEAD_SIZE)
    values = row_pairs[:, KV_WIDTH:].reshape(-1, KEY_VALUE_HEADS, HEAD_SIZE)
    local_index = jnp.arange(count)
    key_index = jnp.concatenate(
        [(ctx - step) * count + local_index for step in range(ctx_size)]
    )
    query_index = ctx * count + local_index
    doc_start = query_index - positions[0]
    allowed = (key_index[None, :] >= doc_start[:, None]) & (
        key_index[None, :] <= query_index[:, None]
    )
    query_heads = query.reshape(count, KEY_VALUE_HEADS, GROUP, HEAD_SIZE)
    scores = jnp.einsum("qkgd,rkd->kgqr", query_heads, keys, preferred_element_type=F32) * scale
    scores = jnp.where(allowed, scores, -1e30)
    top = jnp.max(scores, axis=-1, keepdims=True)
    weights = jnp.where(allowed, jnp.exp(scores - top), 0.0)
    probs = weights / jnp.sum(weights, axis=-1, keepdims=True)
    probs_low = probs.astype(BF16)
    mixed = jnp.einsum("kgqr,rkd->qkgd", probs_low, values, preferred_element_type=F32)
    mixed_low = mixed.reshape(count, -1).astype(BF16)
    hidden_one = stream + nn(mixed_low, weight_o)

    scale_two = rms_scale(hidden_one)
    unit_two = hidden_one * scale_two
    normed_two = (unit_two * gain_two).astype(BF16)
    group_normed = spread_tokens(links, normed_two)
    gate_pre = nn(group_normed, weight_gate)
    up_pre = nn(group_normed, weight_up)
    grad_act = nn(group_out, weight_down)
    sigmoid_gate = jax.nn.sigmoid(gate_pre)
    activated = (gate_pre * sigmoid_gate * up_pre).astype(BF16)
    grad_gate_low = (
        grad_act * up_pre * sigmoid_gate * (1.0 + gate_pre * (1.0 - sigmoid_gate))
    ).astype(BF16)
    grad_up_low = (grad_act * gate_pre * sigmoid_gate).astype(BF16)
    grad_normed_two = collect_tokens(
        links, nt(grad_gate_low, weight_gate) + nt(grad_up_low, weight_up)
    )
    layer_out = hidden_one + collect_tokens(links, nt(activated, weight_down))

    planes = [
        [c * fsdp_size + 2 * p + k for p in range(fsdp_size // 2)]
        for c in range(ctx_size)
        for k in range(2)
    ]

    def ff_grad(left, right):
        term = tn(left, right).astype(BF16)
        part = lax.psum_scatter(
            term, BOTH, scatter_dimension=0, tiled=True, axis_index_groups=planes
        )
        part = part.reshape(2, -1, part.shape[1])
        mine, got = pick(part, core), links.core(pick(part, 1 - core))
        return jnp.concatenate(
            [jnp.where(even, mine, got), jnp.where(even, got, mine)], axis=1
        ).astype(F32)

    grad_gate = ff_grad(group_normed, grad_gate_low)
    grad_up = ff_grad(group_normed, grad_up_low)
    grad_down = jnp.transpose(ff_grad(group_out, activated))

    grad_gain_two = jnp.sum(grad_normed_two * unit_two, axis=0)
    weighted_two = grad_normed_two * gain_two
    grad_hidden = out_low.astype(F32) + scale_two * (
        weighted_two - unit_two * jnp.mean(weighted_two * unit_two, axis=-1, keepdims=True)
    )

    grad_hidden_low = grad_hidden.astype(BF16)
    grad_mixed = nt(grad_hidden_low, weight_o).astype(BF16)
    grad_mixed = grad_mixed.reshape(count, KEY_VALUE_HEADS, GROUP, HEAD_SIZE)
    grad_probs = jnp.einsum("qkgd,rkd->kgqr", grad_mixed, values, preferred_element_type=F32)
    delta = jnp.sum(probs * grad_probs, axis=-1, keepdims=True)
    grad_scores = (probs * (grad_probs - delta)).astype(BF16)
    grad_query = jnp.einsum("kgqr,rkd->qkgd", grad_scores, keys, preferred_element_type=F32)
    grad_key = (
        jnp.einsum("kgqr,qkgd->rkd", grad_scores, query_heads, preferred_element_type=F32) * scale
    )
    grad_value = jnp.einsum("kgqr,qkgd->rkd", probs_low, grad_mixed, preferred_element_type=F32)
    pair_terms = jnp.concatenate(
        [grad_key.reshape(-1, KV_WIDTH), grad_value.reshape(-1, KV_WIDTH)], axis=1
    ).reshape(ctx_size, count, -1)
    pair_grads = pair_terms[0]
    for step in range(1, ctx_size):
        pair_grads = pair_grads + links.shift(pair_terms[step].astype(BF16), -step).astype(F32)
    grad_q_low = rotate(grad_query.reshape(count, -1) * scale, cosine, -sine).astype(BF16)
    grad_k_low = rotate(pair_grads[:, :KV_WIDTH], cosine, -sine).astype(BF16)
    grad_v_low = pair_grads[:, KV_WIDTH:].astype(BF16)
    grad_qkv = jnp.concatenate([grad_q_low, grad_k_low, grad_v_low], axis=1)
    grad_normed_one = nt(grad_qkv, weight_qkv)
    grad_gain_one = jnp.sum(grad_normed_one * unit_one, axis=0)
    weighted_one = grad_normed_one * gain_one
    grad_stream = grad_hidden + scale_one * (
        weighted_one - unit_one * jnp.mean(weighted_one * unit_one, axis=-1, keepdims=True)
    )

    def columns_over_ctx(arrays):
        parts = jnp.concatenate([x.reshape(count, ctx_size, -1) for x in arrays], axis=2)
        parts = jnp.transpose(parts, (1, 0, 2))
        whole = jnp.zeros_like(parts)
        whole = lax.dynamic_update_index_in_dim(whole, pick(parts, ctx), ctx, 0)
        for step in range(1, ctx_size):
            piece = links.turn(pick(parts, (ctx + step) % ctx_size), step)
            whole = lax.dynamic_update_index_in_dim(whole, piece, (ctx - step) % ctx_size, 0)
        return whole.reshape(ctx_size * count, -1)

    def attention_grad(rows, arrays):
        left = lax.all_gather(rows, "ctx", axis=0, tiled=True)
        term = tn(left, columns_over_ctx(arrays)).astype(BF16)
        return lax.psum_scatter(term, "fsdp", scatter_dimension=0, tiled=True).astype(F32)

    grad_o = attention_grad(mixed_low, [grad_hidden_low])
    grad_packed = attention_grad(normed_one, [grad_q_low, grad_k_low, grad_v_low])
    q_columns, kv_columns = width // ctx_size, KV_WIDTH // ctx_size

    sums = jnp.concatenate(
        [grad_gain_one, grad_gain_two, jnp.sum(grad_qkv.astype(F32), axis=0)]
    )
    sums = lax.psum(sums, BOTH)
    device = ctx * fsdp_size + row_index

    def own(start, size):
        part = size // (ctx_size * fsdp_size)
        return lax.dynamic_slice_in_dim(sums, start + device * part, part)

    return (
        layer_out[None],
        grad_stream[None],
        own(0, width),
        grad_packed[:, :q_columns],
        own(2 * width, width),
        grad_packed[:, q_columns : q_columns + kv_columns],
        own(3 * width, KV_WIDTH),
        grad_packed[:, q_columns + kv_columns :],
        own(3 * width + KV_WIDTH, KV_WIDTH),
        grad_o,
        own(width, width),
        grad_gate,
        grad_up,
        grad_down,
    )


def after(x, *others):
    return lax.optimization_barrier((x, *others))[0]


def phase(*groups):
    flat = lax.optimization_barrier(tuple(x for group in groups for x in group))
    out = []
    for group in groups:
        out.append(list(flat[: len(group)]))
        flat = flat[len(group) :]
    return out


def plane_start(links, shard):
    return links.plane(shard, 2), links.plane(shard, 4)


def plane_end(links, shard, a, b):
    half = shard.shape[0] // 2
    return shard, a, b, links.plane(b[:half], 2), links.plane(a[half:], 4)


def load_pieces(layout, sizes, place, pieces, which, weight, semaphore):
    ctx_size, chips, rows = sizes
    for (entries, mask, _), piece in zip(layout, pieces):
        for i, (step, core) in enumerate(entries):
            source = lax.rem(place[0] - step + ctx_size, ctx_size)
            start = ((source * chips + (place[1] ^ mask)) * 2 + core) * rows
            pltpu.make_async_copy(
                piece.at[i, which],
                weight.at[pl.ds(pl.multiple_of(start, rows), rows)],
                semaphore,
            ).start()


def ff_kernel(layout, sizes, place, normed, out_grad, *refs):
    pieces, refs = refs[: len(layout)], refs[len(layout) :]
    act_ref, gate_ref, up_ref, down_ref, weights, semaphores = refs

    @pl.when(pl.program_id(0) == 0)
    def _():
        for which in range(3):
            load_pieces(
                layout, sizes, place, pieces, which, weights.at[which], semaphores.at[which]
            )

    def arrived(which):
        @pl.when(pl.program_id(0) == 0)
        def _():
            wait_all(weights.at[which], semaphores.at[which])

    x, gy = normed[...], out_grad[...]
    arrived(0)
    gate = nn(x, weights[0])
    arrived(1)
    up = nn(x, weights[1])
    arrived(2)
    grad = nn(gy, weights[2])
    sigmoid = 1.0 / (1.0 + jnp.exp(-gate))
    silu = gate * sigmoid
    grad_gate = (grad * up * sigmoid * (1.0 + gate * (1.0 - sigmoid))).astype(BF16)
    grad_up = (grad * silu).astype(BF16)
    act_ref[...] = (silu * up).astype(BF16)
    gate_ref[...] = grad_gate
    up_ref[...] = grad_up
    down_ref[...] = (nt(grad_gate, weights[0]) + nt(grad_up, weights[1])).astype(BF16)


def y_kernel(layout, sizes, place, act_a, act_b, *refs):
    pieces, (y_a, y_b, weight, semaphore) = refs[: len(layout)], refs[len(layout) :]

    @pl.when(pl.program_id(0) == 0)
    def _():
        load_pieces(layout, sizes, place, pieces, 2, weight, semaphore)
        wait_all(weight, semaphore)

    y_a[...] = nt(act_a[...], weight[...]).astype(BF16)
    y_b[...] = nt(act_b[...], weight[...]).astype(BF16)


def ff_call(links, kernel, layout, place, arrays, widths, matrices):
    tokens = arrays[0].shape[0]
    rows, block = layout[0][2].shape[2:]
    sizes = (links.ctx_size, links.fsdp_size // 2, rows)
    depth = 2 * sizes[0] * sizes[1] * rows
    tile = 256

    def spec(size):
        return pl.BlockSpec((tile, size), lambda i, place: (i, 0))

    def body(*refs):
        kernel(layout, sizes, *refs)

    if matrices == 1:
        scratch = [pltpu.VMEM((depth, block), BF16), pltpu.SemaphoreType.DMA]
    else:
        scratch = [
            pltpu.VMEM((matrices, depth, block), BF16),
            pltpu.SemaphoreType.DMA((matrices,)),
        ]
    return pl.pallas_call(
        body,
        grid_spec=pltpu.PrefetchScalarGridSpec(
            num_scalar_prefetch=1,
            grid=(tokens // tile,),
            in_specs=[spec(x.shape[1]) for x in arrays]
            + [pl.BlockSpec(memory_space=pl.ANY)] * len(layout),
            out_specs=[spec(x) for x in widths],
            scratch_shapes=scratch,
        ),
        out_shape=[jax.ShapeDtypeStruct((tokens, x), BF16) for x in widths],
        compiler_params=pltpu.CompilerParams(vmem_limit_bytes=56 * 2**20),
        cost_estimate=pl.CostEstimate(flops=0, bytes_accessed=0, transcendentals=0),
    )(place, *arrays, *[piece for _, _, piece in layout])


def grad_kernel(place, *refs):
    lefts, rights, outs = refs[:8], refs[8:14], refs[14:]
    low, high = outs[: len(outs) // 2], outs[len(outs) // 2 :]
    for which in range(3):
        first = 4 * (which // 2)
        for parts, (left_a, left_b), core in (
            (low, lefts[first : first + 2], 0),
            (high, lefts[first + 2 : first + 4], 1),
        ):
            out, at = (parts[0], which) if len(parts) == 1 else (parts[which > 0], max(which - 1, 0))
            half = left_a.shape[1] // 2
            rows = slice(core * half, (core + 1) * half)
            right_a, right_b = rights[2 * which : 2 * which + 2]
            term = tn(left_a[:, rows], right_a[...]) + tn(left_b[:, rows], right_b[...])
            out[0, at] = term.astype(BF16)


def ff_grad_terms(place, lefts, rights, low_at, high_at, parts):
    tokens, width = lefts[0].shape
    block = rights[0].shape[1]
    part = width // 4

    def left(at):
        return pl.BlockSpec((tokens, part), lambda j, place: (0, place[1] ^ at(j)))

    right = pl.BlockSpec((tokens, block), lambda j, place: (0, 0))
    outs = [pl.BlockSpec((1, n, part // 2, block), lambda j, place: (j, 0, 0, 0)) for n in parts]
    low, high = left(low_at), left(high_at)
    x_a, x_b, y_a, y_b = lefts
    return pl.pallas_call(
        grad_kernel,
        grid_spec=pltpu.PrefetchScalarGridSpec(
            num_scalar_prefetch=1,
            grid=(2,),
            in_specs=[low, low, high, high] * 2 + [right] * 6,
            out_specs=outs * 2,
        ),
        out_shape=[jax.ShapeDtypeStruct((2, n, part // 2, block), BF16) for n in parts] * 2,
        compiler_params=pltpu.CompilerParams(vmem_limit_bytes=56 * 2**20),
        cost_estimate=pl.CostEstimate(flops=0, bytes_accessed=0, transcendentals=0),
    )(place, x_a, x_b, x_a, x_b, y_a, y_b, y_a, y_b, *rights)


def added(a, b):
    return (a.astype(F32) + b.astype(F32)).astype(BF16)


def reduce_start(links, terms):
    return [links.plane(x, mask) for x, mask in zip(terms, (4, 4, 2, 2))]


def add_pairs_kernel(*refs):
    for i, out in enumerate(refs[6:]):
        keep, one, rest = refs[3 * i : 3 * i + 3]
        out[:1] = (keep[0, :1].astype(F32) + one[0].astype(F32)).astype(BF16)
        out[1:] = (keep[0, 1:].astype(F32) + rest[0].astype(F32)).astype(BF16)


def first_specs(index):
    def spec(x):
        return pl.BlockSpec((1, *x.shape[1:]), lambda i, *place: (index, 0, 0, 0))

    return spec


def reduce_next(links, terms, first):
    shape = terms[0].shape
    arrays = (terms[0], first[0], first[1], terms[1], first[2], first[3])
    spec = first_specs(1)
    whole = pl.BlockSpec(shape[1:], lambda i: (0, 0, 0))
    low, high = pl.pallas_call(
        add_pairs_kernel,
        grid=(1,),
        in_specs=[spec(x) for x in arrays],
        out_specs=[whole] * 2,
        out_shape=[jax.ShapeDtypeStruct(shape[1:], BF16)] * 2,
        compiler_params=pltpu.CompilerParams(vmem_limit_bytes=56 * 2**20),
        cost_estimate=pl.CostEstimate(flops=0, bytes_accessed=0, transcendentals=0),
    )(*arrays)
    return links.plane(low, 2), links.plane(high, 4)


def reduce_end_kernel(place, *refs):
    low, high, (mine, send) = refs[:4], refs[4:8], refs[8:]

    def write(ref, parts):
        keep, one, rest, last = parts
        total = keep[0, :1].astype(F32) + one[0].astype(F32) + last[:1].astype(F32)
        ref[:1] = total.astype(ref.dtype)
        total = keep[0, 1:].astype(F32) + rest[0].astype(F32) + last[1:].astype(F32)
        ref[1:] = total.astype(ref.dtype)

    @pl.when(place[2] == 0)
    def _():
        write(mine, low)
        write(send, high)

    @pl.when(place[2] != 0)
    def _():
        write(mine, high)
        write(send, low)


def reduce_end(place, terms, first, second):
    shape = terms[0].shape[1:]
    spec = first_specs(0)
    whole = pl.BlockSpec(shape, lambda i, place: (0, 0, 0))
    low = (terms[0], first[0], first[1])
    high = (terms[1], first[2], first[3])
    return pl.pallas_call(
        reduce_end_kernel,
        grid_spec=pltpu.PrefetchScalarGridSpec(
            num_scalar_prefetch=1,
            grid=(1,),
            in_specs=[*map(spec, low), whole, *map(spec, high), whole],
            out_specs=[whole] * 2,
        ),
        out_shape=[jax.ShapeDtypeStruct(shape, F32), jax.ShapeDtypeStruct(shape, BF16)],
        compiler_params=pltpu.CompilerParams(vmem_limit_bytes=56 * 2**20),
        cost_estimate=pl.CostEstimate(flops=12*10**9, bytes_accessed=0, transcendentals=0),
    )(place, *low, second[0], *high, second[1])


def join_cores_kernel(place, mine, got, gate, up, down):
    def write(even, odd):
        for which, ref in enumerate((gate, up, down)):
            ref[...] = jnp.concatenate([even(which), odd(which)], axis=1)

    def own(which):
        return mine[which]

    def others(which):
        return got[which].astype(F32)

    @pl.when(place[2] == 0)
    def _():
        write(own, others)

    @pl.when(place[2] != 0)
    def _():
        write(others, own)


def split_kernel(place, gate, up, down, mine, other):
    block = mine.shape[3]

    def write(core):
        for which, ref in enumerate((gate, up, down)):
            for target in range(mine.shape[0]):
                start = (2 * target + core) * block
                mine[target, which] = ref[:, start : start + block]
                start = (2 * target + 1 - core) * block
                other[target, which] = ref[:, start : start + block]

    @pl.when(place[2] == 0)
    def _():
        write(0)

    @pl.when(place[2] != 0)
    def _():
        write(1)


def split_hidden(links, place, shards):
    rows, hidden = shards[0].shape
    whole = pl.BlockSpec((rows, hidden), lambda i, place: (0, 0))
    shape = (links.ctx_size, 3, rows, hidden // (2 * links.ctx_size))
    out = pl.BlockSpec(shape, lambda i, place: (0, 0, 0, 0))
    return pl.pallas_call(
        split_kernel,
        grid_spec=pltpu.PrefetchScalarGridSpec(
            num_scalar_prefetch=1, grid=(1,), in_specs=[whole] * 3, out_specs=[out] * 2
        ),
        out_shape=[jax.ShapeDtypeStruct(shape, BF16)] * 2,
        compiler_params=pltpu.CompilerParams(vmem_limit_bytes=32 * 2**20),
    )(place, *shards)


class Rows:
    def __init__(self, sizes, pieces, layout, first, columns):
        self.sizes, self.pieces, self.layout = sizes, pieces, layout
        self.first, self.columns = first, columns
        self.rows = pieces[0].shape[-2]
        self.shape = (2 * sizes[0] * sizes[1] * self.rows, columns)

    def start(self, place, refs, weight, semaphore):
        ctx_size, chips = self.sizes
        for piece, index, step, mask, turned in self.layout:
            source = lax.rem(place[0] - step + ctx_size, ctx_size)
            start = ((source * chips + (place[1] ^ mask)) * 2 + (place[2] ^ turned)) * self.rows
            pltpu.make_async_copy(
                refs[piece].at[(*index, slice(None), pl.ds(self.first, self.columns))],
                weight.at[pl.ds(pl.multiple_of(start, self.rows), self.rows)],
                semaphore,
            ).start()


def rows_layout(ctx_size):
    half = ctx_size // 2
    layout = []
    for step in range(ctx_size):
        layout += [(mask, (step,), step, mask, 0) for mask in range(3)]
        layout.append((3, (step,), step, 3, 0) if step < half else (4, (step - half,), step, 3, 0))
        layout.append((5, (step,), step, 0, 1))
        layout += [(6, (i * ctx_size + step,), step, i + 1, 1) for i in range(3)]
    return layout


def wait_all(weight, semaphore):
    pltpu.make_async_copy(weight, weight, semaphore).wait()


def call(body, place, arrays, weight, out_shapes, cost, scratch=()):
    any_spec = pl.BlockSpec(memory_space=pl.ANY)
    vmem = pl.BlockSpec(memory_space=pltpu.VMEM)
    count, pieces = len(arrays), len(weight.pieces)

    def kernel(place, *refs):
        ins, parts, outs = refs[:count], refs[count : count + pieces], refs[count + pieces : -2]
        whole, semaphore = refs[-2:]
        weight.start(place, parts, whole, semaphore)
        body(place, ins, outs, whole, lambda: wait_all(whole, semaphore))

    return pl.pallas_call(
        kernel,
        in_specs=[pl.BlockSpec(memory_space=pltpu.SMEM)] + [vmem] * count + [any_spec] * pieces,
        out_specs=[vmem] * len(out_shapes),
        out_shape=[jax.ShapeDtypeStruct(shape, dtype) for shape, dtype in out_shapes],
        scratch_shapes=[*scratch, pltpu.VMEM(weight.shape, BF16), pltpu.SemaphoreType.DMA],
        compiler_params=pltpu.CompilerParams(vmem_limit_bytes=56 * 2**20),
        cost_estimate=pl.CostEstimate(flops=cost, bytes_accessed=0, transcendentals=0),
    )(place, *arrays, *weight.pieces)


def turn_halves(x, cosine, sine):
    return x * cosine + pltpu.roll(x, HEAD_SIZE // 2, 1) * sine


def turned_heads(x, cosine, sine):
    heads = [x[:, i : i + HEAD_SIZE] for i in range(0, x.shape[1], HEAD_SIZE)]
    return jnp.concatenate([turn_halves(x, cosine, sine) for x in heads], axis=1)


def qkv_body(shard_rows, place, ins, outs, weight, wait):
    tokens, cosine, sine = ins
    normed_ref, query_ref, pairs_ref, small_ref = outs
    width = tokens.shape[1]
    qkv_width = width + 2 * KV_WIDTH
    x = tokens[...].astype(F32)
    unit = x * rms_scale(x)
    wait()
    small = jnp.transpose(weight[:, qkv_width:].astype(F32))[:8]
    bias_rows = KV_WIDTH * shard_rows // width
    row = lax.broadcasted_iota(jnp.int32, (width, KV_WIDTH), 0)
    at = lax.broadcasted_iota(jnp.int32, (width, KV_WIDTH), 1)
    chosen = row == (at // bias_rows) * shard_rows + at % bias_rows
    kv_bias = nn(small.astype(BF16), chosen.astype(BF16))
    normed = (unit * small[0:1]).astype(BF16)
    normed_ref[...] = normed
    small_ref[...] = small
    linear = nn(normed, weight[:, :qkv_width])
    query = linear[:, :width] + small[1:2]
    key = linear[:, width : width + KV_WIDTH] + kv_bias[3:4]
    query_ref[...] = turned_heads(query, cosine[...], sine[...]).astype(BF16)
    pairs_ref[:, :KV_WIDTH] = turned_heads(key, cosine[...], sine[...]).astype(BF16)
    pairs_ref[:, KV_WIDTH:] = (linear[:, width + KV_WIDTH :] + kv_bias[4:5]).astype(BF16)


def allowed_keys(ctx, positions, blocks):
    count = positions.shape[0]
    shape = (count, blocks * count)
    column = lax.broadcasted_iota(jnp.int32, shape, 1)
    query = ctx * count + lax.broadcasted_iota(jnp.int32, shape, 0)
    key = (ctx - column // count) * count + column % count
    return (key >= query - positions) & (key <= query)


def heads_of(x, group):
    first = group * GROUP
    return jnp.concatenate(
        [x[:, i * HEAD_SIZE : (i + 1) * HEAD_SIZE] for i in range(first, first + GROUP)], axis=0
    )


def softmax_of(query, keys, allowed):
    scores = nt(query, keys) * HEAD_SIZE ** (-0.5)
    scores = jnp.where(allowed, scores, -1e30)
    weights = jnp.exp(scores - jnp.max(scores, axis=-1, keepdims=True))
    weights = jnp.where(allowed, weights, 0.0)
    return weights / jnp.sum(weights, axis=-1, keepdims=True)


def group_pairs(blocks, group):
    def columns(start):
        return jnp.concatenate([b[:, start : start + HEAD_SIZE] for b in blocks], axis=0)

    return columns(group * HEAD_SIZE), columns(KV_WIDTH + group * HEAD_SIZE)


def mix_body(place, ins, outs, weight, wait):
    tokens, small, positions, query, *blocks = ins
    mixed_ref, hidden_ref, normed_ref = outs
    count = tokens.shape[0]
    allowed = allowed_keys(place[0], positions[...], len(blocks))
    allowed = jnp.concatenate([allowed.astype(F32)] * GROUP, axis=0) > 0
    for group in range(KEY_VALUE_HEADS):
        keys, values = group_pairs(blocks, group)
        probs = softmax_of(heads_of(query, group), keys, allowed)
        mixed = nn(probs.astype(BF16), values).astype(BF16)
        for h in range(GROUP):
            start = (group * GROUP + h) * HEAD_SIZE
            mixed_ref[:, start : start + HEAD_SIZE] = mixed[h * count : (h + 1) * count]
    wait()
    hidden = tokens[...].astype(F32) + nn(mixed_ref[...], weight[...])
    hidden_ref[...] = hidden
    normed_ref[...] = (hidden * rms_scale(hidden) * small[2:3]).astype(BF16)


def norm_back(unit, scale, grad, gain):
    weighted = grad * gain
    return scale * (weighted - unit * jnp.mean(weighted * unit, axis=-1, keepdims=True))


def mix_back_body(steps, place, ins, outs, weight, wait):
    terms, ins = ins[:steps], ins[steps:]
    hidden_ref, small, out_grad, positions, query, cosine, sine, *blocks = ins
    grad_hidden_ref, low_ref, grad_query_ref, gain_ref, *pair_refs = outs
    count = hidden_ref.shape[0]
    hidden = hidden_ref[...]
    scale = rms_scale(hidden)
    unit = hidden * scale
    grad = terms[0][...].astype(F32)
    for term in terms[1:]:
        grad = grad + term[...].astype(F32)
    gain_ref[...] = jnp.sum(grad * unit, axis=0, keepdims=True)
    grad_hidden = out_grad[...].astype(F32) + norm_back(unit, scale, grad, small[2:3])
    grad_hidden_ref[...] = grad_hidden
    low = grad_hidden.astype(BF16)
    low_ref[...] = low
    wait()
    grad_mixed = nt(low, weight[...]).astype(BF16)
    allowed = allowed_keys(place[0], positions[...], len(blocks))
    allowed = jnp.concatenate([allowed.astype(F32)] * GROUP, axis=0) > 0
    score_scale = HEAD_SIZE ** (-0.5)
    for group in range(KEY_VALUE_HEADS):
        keys, values = group_pairs(blocks, group)
        queries, grads = heads_of(query, group), heads_of(grad_mixed, group)
        probs = softmax_of(queries, keys, allowed)
        grad_probs = nt(grads, values)
        delta = jnp.sum(probs * grad_probs, axis=-1, keepdims=True)
        grad_scores = (probs * (grad_probs - delta)).astype(BF16)
        grad_query = nn(grad_scores, keys) * score_scale
        for h in range(GROUP):
            start = (group * GROUP + h) * HEAD_SIZE
            grad_query_ref[:, start : start + HEAD_SIZE] = turn_halves(
                grad_query[h * count : (h + 1) * count], cosine[...], -sine[...]
            ).astype(BF16)
        grad_key = (tn(grad_scores, queries) * score_scale).astype(BF16)
        grad_value = tn(probs.astype(BF16), grads).astype(BF16)
        start = group * HEAD_SIZE
        for block, ref in enumerate(pair_refs):
            rows = slice(block * count, (block + 1) * count)
            ref[:, start : start + HEAD_SIZE] = grad_key[rows]
            ref[:, KV_WIDTH + start : KV_WIDTH + start + HEAD_SIZE] = grad_value[rows]


def qkv_back_body(steps, place, ins, outs, weight, wait):
    terms, ins = ins[:steps], ins[steps:]
    tokens, small, cosine, sine, grad_query, grad_hidden, grad_hidden_low, gain_two = ins
    stream_ref, *share_refs, share_ref = outs
    count, width = tokens.shape
    pairs = terms[0][...].astype(F32)
    for term in terms[1:]:
        pairs = pairs + term[...].astype(F32)
    grad_key = turned_heads(pairs[:, :KV_WIDTH], cosine[...], -sine[...]).astype(BF16)
    grad_value = pairs[:, KV_WIDTH:].astype(BF16)
    wait()
    kv_end = width + KV_WIDTH
    grad = (
        nt(grad_query[...], weight[:, :width])
        + nt(grad_key, weight[:, width:kv_end])
        + nt(grad_value, weight[:, kv_end : kv_end + KV_WIDTH])
    )
    x = tokens[...].astype(F32)
    scale = rms_scale(x)
    unit = x * scale
    stream_ref[...] = grad_hidden[...] + norm_back(unit, scale, grad, small[0:1])
    gains = jnp.concatenate([jnp.sum(grad * unit, axis=0, keepdims=True), gain_two[...]], axis=0)
    gains = jnp.concatenate([gains, jnp.zeros((14, width), F32)], axis=0).astype(BF16)
    targets = share_ref.shape[0]
    q_columns, kv_columns = width // targets, KV_WIDTH // targets
    for target in range(targets):
        q, kv = target * q_columns, target * kv_columns
        share_ref[target, :count, :q_columns] = grad_query[:, q : q + q_columns]
        kv_end = q_columns + 2 * kv_columns
        share_ref[target, :count, q_columns:kv_end] = jnp.concatenate(
            [grad_key[:, kv : kv + kv_columns], grad_value[:, kv : kv + kv_columns]], axis=1
        )
        share_ref[target, :count, kv_end:] = grad_hidden_low[:, q : q + q_columns]
        share_ref[target, count:, :q_columns] = gains[:, q : q + q_columns]
        share_ref[target, count:, q_columns:] = jnp.zeros(
            (16, share_ref.shape[2] - q_columns), BF16
        )
    for step, ref in enumerate(share_refs):
        ref[...] = share_ref[lax.rem(place[0] + step, targets)]


def term_kernel(place, *refs):
    *shares, normed_rows, mixed_rows, mine, other, share, terms, vectors = refs
    ctx_size, width = len(shares), normed_rows.shape[1]
    count = normed_rows.shape[0] // ctx_size
    chips, height = mine.shape[0], mine.shape[1] - 16
    devices = 2 * chips
    q_columns, kv_columns = width // ctx_size, KV_WIDTH // ctx_size
    kv_end = q_columns + 2 * kv_columns
    gains = jnp.zeros((16, q_columns), F32)
    for step, ref in enumerate(shares):
        source = lax.rem(place[0] - step + ctx_size, ctx_size)
        share[pl.ds(pl.multiple_of(source * count, count), count)] = ref[:count]
        gains = gains + ref[count:, :q_columns].astype(F32)
    terms[:, :kv_end] = tn(normed_rows[...], share[:, :kv_end])
    terms[:, kv_end:] = tn(mixed_rows[...], share[:, kv_end:])
    biases = jnp.sum(share[:, :kv_end].astype(F32), axis=0, keepdims=True)
    vectors[...] = jnp.zeros_like(vectors)
    parts = (gains[0:1], gains[1:2], biases[:, :q_columns])
    parts += (biases[:, q_columns : q_columns + kv_columns], biases[:, q_columns + kv_columns :])
    for f in range(devices):
        start = 0
        for part in parts:
            size = part.shape[1] // devices
            vectors[f : f + 1, start : start + size] = part[:, f * size : (f + 1) * size]
            start += size
    first = lax.broadcasted_iota(jnp.int32, (16, terms.shape[1]), 0) == 0
    for ref, core in ((mine, place[2]), (other, 1 - place[2])):
        for mask in range(chips):
            f = (place[1] ^ mask) * 2 + core
            start = pl.multiple_of(f * height, 64)
            ref[mask, :height] = terms[pl.ds(start, height)].astype(BF16)
            row = jnp.broadcast_to(vectors[pl.ds(f, 1)], first.shape)
            ref[mask, height:] = jnp.where(first, row, 0.0).astype(BF16)


def sum_cores_kernel(mine, got, keep, *sends):
    keep[...] = mine[0].astype(F32) + got[0].astype(F32)
    for mask, ref in enumerate(sends, 1):
        ref[...] = (mine[mask].astype(F32) + got[mask].astype(F32)).astype(BF16)


def sum_plane_kernel(keep, *refs):
    got, outs = refs[:3], refs[3:]
    total = keep[...] + got[0][...].astype(F32) + got[1][...].astype(F32) + got[2][...].astype(F32)
    height = total.shape[0] - 16
    start = 0
    for ref, turned in zip(outs[:4], (False, True, True, False)):
        size = ref.shape[0] if turned else ref.shape[1]
        part = total[:height, start : start + size]
        ref[...] = jnp.transpose(part) if turned else part
        start += size
    start = 0
    for ref in outs[4:]:
        ref[...] = total[height : height + 1, start : start + ref.shape[1]]
        start += ref.shape[1]


def small_call(body, arrays, out_shapes, scratch=(), place=None, cost=0):
    vmem = pl.BlockSpec(memory_space=pltpu.VMEM)
    smem = [] if place is None else [place]
    return pl.pallas_call(
        body,
        in_specs=[pl.BlockSpec(memory_space=pltpu.SMEM)] * len(smem) + [vmem] * len(arrays),
        out_specs=[vmem] * len(out_shapes),
        out_shape=[jax.ShapeDtypeStruct(shape, dtype) for shape, dtype in out_shapes],
        scratch_shapes=list(scratch),
        compiler_params=pltpu.CompilerParams(vmem_limit_bytes=56 * 2**20),
        cost_estimate=pl.CostEstimate(flops=cost, bytes_accessed=0, transcendentals=0),
    )(*smem, *arrays)


def per_device_plane_of_four(
    tokens,
    positions,
    norm1_gain,
    q_weight,
    q_bias,
    key_projection,
    key_bias_vector,
    value_projection,
    value_bias_vector,
    o_weight,
    norm2_gain,
    gate_weight,
    up_weight,
    down_weight,
    cotangent,
    *,
    links,
):
    ctx_size, fsdp_size = links.ctx_size, links.fsdp_size
    ctx, row_index = lax.axis_index("ctx"), lax.axis_index("fsdp")
    chip, core = row_index // 2, row_index % 2
    place = jnp.stack([ctx, chip, core])
    count, width = tokens.shape[1:]
    shard_rows = q_weight.shape[0]
    even = core == 0
    steps = range(1, ctx_size)

    def column(x):
        return jnp.pad(x, (0, shard_rows - x.shape[0]))[:, None]

    extra = jnp.concatenate(
        [
            column(x)
            for x in (norm1_gain, q_bias, norm2_gain, key_bias_vector, value_bias_vector)
        ],
        axis=1,
    )
    extra = jnp.pad(extra, ((0, 0), (0, 128 - extra.shape[1])))
    packed = jnp.concatenate([q_weight, key_projection, value_projection, extra, o_weight], axis=1)
    links.label = "qkvo_ctx"
    packed_got = [links.turn(packed, step) for step in steps]

    mine, other = split_hidden(
        links, place, (gate_weight, up_weight, jnp.transpose(down_weight))
    )
    links.label = "ff_core"
    got = links.core(other)

    def for_ctx(step):
        target = (ctx + step) % ctx_size
        a, b = pick(mine, target), pick(got, target)
        return jnp.stack([jnp.where(even, a, b), jnp.where(even, b, a)])

    packed_got, (mine, got) = phase(packed_got, (mine, got))
    packed_mine = jnp.stack([packed] + packed_got)
    links.label = "qkvo_plane1"
    packed_stage = plane_start(links, packed_mine)
    links.label = "ff_ctx_a"
    near_steps, far_steps = (1, ctx_size - 1), tuple(range(2, ctx_size - 1))
    near = [links.turn(for_ctx(step), step) for step in near_steps]
    far = [for_ctx(step) for step in far_steps]
    links.label = "qkvo_core"
    packed_stage, near, far, (own_piece, early) = phase(
        packed_stage, near, far, (for_ctx(0), links.core(packed_mine))
    )
    links.label = "ff_ctx_b"
    far = [links.turn(piece, step) for step, piece in zip(far_steps, far)]
    links.label = "qkvo_plane2"
    packed_parts = plane_end(links, packed_mine, *packed_stage)
    links.label = "ff_own1"
    own_stage = plane_start(links, own_piece)
    near, far, late, own_stage = phase(near, far, packed_parts[3:], own_stage)
    links.label = "qkvo_core"
    pieces = [*packed_parts[:3], *late, early]
    pieces.append(links.core(jnp.concatenate([*packed_parts[1:3], *late])))
    sizes, qkv_columns = (ctx_size, fsdp_size // 2), packed.shape[1] - width
    weight_qkv = Rows(sizes, pieces, rows_layout(ctx_size), 0, qkv_columns)
    weight_o = Rows(sizes, pieces, rows_layout(ctx_size), qkv_columns, width)
    links.label = "ff_plane1"
    moved = dict(zip(near_steps + far_steps, near + far))
    moved_piece = jnp.concatenate([moved[step] for step in steps])
    moved_stage = plane_start(links, moved_piece)

    low_tokens, out_low = tokens[0], cotangent[0]
    cosine, sine = (x[:, 0] for x in angle_tables(positions[0]))
    cosine = jnp.concatenate([cosine, cosine], axis=1)
    sine = jnp.concatenate([-sine, sine], axis=1)
    place_column = positions[0][:, None]
    wide, narrow = (count, width), (count, 2 * KV_WIDTH)

    def qkv(*refs):
        qkv_body(shard_rows, *refs)

    normed_one, query, pairs, small = call(
        qkv,
        place,
        (low_tokens, cosine, sine),
        weight_qkv,
        [(wide, BF16), (wide, BF16), (narrow, BF16), ((8, width), F32)],
        0,
    )
    links.label = "kv"
    blocks = [pairs] + [links.shift(pairs, step) for step in steps]
    mixed_low, hidden_one, normed_two = call(
        mix_body,
        place,
        (low_tokens, small, place_column, query, *blocks),
        weight_o,
        [(wide, BF16), (wide, F32), (wide, BF16)],
        0,
    )

    out_row = lax.all_gather(after(out_low, *far), "ctx", axis=0, tiled=True)
    normed_row = lax.all_gather(normed_two, "ctx", axis=0, tiled=True)
    links.label = "gy_core"
    out_other = links.core(out_row)
    links.label = "ff_plane2"
    half = ctx_size - 1
    last = [
        links.plane(jnp.concatenate([moved_stage[1][:half], own_stage[1][:1]]), 2),
        links.plane(jnp.concatenate([moved_stage[0][half:], own_stage[0][1:]]), 4),
    ]
    own_entries = [(0, 0), (0, 1)]
    entries = [(step, core) for step in steps for core in range(2)]
    layout = [(own_entries, mask, x) for mask, x in enumerate((own_piece, *own_stage))]
    layout += [(entries, mask, x) for mask, x in enumerate((moved_piece, *moved_stage))]
    layout += [
        (entries[:half] + own_entries[:1], 3, last[0]),
        (entries[half:] + own_entries[1:], 3, last[1]),
    ]
    links.label = "n2_core"
    normed_other = links.core(after(normed_row, *last, out_other))
    block = own_piece.shape[3]
    ff_widths = (block, block, block, width)
    act_a, gate_a, up_a, down_a = ff_call(
        links, ff_kernel, layout, place, (normed_row, out_row), ff_widths, 3
    )
    normed_other = after(normed_other, act_a)
    act_b, gate_b, up_b, down_b = ff_call(
        links, ff_kernel, layout, place, (normed_other, out_other), ff_widths, 3
    )
    links.label = "gn2_core"
    down_got = links.core(down_b)
    normed_rows = lax.all_gather(after(normed_one, normed_row), "ctx", axis=0, tiled=True)
    grad_normed_two = lax.psum_scatter(
        after(added(down_a, down_got), normed_rows), "ctx", scatter_dimension=0, tiled=True
    )

    rights = (gate_a, gate_b, up_a, up_b, act_a, act_b)
    lefts = (after(normed_row, down_got), normed_other, out_row, out_other)
    send_terms = ff_grad_terms(place, lefts, rights, lambda j: 2 + j, lambda j: 1 + 2 * j, (1, 2))
    links.label = "ff_sum1"
    ff_first = reduce_start(links, send_terms)
    links.label = "y_core"
    y_a, y_b = ff_call(
        links, y_kernel, layout, place, (after(act_a, *send_terms), act_b), (width, width), 1
    )
    y_got = links.core(y_b)
    grad_normed_two = after(grad_normed_two, y_b, *ff_first[::2])

    def mix_back(*refs):
        mix_back_body(1, *refs)

    grad_hidden, grad_hidden_low, grad_query, gain_two, *pair_terms = call(
        mix_back,
        place,
        (grad_normed_two, hidden_one, small, out_low, place_column, query, cosine, sine, *blocks),
        weight_o,
        [(wide, F32), (wide, BF16), (wide, BF16), ((1, width), F32)] + [(narrow, BF16)] * ctx_size,
        BACK_COST,
    )
    links.label = "y_core"
    mixed_rows = lax.all_gather(
        after(mixed_low, grad_normed_two), "ctx", axis=0, tiled=True
    )
    lefts = (after(normed_row, grad_hidden_low, y_got), *lefts[1:])
    ff_terms = ff_grad_terms(place, lefts, rights, lambda j: j, lambda j: 2 * j, (3,))
    links.label = "gkv"
    pair_terms = [pair_terms[0]] + [links.shift(pair_terms[step], -step) for step in steps]
    pair_terms[0] = after(pair_terms[0], ff_terms[0])
    def columns_over_ctx(parts):
        whole = jnp.zeros_like(parts)
        whole = lax.dynamic_update_index_in_dim(whole, pick(parts, ctx), ctx, 0)
        for step in steps:
            piece = links.turn(pick(parts, (ctx + step) % ctx_size), step)
            whole = lax.dynamic_update_index_in_dim(whole, piece, (ctx - step) % ctx_size, 0)
        return whole

    def qkv_back(*refs):
        qkv_back_body(ctx_size, *refs)

    columns = (width + 2 * KV_WIDTH) // ctx_size
    share_shape = (count + 16, columns + width // ctx_size)
    grad_stream, *shares = call(
        qkv_back,
        place,
        (*pair_terms, low_tokens, small, cosine, sine, grad_query, grad_hidden, grad_hidden_low, gain_two),
        weight_qkv,
        [(wide, F32)] + [(share_shape, BF16)] * ctx_size,
        0,
        [pltpu.VMEM((ctx_size, *share_shape), BF16)],
    )

    links.label = "gqkv_ctx"
    first_share = shares[0]
    shares = [first_share] + [links.turn(shares[step], step) for step in steps]
    shares[0] = after(shares[0], *ff_first)
    y_both = after(added(y_a, y_got), *shares[1:])
    y_sum = lax.psum_scatter(y_both, "ctx", scatter_dimension=0, tiled=True)
    layer_out = hidden_one + y_sum.astype(F32)
    links.label = "ff_sum2"
    ff_second = reduce_next(links, ff_terms, phase(ff_first, (first_share,))[0])
    chips = fsdp_size // 2
    term_shape = (chips, width // fsdp_size + 16, share_shape[1])
    term_mine, term_other = small_call(
        term_kernel,
        (*shares, normed_rows, mixed_rows),
        [(term_shape, BF16)] * 2,
        [
            pltpu.VMEM((ctx_size * count, share_shape[1]), BF16),
            pltpu.VMEM((width, share_shape[1]), F32),
            pltpu.VMEM((fsdp_size, share_shape[1]), F32),
        ],
        place,
    )
    links.label = "term_core"
    keep, *sends = small_call(
        sum_cores_kernel,
        (term_mine, links.core(term_other)),
        [(term_shape[1:], F32)] + [(term_shape[1:], BF16)] * (chips - 1),
    )
    links.label = "term_plane"
    q_columns, kv_columns = width // ctx_size, KV_WIDTH // ctx_size
    height, devices = width // fsdp_size, ctx_size * fsdp_size
    plane_got = [links.plane(x, 2 * mask) for mask, x in enumerate(sends, 1)]
    grad_q, grad_k, grad_v, grad_o, *vectors = small_call(
        sum_plane_kernel,
        (keep, *plane_got),
        [((height, q_columns), F32)]
        + [((kv_columns, height), F32)] * 2
        + [((height, q_columns), F32)]
        + [((1, x // devices), F32) for x in (width, width, width, KV_WIDTH, KV_WIDTH)],
        cost=0,
    )
    vectors = [x[0] for x in vectors]

    links.label = "final_core"
    ff_mine, ff_send = reduce_end(place, ff_terms, ff_first, phase(ff_second, sends)[0])
    hidden = 2 * ff_mine.shape[2]
    grad_gate, grad_up, grad_down = small_call(
        join_cores_kernel,
        (ff_mine, after(links.core(ff_send), *sends)),
        [((height, hidden), F32)] * 3,
        place=place,
        cost=2*10**9,
    )

    return (
        layer_out[None],
        grad_stream[None],
        vectors[0],
        grad_q,
        vectors[2],
        jnp.transpose(grad_k),
        vectors[3],
        jnp.transpose(grad_v),
        vectors[4],
        grad_o,
        vectors[1],
        grad_gate,
        grad_up,
        jnp.transpose(grad_down),
    )


def solution(mesh):
    links = Links(mesh.shape["ctx"], mesh.shape["fsdp"])
    vector, matrix, stream = P(BOTH), P(BOTH, None), P("fsdp", "ctx", None)
    grid = P("fsdp", "ctx")
    in_specs = (
        stream,
        grid,
        vector,
        matrix,
        vector,
        matrix,
        vector,
        matrix,
        vector,
        matrix,
        vector,
        matrix,
        matrix,
        P(None, BOTH),
        stream,
    )
    out_specs = (
        stream,
        stream,
        vector,
        grid,
        vector,
        grid,
        vector,
        grid,
        vector,
        grid,
        vector,
        grid,
        grid,
        P("ctx", "fsdp"),
    )

    def run(*arrays):
        plane_of_four = mesh.shape["fsdp"] == 8 and arrays[3].shape[0] % 16 == 0
        form = per_device_plane_of_four if plane_of_four else per_device_any_mesh
        return form(*arrays, links=links)

    return jax.shard_map(run, mesh=mesh, in_specs=in_specs, out_specs=out_specs, check_vma=False)
```

```python
import jax
import jax.numpy as jnp
from jax import lax
from jax.experimental import pallas as pl
from jax.experimental.pallas import tpu as pltpu
from jax.sharding import PartitionSpec as P

QUERY_HEADS = 12
KEY_VALUE_HEADS = 2
HEAD_SIZE = 128
GROUP = QUERY_HEADS // KEY_VALUE_HEADS
KV_WIDTH = KEY_VALUE_HEADS * HEAD_SIZE
EPSILON = 1e-06
BACK_COST = 8 * 10**9
BOTH = ("ctx", "fsdp")
F32 = jnp.float32
BF16 = jnp.bfloat16


def dot(a, b, dims):
    return lax.dot_general(a, b, ((dims[:1], dims[1:]), ((), ())), preferred_element_type=F32)


def nn(a, b):
    return dot(a, b, (1, 0))


def nt(a, b):
    return dot(a, b, (1, 1))


def tn(a, b):
    return dot(a, b, (0, 0))


def rms_scale(matrix):
    return lax.rsqrt(jnp.mean(matrix * matrix, axis=-1, keepdims=True) + EPSILON)


def angle_tables(positions):
    step_index = jnp.arange(HEAD_SIZE // 2, dtype=F32) * 2.0
    frequency = 10000.0 ** (-step_index / HEAD_SIZE)
    angles = positions.astype(F32)[:, None] * frequency[None, :]
    return jnp.cos(angles)[:, None, :], jnp.sin(angles)[:, None, :]


def rotate(matrix, cosine, sine):
    rows = matrix.shape[0]
    heads = matrix.reshape(rows, -1, HEAD_SIZE)
    a, b = heads[..., : HEAD_SIZE // 2], heads[..., HEAD_SIZE // 2 :]
    turned = jnp.concatenate([a * cosine - b * sine, b * cosine + a * sine], axis=-1)
    return turned.reshape(rows, -1)


def pick(stacked, index):
    return lax.dynamic_index_in_dim(stacked, index, 0, keepdims=False)


class Links:
    def __init__(self, ctx_size, fsdp_size):
        self.ctx_size, self.fsdp_size = ctx_size, fsdp_size
        self.label = "move"
        self.planes = [m for m in (2, 4, 8, 16, 32, 64) if m < fsdp_size]

    def send(self, x, target):
        pairs = []
        for c in range(self.ctx_size):
            for f in range(self.fsdp_size):
                to = target(c, f)
                if to is not None:
                    pairs.append((c * self.fsdp_size + f, to[0] * self.fsdp_size + to[1]))
        with jax.named_scope(self.label):
            return lax.ppermute(x, BOTH, pairs)

    def core(self, x):
        return self.send(x, lambda c, f: (c, f ^ 1))

    def plane(self, x, mask):
        return self.send(x, lambda c, f: (c, f ^ mask))

    def turn(self, x, step):
        return self.send(x, lambda c, f: ((c + step) % self.ctx_size, f))

    def shift(self, x, step):
        return self.send(
            x, lambda c, f: (c + step, f) if 0 <= c + step < self.ctx_size else None
        )


def plane_gather(links, shard):
    first, second, *rest = links.planes
    half = shard.shape[0] // 2
    a = links.plane(shard, first)
    b = links.plane(shard, second)
    low = links.plane(b[:half], first)
    high = links.plane(a[half:], second)
    pieces = {0: shard, first: a, second: b, first | second: jnp.concatenate([low, high])}
    for mask in rest:
        pieces.update({had | mask: links.plane(piece, mask) for had, piece in pieces.items()})
    return pieces


def ff_weight(links, ctx, chip, core, shard):
    ctx_size = links.ctx_size
    rows, hidden = shard.shape
    block = hidden // (2 * ctx_size)
    parts = jnp.transpose(shard.reshape(rows, ctx_size, 2, block), (2, 1, 0, 3))
    mine, other = pick(parts, core), pick(parts, 1 - core)
    got = links.core(other)
    even = core == 0
    pairs = jnp.stack([jnp.where(even, mine, got), jnp.where(even, got, mine)], axis=1)
    by_source = jnp.zeros_like(pairs)
    by_source = lax.dynamic_update_index_in_dim(by_source, pick(pairs, ctx), ctx, 0)
    for step in range(1, ctx_size):
        piece = links.turn(pick(pairs, (ctx + step) % ctx_size), step)
        by_source = lax.dynamic_update_index_in_dim(by_source, piece, (ctx - step) % ctx_size, 0)
    pieces = plane_gather(links, by_source)
    whole = jnp.zeros((ctx_size, links.fsdp_size // 2, 2, rows, block), shard.dtype)
    for mask, piece in pieces.items():
        whole = lax.dynamic_update_index_in_dim(whole, piece, chip ^ (mask // 2), 1)
    return whole.reshape(-1, block)


def spread_tokens(links, x):
    row = jnp.concatenate([x] + [links.turn(x, step) for step in range(1, links.ctx_size)])
    return jnp.concatenate([row, links.core(row)])


def collect_tokens(links, partial):
    rows = partial.shape[0] // 2
    got = links.core(partial[rows:].astype(BF16))
    count = rows // links.ctx_size
    row = (partial[:rows].astype(F32) + got.astype(F32)).reshape(links.ctx_size, count, -1)
    total = row[0]
    for step in range(1, links.ctx_size):
        total = total + links.turn(row[step].astype(BF16), -step).astype(F32)
    return total


def per_device_any_mesh(
    tokens,
    positions,
    norm1_gain,
    q_weight,
    q_bias,
    key_projection,
    key_bias_vector,
    value_projection,
    value_bias_vector,
    o_weight,
    norm2_gain,
    gate_weight,
    up_weight,
    down_weight,
    cotangent,
    *,
    links,
):
    ctx_size, fsdp_size = links.ctx_size, links.fsdp_size
    ctx, row_index = lax.axis_index("ctx"), lax.axis_index("fsdp")
    chip, core = row_index // 2, row_index % 2
    count, width = tokens.shape[1:]
    scale = HEAD_SIZE ** (-0.5)
    even = core == 0

    shard_rows = q_weight.shape[0]

    def column(x):
        return jnp.pad(x, (0, shard_rows - x.shape[0]))[:, None]

    kv_bias_rows = key_bias_vector.shape[0]
    extra = jnp.concatenate(
        [
            column(x)
            for x in (norm1_gain, q_bias, norm2_gain, key_bias_vector, value_bias_vector)
        ],
        axis=1,
    )
    extra = jnp.pad(extra, ((0, 0), (0, 128 - extra.shape[1])))
    packed = jnp.concatenate([q_weight, key_projection, value_projection, extra], axis=1)
    packed = lax.all_gather(packed, BOTH, axis=0, tiled=True)
    weight_o = lax.all_gather(o_weight, BOTH, axis=0, tiled=True)

    weight_gate = ff_weight(links, ctx, chip, core, gate_weight)
    weight_up = ff_weight(links, ctx, chip, core, up_weight)
    weight_down = ff_weight(links, ctx, chip, core, jnp.transpose(down_weight))

    qkv_width = width + 2 * KV_WIDTH
    weight_qkv = packed[:, :qkv_width]
    small = jnp.transpose(packed[:, qkv_width:])[:5].astype(F32)
    gain_one, bias_q, gain_two = small[0:1], small[1:2], small[2:3]

    def bias_of(row):
        return row.reshape(-1, shard_rows)[:, :kv_bias_rows].reshape(1, -1)

    bias_k, bias_v = bias_of(small[3]), bias_of(small[4])
    out_low = cotangent[0]
    group_out = spread_tokens(links, out_low)

    stream = tokens[0].astype(F32)
    scale_one = rms_scale(stream)
    unit_one = stream * scale_one
    normed_one = (unit_one * gain_one).astype(BF16)
    cosine, sine = angle_tables(positions[0])
    linear = nn(normed_one, weight_qkv)
    query = rotate(linear[:, :width] + bias_q, cosine, sine).astype(BF16)
    key = rotate(linear[:, width : width + KV_WIDTH] + bias_k, cosine, sine).astype(BF16)
    value = (linear[:, width + KV_WIDTH :] + bias_v).astype(BF16)
    pairs = jnp.concatenate([key, value], axis=1)
    row_pairs = jnp.concatenate(
        [pairs] + [links.shift(pairs, step) for step in range(1, ctx_size)]
    )
    keys = row_pairs[:, :KV_WIDTH].reshape(-1, KEY_VALUE_HEADS, HEAD_SIZE)
    values = row_pairs[:, KV_WIDTH:].reshape(-1, KEY_VALUE_HEADS, HEAD_SIZE)
    local_index = jnp.arange(count)
    key_index = jnp.concatenate(
        [(ctx - step) * count + local_index for step in range(ctx_size)]
    )
    query_index = ctx * count + local_index
    doc_start = query_index - positions[0]
    allowed = (key_index[None, :] >= doc_start[:, None]) & (
        key_index[None, :] <= query_index[:, None]
    )
    query_heads = query.reshape(count, KEY_VALUE_HEADS, GROUP, HEAD_SIZE)
    scores = jnp.einsum("qkgd,rkd->kgqr", query_heads, keys, preferred_element_type=F32) * scale
    scores = jnp.where(allowed, scores, -1e30)
    top = jnp.max(scores, axis=-1, keepdims=True)
    weights = jnp.where(allowed, jnp.exp(scores - top), 0.0)
    probs = weights / jnp.sum(weights, axis=-1, keepdims=True)
    probs_low = probs.astype(BF16)
    mixed = jnp.einsum("kgqr,rkd->qkgd", probs_low, values, preferred_element_type=F32)
    mixed_low = mixed.reshape(count, -1).astype(BF16)
    hidden_one = stream + nn(mixed_low, weight_o)

    scale_two = rms_scale(hidden_one)
    unit_two = hidden_one * scale_two
    normed_two = (unit_two * gain_two).astype(BF16)
    group_normed = spread_tokens(links, normed_two)
    gate_pre = nn(group_normed, weight_gate)
    up_pre = nn(group_normed, weight_up)
    grad_act = nn(group_out, weight_down)
    sigmoid_gate = jax.nn.sigmoid(gate_pre)
    activated = (gate_pre * sigmoid_gate * up_pre).astype(BF16)
    grad_gate_low = (
        grad_act * up_pre * sigmoid_gate * (1.0 + gate_pre * (1.0 - sigmoid_gate))
    ).astype(BF16)
    grad_up_low = (grad_act * gate_pre * sigmoid_gate).astype(BF16)
    grad_normed_two = collect_tokens(
        links, nt(grad_gate_low, weight_gate) + nt(grad_up_low, weight_up)
    )
    layer_out = hidden_one + collect_tokens(links, nt(activated, weight_down))

    planes = [
        [c * fsdp_size + 2 * p + k for p in range(fsdp_size // 2)]
        for c in range(ctx_size)
        for k in range(2)
    ]

    def ff_grad(left, right):
        term = tn(left, right).astype(BF16)
        part = lax.psum_scatter(
            term, BOTH, scatter_dimension=0, tiled=True, axis_index_groups=planes
        )
        part = part.reshape(2, -1, part.shape[1])
        mine, got = pick(part, core), links.core(pick(part, 1 - core))
        return jnp.concatenate(
            [jnp.where(even, mine, got), jnp.where(even, got, mine)], axis=1
        ).astype(F32)

    grad_gate = ff_grad(group_normed, grad_gate_low)
    grad_up = ff_grad(group_normed, grad_up_low)
    grad_down = jnp.transpose(ff_grad(group_out, activated))

    grad_gain_two = jnp.sum(grad_normed_two * unit_two, axis=0)
    weighted_two = grad_normed_two * gain_two
    grad_hidden = out_low.astype(F32) + scale_two * (
        weighted_two - unit_two * jnp.mean(weighted_two * unit_two, axis=-1, keepdims=True)
    )

    grad_hidden_low = grad_hidden.astype(BF16)
    grad_mixed = nt(grad_hidden_low, weight_o).astype(BF16)
    grad_mixed = grad_mixed.reshape(count, KEY_VALUE_HEADS, GROUP, HEAD_SIZE)
    grad_probs = jnp.einsum("qkgd,rkd->kgqr", grad_mixed, values, preferred_element_type=F32)
    delta = jnp.sum(probs * grad_probs, axis=-1, keepdims=True)
    grad_scores = (probs * (grad_probs - delta)).astype(BF16)
    grad_query = jnp.einsum("kgqr,rkd->qkgd", grad_scores, keys, preferred_element_type=F32)
    grad_key = (
        jnp.einsum("kgqr,qkgd->rkd", grad_scores, query_heads, preferred_element_type=F32) * scale
    )
    grad_value = jnp.einsum("kgqr,qkgd->rkd", probs_low, grad_mixed, preferred_element_type=F32)
    pair_terms = jnp.concatenate(
        [grad_key.reshape(-1, KV_WIDTH), grad_value.reshape(-1, KV_WIDTH)], axis=1
    ).reshape(ctx_size, count, -1)
    pair_grads = pair_terms[0]
    for step in range(1, ctx_size):
        pair_grads = pair_grads + links.shift(pair_terms[step].astype(BF16), -step).astype(F32)
    grad_q_low = rotate(grad_query.reshape(count, -1) * scale, cosine, -sine).astype(BF16)
    grad_k_low = rotate(pair_grads[:, :KV_WIDTH], cosine, -sine).astype(BF16)
    grad_v_low = pair_grads[:, KV_WIDTH:].astype(BF16)
    grad_qkv = jnp.concatenate([grad_q_low, grad_k_low, grad_v_low], axis=1)
    grad_normed_one = nt(grad_qkv, weight_qkv)
    grad_gain_one = jnp.sum(grad_normed_one * unit_one, axis=0)
    weighted_one = grad_normed_one * gain_one
    grad_stream = grad_hidden + scale_one * (
        weighted_one - unit_one * jnp.mean(weighted_one * unit_one, axis=-1, keepdims=True)
    )

    def columns_over_ctx(arrays):
        parts = jnp.concatenate([x.reshape(count, ctx_size, -1) for x in arrays], axis=2)
        parts = jnp.transpose(parts, (1, 0, 2))
        whole = jnp.zeros_like(parts)
        whole = lax.dynamic_update_index_in_dim(whole, pick(parts, ctx), ctx, 0)
        for step in range(1, ctx_size):
            piece = links.turn(pick(parts, (ctx + step) % ctx_size), step)
            whole = lax.dynamic_update_index_in_dim(whole, piece, (ctx - step) % ctx_size, 0)
        return whole.reshape(ctx_size * count, -1)

    def attention_grad(rows, arrays):
        left = lax.all_gather(rows, "ctx", axis=0, tiled=True)
        term = tn(left, columns_over_ctx(arrays)).astype(BF16)
        return lax.psum_scatter(term, "fsdp", scatter_dimension=0, tiled=True).astype(F32)

    grad_o = attention_grad(mixed_low, [grad_hidden_low])
    grad_packed = attention_grad(normed_one, [grad_q_low, grad_k_low, grad_v_low])
    q_columns, kv_columns = width // ctx_size, KV_WIDTH // ctx_size

    sums = jnp.concatenate(
        [grad_gain_one, grad_gain_two, jnp.sum(grad_qkv.astype(F32), axis=0)]
    )
    sums = lax.psum(sums, BOTH)
    device = ctx * fsdp_size + row_index

    def own(start, size):
        part = size // (ctx_size * fsdp_size)
        return lax.dynamic_slice_in_dim(sums, start + device * part, part)

    return (
        layer_out[None],
        grad_stream[None],
        own(0, width),
        grad_packed[:, :q_columns],
        own(2 * width, width),
        grad_packed[:, q_columns : q_columns + kv_columns],
        own(3 * width, KV_WIDTH),
        grad_packed[:, q_columns + kv_columns :],
        own(3 * width + KV_WIDTH, KV_WIDTH),
        grad_o,
        own(width, width),
        grad_gate,
        grad_up,
        grad_down,
    )


def after(x, *others):
    return lax.optimization_barrier((x, *others))[0]


def phase(*groups):
    flat = lax.optimization_barrier(tuple(x for group in groups for x in group))
    out = []
    for group in groups:
        out.append(list(flat[: len(group)]))
        flat = flat[len(group) :]
    return out


def plane_start(links, shard):
    return links.plane(shard, 2), links.plane(shard, 4)


def plane_end(links, shard, a, b):
    half = shard.shape[0] // 2
    return shard, a, b, links.plane(b[:half], 2), links.plane(a[half:], 4)


def load_pieces(layout, sizes, place, pieces, which, weight, semaphore):
    ctx_size, chips, rows = sizes
    for (entries, mask, _), piece in zip(layout, pieces):
        for i, (step, core) in enumerate(entries):
            source = lax.rem(place[0] - step + ctx_size, ctx_size)
            start = ((source * chips + (place[1] ^ mask)) * 2 + core) * rows
            pltpu.make_async_copy(
                piece.at[i, which],
                weight.at[pl.ds(pl.multiple_of(start, rows), rows)],
                semaphore,
            ).start()


def ff_kernel(layout, sizes, place, normed, out_grad, *refs):
    pieces, refs = refs[: len(layout)], refs[len(layout) :]
    act_ref, gate_ref, up_ref, down_ref, weights, semaphores = refs

    @pl.when(pl.program_id(0) == 0)
    def _():
        for which in range(3):
            load_pieces(
                layout, sizes, place, pieces, which, weights.at[which], semaphores.at[which]
            )

    def arrived(which):
        @pl.when(pl.program_id(0) == 0)
        def _():
            wait_all(weights.at[which], semaphores.at[which])

    x, gy = normed[...], out_grad[...]
    arrived(0)
    gate = nn(x, weights[0])
    arrived(1)
    up = nn(x, weights[1])
    arrived(2)
    grad = nn(gy, weights[2])
    sigmoid = 1.0 / (1.0 + jnp.exp(-gate))
    silu = gate * sigmoid
    grad_gate = (grad * up * sigmoid * (1.0 + gate * (1.0 - sigmoid))).astype(BF16)
    grad_up = (grad * silu).astype(BF16)
    act_ref[...] = (silu * up).astype(BF16)
    gate_ref[...] = grad_gate
    up_ref[...] = grad_up
    down_ref[...] = (nt(grad_gate, weights[0]) + nt(grad_up, weights[1])).astype(BF16)


def y_kernel(layout, sizes, place, act_a, act_b, *refs):
    pieces, (y_a, y_b, weight, semaphore) = refs[: len(layout)], refs[len(layout) :]

    @pl.when(pl.program_id(0) == 0)
    def _():
        load_pieces(layout, sizes, place, pieces, 2, weight, semaphore)
        wait_all(weight, semaphore)

    y_a[...] = nt(act_a[...], weight[...]).astype(BF16)
    y_b[...] = nt(act_b[...], weight[...]).astype(BF16)


def ff_call(links, kernel, layout, place, arrays, widths, matrices):
    tokens = arrays[0].shape[0]
    rows, block = layout[0][2].shape[2:]
    sizes = (links.ctx_size, links.fsdp_size // 2, rows)
    depth = 2 * sizes[0] * sizes[1] * rows
    tile = 256

    def spec(size):
        return pl.BlockSpec((tile, size), lambda i, place: (i, 0))

    def body(*refs):
        kernel(layout, sizes, *refs)

    if matrices == 1:
        scratch = [pltpu.VMEM((depth, block), BF16), pltpu.SemaphoreType.DMA]
    else:
        scratch = [
            pltpu.VMEM((matrices, depth, block), BF16),
            pltpu.SemaphoreType.DMA((matrices,)),
        ]
    return pl.pallas_call(
        body,
        grid_spec=pltpu.PrefetchScalarGridSpec(
            num_scalar_prefetch=1,
            grid=(tokens // tile,),
            in_specs=[spec(x.shape[1]) for x in arrays]
            + [pl.BlockSpec(memory_space=pl.ANY)] * len(layout),
            out_specs=[spec(x) for x in widths],
            scratch_shapes=scratch,
        ),
        out_shape=[jax.ShapeDtypeStruct((tokens, x), BF16) for x in widths],
        compiler_params=pltpu.CompilerParams(vmem_limit_bytes=56 * 2**20),
        cost_estimate=pl.CostEstimate(flops=0, bytes_accessed=0, transcendentals=0),
    )(place, *arrays, *[piece for _, _, piece in layout])


def grad_kernel(place, *refs):
    lefts, rights, outs = refs[:8], refs[8:14], refs[14:]
    low, high = outs[: len(outs) // 2], outs[len(outs) // 2 :]
    for which in range(3):
        first = 4 * (which // 2)
        for parts, (left_a, left_b), core in (
            (low, lefts[first : first + 2], 0),
            (high, lefts[first + 2 : first + 4], 1),
        ):
            out, at = (parts[0], which) if len(parts) == 1 else (parts[which > 0], max(which - 1, 0))
            half = left_a.shape[1] // 2
            rows = slice(core * half, (core + 1) * half)
            right_a, right_b = rights[2 * which : 2 * which + 2]
            term = tn(left_a[:, rows], right_a[...]) + tn(left_b[:, rows], right_b[...])
            out[0, at] = term.astype(BF16)


def ff_grad_terms(place, lefts, rights, low_at, high_at, parts):
    tokens, width = lefts[0].shape
    block = rights[0].shape[1]
    part = width // 4

    def left(at):
        return pl.BlockSpec((tokens, part), lambda j, place: (0, place[1] ^ at(j)))

    right = pl.BlockSpec((tokens, block), lambda j, place: (0, 0))
    outs = [pl.BlockSpec((1, n, part // 2, block), lambda j, place: (j, 0, 0, 0)) for n in parts]
    low, high = left(low_at), left(high_at)
    x_a, x_b, y_a, y_b = lefts
    return pl.pallas_call(
        grad_kernel,
        grid_spec=pltpu.PrefetchScalarGridSpec(
            num_scalar_prefetch=1,
            grid=(2,),
            in_specs=[low, low, high, high] * 2 + [right] * 6,
            out_specs=outs * 2,
        ),
        out_shape=[jax.ShapeDtypeStruct((2, n, part // 2, block), BF16) for n in parts] * 2,
        compiler_params=pltpu.CompilerParams(vmem_limit_bytes=56 * 2**20),
        cost_estimate=pl.CostEstimate(flops=0, bytes_accessed=0, transcendentals=0),
    )(place, x_a, x_b, x_a, x_b, y_a, y_b, y_a, y_b, *rights)


def added(a, b):
    return (a.astype(F32) + b.astype(F32)).astype(BF16)


def reduce_start(links, terms):
    return [links.plane(x, mask) for x, mask in zip(terms, (4, 4, 2, 2))]


def add_pairs_kernel(*refs):
    for i, out in enumerate(refs[6:]):
        keep, one, rest = refs[3 * i : 3 * i + 3]
        out[:1] = (keep[0, :1].astype(F32) + one[0].astype(F32)).astype(BF16)
        out[1:] = (keep[0, 1:].astype(F32) + rest[0].astype(F32)).astype(BF16)


def first_specs(index):
    def spec(x):
        return pl.BlockSpec((1, *x.shape[1:]), lambda i, *place: (index, 0, 0, 0))

    return spec


def reduce_next(links, terms, first):
    shape = terms[0].shape
    arrays = (terms[0], first[0], first[1], terms[1], first[2], first[3])
    spec = first_specs(1)
    whole = pl.BlockSpec(shape[1:], lambda i: (0, 0, 0))
    low, high = pl.pallas_call(
        add_pairs_kernel,
        grid=(1,),
        in_specs=[spec(x) for x in arrays],
        out_specs=[whole] * 2,
        out_shape=[jax.ShapeDtypeStruct(shape[1:], BF16)] * 2,
        compiler_params=pltpu.CompilerParams(vmem_limit_bytes=56 * 2**20),
        cost_estimate=pl.CostEstimate(flops=0, bytes_accessed=0, transcendentals=0),
    )(*arrays)
    return links.plane(low, 2), links.plane(high, 4)


def reduce_end_kernel(place, *refs):
    low, high, (mine, send) = refs[:4], refs[4:8], refs[8:]

    def write(ref, parts):
        keep, one, rest, last = parts
        total = keep[0, :1].astype(F32) + one[0].astype(F32) + last[:1].astype(F32)
        ref[:1] = total.astype(ref.dtype)
        total = keep[0, 1:].astype(F32) + rest[0].astype(F32) + last[1:].astype(F32)
        ref[1:] = total.astype(ref.dtype)

    @pl.when(place[2] == 0)
    def _():
        write(mine, low)
        write(send, high)

    @pl.when(place[2] != 0)
    def _():
        write(mine, high)
        write(send, low)


def reduce_end(place, terms, first, second):
    shape = terms[0].shape[1:]
    spec = first_specs(0)
    whole = pl.BlockSpec(shape, lambda i, place: (0, 0, 0))
    low = (terms[0], first[0], first[1])
    high = (terms[1], first[2], first[3])
    return pl.pallas_call(
        reduce_end_kernel,
        grid_spec=pltpu.PrefetchScalarGridSpec(
            num_scalar_prefetch=1,
            grid=(1,),
            in_specs=[*map(spec, low), whole, *map(spec, high), whole],
            out_specs=[whole] * 2,
        ),
        out_shape=[jax.ShapeDtypeStruct(shape, F32), jax.ShapeDtypeStruct(shape, BF16)],
        compiler_params=pltpu.CompilerParams(vmem_limit_bytes=56 * 2**20),
        cost_estimate=pl.CostEstimate(flops=12*10**9, bytes_accessed=0, transcendentals=0),
    )(place, *low, second[0], *high, second[1])


def join_cores_kernel(place, mine, got, gate, up, down):
    def write(even, odd):
        for which, ref in enumerate((gate, up, down)):
            ref[...] = jnp.concatenate([even(which), odd(which)], axis=1)

    def own(which):
        return mine[which]

    def others(which):
        return got[which].astype(F32)

    @pl.when(place[2] == 0)
    def _():
        write(own, others)

    @pl.when(place[2] != 0)
    def _():
        write(others, own)


def split_kernel(place, gate, up, down, mine, other):
    block = mine.shape[3]

    def write(core):
        for which, ref in enumerate((gate, up, down)):
            for target in range(mine.shape[0]):
                start = (2 * target + core) * block
                mine[target, which] = ref[:, start : start + block]
                start = (2 * target + 1 - core) * block
                other[target, which] = ref[:, start : start + block]

    @pl.when(place[2] == 0)
    def _():
        write(0)

    @pl.when(place[2] != 0)
    def _():
        write(1)


def split_hidden(links, place, shards):
    rows, hidden = shards[0].shape
    whole = pl.BlockSpec((rows, hidden), lambda i, place: (0, 0))
    shape = (links.ctx_size, 3, rows, hidden // (2 * links.ctx_size))
    out = pl.BlockSpec(shape, lambda i, place: (0, 0, 0, 0))
    return pl.pallas_call(
        split_kernel,
        grid_spec=pltpu.PrefetchScalarGridSpec(
            num_scalar_prefetch=1, grid=(1,), in_specs=[whole] * 3, out_specs=[out] * 2
        ),
        out_shape=[jax.ShapeDtypeStruct(shape, BF16)] * 2,
        compiler_params=pltpu.CompilerParams(vmem_limit_bytes=32 * 2**20),
    )(place, *shards)


class Rows:
    def __init__(self, sizes, pieces, layout, first, columns):
        self.sizes, self.pieces, self.layout = sizes, pieces, layout
        self.first, self.columns = first, columns
        self.rows = pieces[0].shape[-2]
        self.shape = (2 * sizes[0] * sizes[1] * self.rows, columns)

    def start(self, place, refs, weight, semaphore):
        ctx_size, chips = self.sizes
        for piece, index, step, mask, turned in self.layout:
            source = lax.rem(place[0] - step + ctx_size, ctx_size)
            start = ((source * chips + (place[1] ^ mask)) * 2 + (place[2] ^ turned)) * self.rows
            pltpu.make_async_copy(
                refs[piece].at[(*index, slice(None), pl.ds(self.first, self.columns))],
                weight.at[pl.ds(pl.multiple_of(start, self.rows), self.rows)],
                semaphore,
            ).start()


def rows_layout(ctx_size):
    half = ctx_size // 2
    layout = []
    for step in range(ctx_size):
        layout += [(mask, (step,), step, mask, 0) for mask in range(3)]
        layout.append((3, (step,), step, 3, 0) if step < half else (4, (step - half,), step, 3, 0))
        layout.append((5, (step,), step, 0, 1))
        layout += [(6, (i * ctx_size + step,), step, i + 1, 1) for i in range(3)]
    return layout


def wait_all(weight, semaphore):
    pltpu.make_async_copy(weight, weight, semaphore).wait()


def call(body, place, arrays, weight, out_shapes, cost, scratch=()):
    any_spec = pl.BlockSpec(memory_space=pl.ANY)
    vmem = pl.BlockSpec(memory_space=pltpu.VMEM)
    count, pieces = len(arrays), len(weight.pieces)

    def kernel(place, *refs):
        ins, parts, outs = refs[:count], refs[count : count + pieces], refs[count + pieces : -2]
        whole, semaphore = refs[-2:]
        weight.start(place, parts, whole, semaphore)
        body(place, ins, outs, whole, lambda: wait_all(whole, semaphore))

    return pl.pallas_call(
        kernel,
        in_specs=[pl.BlockSpec(memory_space=pltpu.SMEM)] + [vmem] * count + [any_spec] * pieces,
        out_specs=[vmem] * len(out_shapes),
        out_shape=[jax.ShapeDtypeStruct(shape, dtype) for shape, dtype in out_shapes],
        scratch_shapes=[*scratch, pltpu.VMEM(weight.shape, BF16), pltpu.SemaphoreType.DMA],
        compiler_params=pltpu.CompilerParams(vmem_limit_bytes=56 * 2**20),
        cost_estimate=pl.CostEstimate(flops=cost, bytes_accessed=0, transcendentals=0),
    )(place, *arrays, *weight.pieces)


def turn_halves(x, cosine, sine):
    return x * cosine + pltpu.roll(x, HEAD_SIZE // 2, 1) * sine


def turned_heads(x, cosine, sine):
    heads = [x[:, i : i + HEAD_SIZE] for i in range(0, x.shape[1], HEAD_SIZE)]
    return jnp.concatenate([turn_halves(x, cosine, sine) for x in heads], axis=1)


def qkv_body(shard_rows, place, ins, outs, weight, wait):
    tokens, cosine, sine = ins
    normed_ref, query_ref, pairs_ref, small_ref = outs
    width = tokens.shape[1]
    qkv_width = width + 2 * KV_WIDTH
    x = tokens[...].astype(F32)
    unit = x * rms_scale(x)
    wait()
    small = jnp.transpose(weight[:, qkv_width:].astype(F32))[:8]
    bias_rows = KV_WIDTH * shard_rows // width
    row = lax.broadcasted_iota(jnp.int32, (width, KV_WIDTH), 0)
    at = lax.broadcasted_iota(jnp.int32, (width, KV_WIDTH), 1)
    chosen = row == (at // bias_rows) * shard_rows + at % bias_rows
    kv_bias = nn(small.astype(BF16), chosen.astype(BF16))
    normed = (unit * small[0:1]).astype(BF16)
    normed_ref[...] = normed
    small_ref[...] = small
    linear = nn(normed, weight[:, :qkv_width])
    query = linear[:, :width] + small[1:2]
    key = linear[:, width : width + KV_WIDTH] + kv_bias[3:4]
    query_ref[...] = turned_heads(query, cosine[...], sine[...]).astype(BF16)
    pairs_ref[:, :KV_WIDTH] = turned_heads(key, cosine[...], sine[...]).astype(BF16)
    pairs_ref[:, KV_WIDTH:] = (linear[:, width + KV_WIDTH :] + kv_bias[4:5]).astype(BF16)


def allowed_keys(ctx, positions, blocks):
    count = positions.shape[0]
    shape = (count, blocks * count)
    column = lax.broadcasted_iota(jnp.int32, shape, 1)
    query = ctx * count + lax.broadcasted_iota(jnp.int32, shape, 0)
    key = (ctx - column // count) * count + column % count
    return (key >= query - positions) & (key <= query)


def heads_of(x, group):
    first = group * GROUP
    return jnp.concatenate(
        [x[:, i * HEAD_SIZE : (i + 1) * HEAD_SIZE] for i in range(first, first + GROUP)], axis=0
    )


def softmax_of(query, keys, allowed):
    scores = nt(query, keys) * HEAD_SIZE ** (-0.5)
    scores = jnp.where(allowed, scores, -1e30)
    weights = jnp.exp(scores - jnp.max(scores, axis=-1, keepdims=True))
    weights = jnp.where(allowed, weights, 0.0)
    return weights / jnp.sum(weights, axis=-1, keepdims=True)


def group_pairs(blocks, group):
    def columns(start):
        return jnp.concatenate([b[:, start : start + HEAD_SIZE] for b in blocks], axis=0)

    return columns(group * HEAD_SIZE), columns(KV_WIDTH + group * HEAD_SIZE)


def mix_body(place, ins, outs, weight, wait):
    tokens, small, positions, query, *blocks = ins
    mixed_ref, hidden_ref, normed_ref = outs
    count = tokens.shape[0]
    allowed = allowed_keys(place[0], positions[...], len(blocks))
    allowed = jnp.concatenate([allowed.astype(F32)] * GROUP, axis=0) > 0
    for group in range(KEY_VALUE_HEADS):
        keys, values = group_pairs(blocks, group)
        probs = softmax_of(heads_of(query, group), keys, allowed)
        mixed = nn(probs.astype(BF16), values).astype(BF16)
        for h in range(GROUP):
            start = (group * GROUP + h) * HEAD_SIZE
            mixed_ref[:, start : start + HEAD_SIZE] = mixed[h * count : (h + 1) * count]
    wait()
    hidden = tokens[...].astype(F32) + nn(mixed_ref[...], weight[...])
    hidden_ref[...] = hidden
    normed_ref[...] = (hidden * rms_scale(hidden) * small[2:3]).astype(BF16)


def norm_back(unit, scale, grad, gain):
    weighted = grad * gain
    return scale * (weighted - unit * jnp.mean(weighted * unit, axis=-1, keepdims=True))


def mix_back_body(steps, place, ins, outs, weight, wait):
    terms, ins = ins[:steps], ins[steps:]
    hidden_ref, small, out_grad, positions, query, cosine, sine, *blocks = ins
    grad_hidden_ref, low_ref, grad_query_ref, gain_ref, *pair_refs = outs
    count = hidden_ref.shape[0]
    hidden = hidden_ref[...]
    scale = rms_scale(hidden)
    unit = hidden * scale
    grad = terms[0][...].astype(F32)
    for term in terms[1:]:
        grad = grad + term[...].astype(F32)
    gain_ref[...] = jnp.sum(grad * unit, axis=0, keepdims=True)
    grad_hidden = out_grad[...].astype(F32) + norm_back(unit, scale, grad, small[2:3])
    grad_hidden_ref[...] = grad_hidden
    low = grad_hidden.astype(BF16)
    low_ref[...] = low
    wait()
    grad_mixed = nt(low, weight[...]).astype(BF16)
    allowed = allowed_keys(place[0], positions[...], len(blocks))
    allowed = jnp.concatenate([allowed.astype(F32)] * GROUP, axis=0) > 0
    score_scale = HEAD_SIZE ** (-0.5)
    for group in range(KEY_VALUE_HEADS):
        keys, values = group_pairs(blocks, group)
        queries, grads = heads_of(query, group), heads_of(grad_mixed, group)
        probs = softmax_of(queries, keys, allowed)
        grad_probs = nt(grads, values)
        delta = jnp.sum(probs * grad_probs, axis=-1, keepdims=True)
        grad_scores = (probs * (grad_probs - delta)).astype(BF16)
        grad_query = nn(grad_scores, keys) * score_scale
        for h in range(GROUP):
            start = (group * GROUP + h) * HEAD_SIZE
            grad_query_ref[:, start : start + HEAD_SIZE] = turn_halves(
                grad_query[h * count : (h + 1) * count], cosine[...], -sine[...]
            ).astype(BF16)
        grad_key = (tn(grad_scores, queries) * score_scale).astype(BF16)
        grad_value = tn(probs.astype(BF16), grads).astype(BF16)
        start = group * HEAD_SIZE
        for block, ref in enumerate(pair_refs):
            rows = slice(block * count, (block + 1) * count)
            ref[:, start : start + HEAD_SIZE] = grad_key[rows]
            ref[:, KV_WIDTH + start : KV_WIDTH + start + HEAD_SIZE] = grad_value[rows]


def qkv_back_body(steps, place, ins, outs, weight, wait):
    terms, ins = ins[:steps], ins[steps:]
    tokens, small, cosine, sine, grad_query, grad_hidden, grad_hidden_low, gain_two = ins
    stream_ref, *share_refs, share_ref = outs
    count, width = tokens.shape
    pairs = terms[0][...].astype(F32)
    for term in terms[1:]:
        pairs = pairs + term[...].astype(F32)
    grad_key = turned_heads(pairs[:, :KV_WIDTH], cosine[...], -sine[...]).astype(BF16)
    grad_value = pairs[:, KV_WIDTH:].astype(BF16)
    wait()
    kv_end = width + KV_WIDTH
    grad = (
        nt(grad_query[...], weight[:, :width])
        + nt(grad_key, weight[:, width:kv_end])
        + nt(grad_value, weight[:, kv_end : kv_end + KV_WIDTH])
    )
    x = tokens[...].astype(F32)
    scale = rms_scale(x)
    unit = x * scale
    stream_ref[...] = grad_hidden[...] + norm_back(unit, scale, grad, small[0:1])
    gains = jnp.concatenate([jnp.sum(grad * unit, axis=0, keepdims=True), gain_two[...]], axis=0)
    gains = jnp.concatenate([gains, jnp.zeros((14, width), F32)], axis=0).astype(BF16)
    targets = share_ref.shape[0]
    q_columns, kv_columns = width // targets, KV_WIDTH // targets
    for target in range(targets):
        q, kv = target * q_columns, target * kv_columns
        share_ref[target, :count, :q_columns] = grad_query[:, q : q + q_columns]
        kv_end = q_columns + 2 * kv_columns
        share_ref[target, :count, q_columns:kv_end] = jnp.concatenate(
            [grad_key[:, kv : kv + kv_columns], grad_value[:, kv : kv + kv_columns]], axis=1
        )
        share_ref[target, :count, kv_end:] = grad_hidden_low[:, q : q + q_columns]
        share_ref[target, count:, :q_columns] = gains[:, q : q + q_columns]
        share_ref[target, count:, q_columns:] = jnp.zeros(
            (16, share_ref.shape[2] - q_columns), BF16
        )
    for step, ref in enumerate(share_refs):
        ref[...] = share_ref[lax.rem(place[0] + step, targets)]


def term_kernel(place, *refs):
    *shares, normed_rows, mixed_rows, mine, other, share, terms, vectors = refs
    ctx_size, width = len(shares), normed_rows.shape[1]
    count = normed_rows.shape[0] // ctx_size
    chips, height = mine.shape[0], mine.shape[1] - 16
    devices = 2 * chips
    q_columns, kv_columns = width // ctx_size, KV_WIDTH // ctx_size
    kv_end = q_columns + 2 * kv_columns
    gains = jnp.zeros((16, q_columns), F32)
    for step, ref in enumerate(shares):
        source = lax.rem(place[0] - step + ctx_size, ctx_size)
        share[pl.ds(pl.multiple_of(source * count, count), count)] = ref[:count]
        gains = gains + ref[count:, :q_columns].astype(F32)
    terms[:, :kv_end] = tn(normed_rows[...], share[:, :kv_end])
    terms[:, kv_end:] = tn(mixed_rows[...], share[:, kv_end:])
    biases = jnp.sum(share[:, :kv_end].astype(F32), axis=0, keepdims=True)
    vectors[...] = jnp.zeros_like(vectors)
    parts = (gains[0:1], gains[1:2], biases[:, :q_columns])
    parts += (biases[:, q_columns : q_columns + kv_columns], biases[:, q_columns + kv_columns :])
    for f in range(devices):
        start = 0
        for part in parts:
            size = part.shape[1] // devices
            vectors[f : f + 1, start : start + size] = part[:, f * size : (f + 1) * size]
            start += size
    first = lax.broadcasted_iota(jnp.int32, (16, terms.shape[1]), 0) == 0
    for ref, core in ((mine, place[2]), (other, 1 - place[2])):
        for mask in range(chips):
            f = (place[1] ^ mask) * 2 + core
            start = pl.multiple_of(f * height, 64)
            ref[mask, :height] = terms[pl.ds(start, height)].astype(BF16)
            row = jnp.broadcast_to(vectors[pl.ds(f, 1)], first.shape)
            ref[mask, height:] = jnp.where(first, row, 0.0).astype(BF16)


def sum_cores_kernel(mine, got, keep, *sends):
    keep[...] = mine[0].astype(F32) + got[0].astype(F32)
    for mask, ref in enumerate(sends, 1):
        ref[...] = (mine[mask].astype(F32) + got[mask].astype(F32)).astype(BF16)


def sum_plane_kernel(keep, *refs):
    got, outs = refs[:3], refs[3:]
    total = keep[...] + got[0][...].astype(F32) + got[1][...].astype(F32) + got[2][...].astype(F32)
    height = total.shape[0] - 16
    start = 0
    for ref, turned in zip(outs[:4], (False, True, True, False)):
        size = ref.shape[0] if turned else ref.shape[1]
        part = total[:height, start : start + size]
        ref[...] = jnp.transpose(part) if turned else part
        start += size
    start = 0
    for ref in outs[4:]:
        ref[...] = total[height : height + 1, start : start + ref.shape[1]]
        start += ref.shape[1]


def small_call(body, arrays, out_shapes, scratch=(), place=None, cost=0):
    vmem = pl.BlockSpec(memory_space=pltpu.VMEM)
    smem = [] if place is None else [place]
    return pl.pallas_call(
        body,
        in_specs=[pl.BlockSpec(memory_space=pltpu.SMEM)] * len(smem) + [vmem] * len(arrays),
        out_specs=[vmem] * len(out_shapes),
        out_shape=[jax.ShapeDtypeStruct(shape, dtype) for shape, dtype in out_shapes],
        scratch_shapes=list(scratch),
        compiler_params=pltpu.CompilerParams(vmem_limit_bytes=56 * 2**20),
        cost_estimate=pl.CostEstimate(flops=cost, bytes_accessed=0, transcendentals=0),
    )(*smem, *arrays)


def per_device_plane_of_four(
    tokens,
    positions,
    norm1_gain,
    q_weight,
    q_bias,
    key_projection,
    key_bias_vector,
    value_projection,
    value_bias_vector,
    o_weight,
    norm2_gain,
    gate_weight,
    up_weight,
    down_weight,
    cotangent,
    *,
    links,
):
    ctx_size, fsdp_size = links.ctx_size, links.fsdp_size
    ctx, row_index = lax.axis_index("ctx"), lax.axis_index("fsdp")
    chip, core = row_index // 2, row_index % 2
    place = jnp.stack([ctx, chip, core])
    count, width = tokens.shape[1:]
    shard_rows = q_weight.shape[0]
    even = core == 0
    steps = range(1, ctx_size)

    def column(x):
        return jnp.pad(x, (0, shard_rows - x.shape[0]))[:, None]

    extra = jnp.concatenate(
        [
            column(x)
            for x in (norm1_gain, q_bias, norm2_gain, key_bias_vector, value_bias_vector)
        ],
        axis=1,
    )
    extra = jnp.pad(extra, ((0, 0), (0, 128 - extra.shape[1])))
    packed = jnp.concatenate([q_weight, key_projection, value_projection, extra, o_weight], axis=1)
    links.label = "qkvo_ctx"
    packed_got = [links.turn(packed, step) for step in steps]

    mine, other = split_hidden(
        links, place, (gate_weight, up_weight, jnp.transpose(down_weight))
    )
    links.label = "ff_core"
    got = links.core(other)

    def for_ctx(step):
        target = (ctx + step) % ctx_size
        a, b = pick(mine, target), pick(got, target)
        return jnp.stack([jnp.where(even, a, b), jnp.where(even, b, a)])

    packed_got, (mine, got) = phase(packed_got, (mine, got))
    packed_mine = jnp.stack([packed] + packed_got)
    links.label = "qkvo_plane1"
    packed_stage = plane_start(links, packed_mine)
    links.label = "ff_ctx_a"
    near_steps, far_steps = (1, ctx_size - 1), tuple(range(2, ctx_size - 1))
    near = [links.turn(for_ctx(step), step) for step in near_steps]
    far = [for_ctx(step) for step in far_steps]
    links.label = "qkvo_core"
    packed_stage, near, far, (own_piece, early) = phase(
        packed_stage, near, far, (for_ctx(0), links.core(packed_mine))
    )
    links.label = "ff_ctx_b"
    far = [links.turn(piece, step) for step, piece in zip(far_steps, far)]
    links.label = "qkvo_plane2"
    packed_parts = plane_end(links, packed_mine, *packed_stage)
    links.label = "ff_own1"
    own_stage = plane_start(links, own_piece)
    near, far, late, own_stage = phase(near, far, packed_parts[3:], own_stage)
    links.label = "qkvo_core"
    pieces = [*packed_parts[:3], *late, early]
    pieces.append(links.core(jnp.concatenate([*packed_parts[1:3], *late])))
    sizes, qkv_columns = (ctx_size, fsdp_size // 2), packed.shape[1] - width
    weight_qkv = Rows(sizes, pieces, rows_layout(ctx_size), 0, qkv_columns)
    weight_o = Rows(sizes, pieces, rows_layout(ctx_size), qkv_columns, width)
    links.label = "ff_plane1"
    moved = dict(zip(near_steps + far_steps, near + far))
    moved_piece = jnp.concatenate([moved[step] for step in steps])
    moved_stage = plane_start(links, moved_piece)

    low_tokens, out_low = tokens[0], cotangent[0]
    cosine, sine = (x[:, 0] for x in angle_tables(positions[0]))
    cosine = jnp.concatenate([cosine, cosine], axis=1)
    sine = jnp.concatenate([-sine, sine], axis=1)
    place_column = positions[0][:, None]
    wide, narrow = (count, width), (count, 2 * KV_WIDTH)

    def qkv(*refs):
        qkv_body(shard_rows, *refs)

    normed_one, query, pairs, small = call(
        qkv,
        place,
        (low_tokens, cosine, sine),
        weight_qkv,
        [(wide, BF16), (wide, BF16), (narrow, BF16), ((8, width), F32)],
        0,
    )
    links.label = "kv"
    blocks = [pairs] + [links.shift(pairs, step) for step in steps]
    mixed_low, hidden_one, normed_two = call(
        mix_body,
        place,
        (low_tokens, small, place_column, query, *blocks),
        weight_o,
        [(wide, BF16), (wide, F32), (wide, BF16)],
        0,
    )

    out_row = lax.all_gather(after(out_low, *far), "ctx", axis=0, tiled=True)
    normed_row = lax.all_gather(normed_two, "ctx", axis=0, tiled=True)
    links.label = "gy_core"
    out_other = links.core(out_row)
    links.label = "ff_plane2"
    half = ctx_size - 1
    last = [
        links.plane(jnp.concatenate([moved_stage[1][:half], own_stage[1][:1]]), 2),
        links.plane(jnp.concatenate([moved_stage[0][half:], own_stage[0][1:]]), 4),
    ]
    own_entries = [(0, 0), (0, 1)]
    entries = [(step, core) for step in steps for core in range(2)]
    layout = [(own_entries, mask, x) for mask, x in enumerate((own_piece, *own_stage))]
    layout += [(entries, mask, x) for mask, x in enumerate((moved_piece, *moved_stage))]
    layout += [
        (entries[:half] + own_entries[:1], 3, last[0]),
        (entries[half:] + own_entries[1:], 3, last[1]),
    ]
    links.label = "n2_core"
    normed_other = links.core(after(normed_row, *last, out_other))
    block = own_piece.shape[3]
    ff_widths = (block, block, block, width)
    act_a, gate_a, up_a, down_a = ff_call(
        links, ff_kernel, layout, place, (normed_row, out_row), ff_widths, 3
    )
    normed_other = after(normed_other, act_a)
    act_b, gate_b, up_b, down_b = ff_call(
        links, ff_kernel, layout, place, (normed_other, out_other), ff_widths, 3
    )
    links.label = "gn2_core"
    down_got = links.core(down_b)
    normed_rows = lax.all_gather(after(normed_one, normed_row), "ctx", axis=0, tiled=True)
    grad_normed_two = lax.psum_scatter(
        after(added(down_a, down_got), normed_rows), "ctx", scatter_dimension=0, tiled=True
    )

    rights = (gate_a, gate_b, up_a, up_b, act_a, act_b)
    lefts = (after(normed_row, down_got), normed_other, out_row, out_other)
    send_terms = ff_grad_terms(place, lefts, rights, lambda j: 2 + j, lambda j: 1 + 2 * j, (1, 2))
    links.label = "ff_sum1"
    ff_first = reduce_start(links, send_terms)
    links.label = "y_core"
    y_a, y_b = ff_call(
        links, y_kernel, layout, place, (after(act_a, *send_terms), act_b), (width, width), 1
    )
    y_got = links.core(y_b)
    grad_normed_two = after(grad_normed_two, y_b, *ff_first[::2])

    def mix_back(*refs):
        mix_back_body(1, *refs)

    grad_hidden, grad_hidden_low, grad_query, gain_two, *pair_terms = call(
        mix_back,
        place,
        (grad_normed_two, hidden_one, small, out_low, place_column, query, cosine, sine, *blocks),
        weight_o,
        [(wide, F32), (wide, BF16), (wide, BF16), ((1, width), F32)] + [(narrow, BF16)] * ctx_size,
        BACK_COST,
    )
    links.label = "y_core"
    mixed_rows = lax.all_gather(
        after(mixed_low, grad_normed_two), "ctx", axis=0, tiled=True
    )
    lefts = (after(normed_row, grad_hidden_low, y_got), *lefts[1:])
    ff_terms = ff_grad_terms(place, lefts, rights, lambda j: j, lambda j: 2 * j, (3,))
    links.label = "gkv"
    pair_terms = [pair_terms[0]] + [links.shift(pair_terms[step], -step) for step in steps]
    pair_terms[0] = after(pair_terms[0], ff_terms[0])
    def columns_over_ctx(parts):
        whole = jnp.zeros_like(parts)
        whole = lax.dynamic_update_index_in_dim(whole, pick(parts, ctx), ctx, 0)
        for step in steps:
            piece = links.turn(pick(parts, (ctx + step) % ctx_size), step)
            whole = lax.dynamic_update_index_in_dim(whole, piece, (ctx - step) % ctx_size, 0)
        return whole

    def qkv_back(*refs):
        qkv_back_body(ctx_size, *refs)

    columns = (width + 2 * KV_WIDTH) // ctx_size
    share_shape = (count + 16, columns + width // ctx_size)
    grad_stream, *shares = call(
        qkv_back,
        place,
        (*pair_terms, low_tokens, small, cosine, sine, grad_query, grad_hidden, grad_hidden_low, gain_two),
        weight_qkv,
        [(wide, F32)] + [(share_shape, BF16)] * ctx_size,
        0,
        [pltpu.VMEM((ctx_size, *share_shape), BF16)],
    )

    links.label = "gqkv_ctx"
    first_share = shares[0]
    shares = [first_share] + [links.turn(shares[step], step) for step in steps]
    shares[0] = after(shares[0], *ff_first)
    y_both = after(added(y_a, y_got), shares[1])
    y_sum = lax.psum_scatter(y_both, "ctx", scatter_dimension=0, tiled=True)
    links.label = "ff_sum2"
    ff_second = reduce_next(links, ff_terms, phase(ff_first, (first_share,))[0])
    chips = fsdp_size // 2
    term_shape = (chips, width // fsdp_size + 16, share_shape[1])
    term_mine, term_other = small_call(
        term_kernel,
        (*shares, normed_rows, mixed_rows),
        [(term_shape, BF16)] * 2,
        [
            pltpu.VMEM((ctx_size * count, share_shape[1]), BF16),
            pltpu.VMEM((width, share_shape[1]), F32),
            pltpu.VMEM((fsdp_size, share_shape[1]), F32),
        ],
        place,
    )
    links.label = "term_core"
    keep, *sends = small_call(
        sum_cores_kernel,
        (term_mine, links.core(term_other)),
        [(term_shape[1:], F32)] + [(term_shape[1:], BF16)] * (chips - 1),
    )
    links.label = "term_plane"
    q_columns, kv_columns = width // ctx_size, KV_WIDTH // ctx_size
    height, devices = width // fsdp_size, ctx_size * fsdp_size
    plane_got = [links.plane(x, 2 * mask) for mask, x in enumerate(sends, 1)]
    grad_q, grad_k, grad_v, grad_o, *vectors = small_call(
        sum_plane_kernel,
        (keep, *plane_got),
        [((height, q_columns), F32)]
        + [((kv_columns, height), F32)] * 2
        + [((height, q_columns), F32)]
        + [((1, x // devices), F32) for x in (width, width, width, KV_WIDTH, KV_WIDTH)],
        cost=0,
    )
    vectors = [x[0] for x in vectors]

    links.label = "final_core"
    ff_mine, ff_send = reduce_end(place, ff_terms, ff_first, phase(ff_second, sends)[0])
    hidden = 2 * ff_mine.shape[2]
    grad_gate, grad_up, grad_down = small_call(
        join_cores_kernel,
        (ff_mine, after(links.core(ff_send), *sends)),
        [((height, hidden), F32)] * 3,
        place=place,
        cost=2*10**9,
    )

    layer_out = hidden_one + after(y_sum, grad_q).astype(F32)

    return (
        layer_out[None],
        grad_stream[None],
        vectors[0],
        grad_q,
        vectors[2],
        jnp.transpose(grad_k),
        vectors[3],
        jnp.transpose(grad_v),
        vectors[4],
        grad_o,
        vectors[1],
        grad_gate,
        grad_up,
        jnp.transpose(grad_down),
    )


def solution(mesh):
    links = Links(mesh.shape["ctx"], mesh.shape["fsdp"])
    vector, matrix, stream = P(BOTH), P(BOTH, None), P("fsdp", "ctx", None)
    grid = P("fsdp", "ctx")
    in_specs = (
        stream,
        grid,
        vector,
        matrix,
        vector,
        matrix,
        vector,
        matrix,
        vector,
        matrix,
        vector,
        matrix,
        matrix,
        P(None, BOTH),
        stream,
    )
    out_specs = (
        stream,
        stream,
        vector,
        grid,
        vector,
        grid,
        vector,
        grid,
        vector,
        grid,
        vector,
        grid,
        grid,
        P("ctx", "fsdp"),
    )

    def run(*arrays):
        plane_of_four = mesh.shape["fsdp"] == 8 and arrays[3].shape[0] % 16 == 0
        form = per_device_plane_of_four if plane_of_four else per_device_any_mesh
        return form(*arrays, links=links)

    return jax.shard_map(run, mesh=mesh, in_specs=in_specs, out_specs=out_specs, check_vma=False)
```

```python
import jax
import jax.numpy as jnp
from jax import lax
from jax.experimental import pallas as pl
from jax.experimental.pallas import tpu as pltpu
from jax.sharding import PartitionSpec as P

QUERY_HEADS = 12
KEY_VALUE_HEADS = 2
HEAD_SIZE = 128
GROUP = QUERY_HEADS // KEY_VALUE_HEADS
KV_WIDTH = KEY_VALUE_HEADS * HEAD_SIZE
EPSILON = 1e-06
BACK_COST = 8 * 10**9
BOTH = ("ctx", "fsdp")
F32 = jnp.float32
BF16 = jnp.bfloat16


def dot(a, b, dims):
    return lax.dot_general(a, b, ((dims[:1], dims[1:]), ((), ())), preferred_element_type=F32)


def nn(a, b):
    return dot(a, b, (1, 0))


def nt(a, b):
    return dot(a, b, (1, 1))


def tn(a, b):
    return dot(a, b, (0, 0))


def rms_scale(matrix):
    return lax.rsqrt(jnp.mean(matrix * matrix, axis=-1, keepdims=True) + EPSILON)


def angle_tables(positions):
    step_index = jnp.arange(HEAD_SIZE // 2, dtype=F32) * 2.0
    frequency = 10000.0 ** (-step_index / HEAD_SIZE)
    angles = positions.astype(F32)[:, None] * frequency[None, :]
    return jnp.cos(angles)[:, None, :], jnp.sin(angles)[:, None, :]


def rotate(matrix, cosine, sine):
    rows = matrix.shape[0]
    heads = matrix.reshape(rows, -1, HEAD_SIZE)
    a, b = heads[..., : HEAD_SIZE // 2], heads[..., HEAD_SIZE // 2 :]
    turned = jnp.concatenate([a * cosine - b * sine, b * cosine + a * sine], axis=-1)
    return turned.reshape(rows, -1)


def pick(stacked, index):
    return lax.dynamic_index_in_dim(stacked, index, 0, keepdims=False)


class Links:
    def __init__(self, ctx_size, fsdp_size):
        self.ctx_size, self.fsdp_size = ctx_size, fsdp_size
        self.label = "move"
        self.planes = [m for m in (2, 4, 8, 16, 32, 64) if m < fsdp_size]

    def send(self, x, target):
        pairs = []
        for c in range(self.ctx_size):
            for f in range(self.fsdp_size):
                to = target(c, f)
                if to is not None:
                    pairs.append((c * self.fsdp_size + f, to[0] * self.fsdp_size + to[1]))
        with jax.named_scope(self.label):
            return lax.ppermute(x, BOTH, pairs)

    def core(self, x):
        return self.send(x, lambda c, f: (c, f ^ 1))

    def plane(self, x, mask):
        return self.send(x, lambda c, f: (c, f ^ mask))

    def turn(self, x, step):
        return self.send(x, lambda c, f: ((c + step) % self.ctx_size, f))

    def shift(self, x, step):
        return self.send(
            x, lambda c, f: (c + step, f) if 0 <= c + step < self.ctx_size else None
        )


def plane_gather(links, shard):
    first, second, *rest = links.planes
    half = shard.shape[0] // 2
    a = links.plane(shard, first)
    b = links.plane(shard, second)
    low = links.plane(b[:half], first)
    high = links.plane(a[half:], second)
    pieces = {0: shard, first: a, second: b, first | second: jnp.concatenate([low, high])}
    for mask in rest:
        pieces.update({had | mask: links.plane(piece, mask) for had, piece in pieces.items()})
    return pieces


def ff_weight(links, ctx, chip, core, shard):
    ctx_size = links.ctx_size
    rows, hidden = shard.shape
    block = hidden // (2 * ctx_size)
    parts = jnp.transpose(shard.reshape(rows, ctx_size, 2, block), (2, 1, 0, 3))
    mine, other = pick(parts, core), pick(parts, 1 - core)
    got = links.core(other)
    even = core == 0
    pairs = jnp.stack([jnp.where(even, mine, got), jnp.where(even, got, mine)], axis=1)
    by_source = jnp.zeros_like(pairs)
    by_source = lax.dynamic_update_index_in_dim(by_source, pick(pairs, ctx), ctx, 0)
    for step in range(1, ctx_size):
        piece = links.turn(pick(pairs, (ctx + step) % ctx_size), step)
        by_source = lax.dynamic_update_index_in_dim(by_source, piece, (ctx - step) % ctx_size, 0)
    pieces = plane_gather(links, by_source)
    whole = jnp.zeros((ctx_size, links.fsdp_size // 2, 2, rows, block), shard.dtype)
    for mask, piece in pieces.items():
        whole = lax.dynamic_update_index_in_dim(whole, piece, chip ^ (mask // 2), 1)
    return whole.reshape(-1, block)


def spread_tokens(links, x):
    row = jnp.concatenate([x] + [links.turn(x, step) for step in range(1, links.ctx_size)])
    return jnp.concatenate([row, links.core(row)])


def collect_tokens(links, partial):
    rows = partial.shape[0] // 2
    got = links.core(partial[rows:].astype(BF16))
    count = rows // links.ctx_size
    row = (partial[:rows].astype(F32) + got.astype(F32)).reshape(links.ctx_size, count, -1)
    total = row[0]
    for step in range(1, links.ctx_size):
        total = total + links.turn(row[step].astype(BF16), -step).astype(F32)
    return total


def per_device_any_mesh(
    tokens,
    positions,
    norm1_gain,
    q_weight,
    q_bias,
    key_projection,
    key_bias_vector,
    value_projection,
    value_bias_vector,
    o_weight,
    norm2_gain,
    gate_weight,
    up_weight,
    down_weight,
    cotangent,
    *,
    links,
):
    ctx_size, fsdp_size = links.ctx_size, links.fsdp_size
    ctx, row_index = lax.axis_index("ctx"), lax.axis_index("fsdp")
    chip, core = row_index // 2, row_index % 2
    count, width = tokens.shape[1:]
    scale = HEAD_SIZE ** (-0.5)
    even = core == 0

    shard_rows = q_weight.shape[0]

    def column(x):
        return jnp.pad(x, (0, shard_rows - x.shape[0]))[:, None]

    kv_bias_rows = key_bias_vector.shape[0]
    extra = jnp.concatenate(
        [
            column(x)
            for x in (norm1_gain, q_bias, norm2_gain, key_bias_vector, value_bias_vector)
        ],
        axis=1,
    )
    extra = jnp.pad(extra, ((0, 0), (0, 128 - extra.shape[1])))
    packed = jnp.concatenate([q_weight, key_projection, value_projection, extra], axis=1)
    packed = lax.all_gather(packed, BOTH, axis=0, tiled=True)
    weight_o = lax.all_gather(o_weight, BOTH, axis=0, tiled=True)

    weight_gate = ff_weight(links, ctx, chip, core, gate_weight)
    weight_up = ff_weight(links, ctx, chip, core, up_weight)
    weight_down = ff_weight(links, ctx, chip, core, jnp.transpose(down_weight))

    qkv_width = width + 2 * KV_WIDTH
    weight_qkv = packed[:, :qkv_width]
    small = jnp.transpose(packed[:, qkv_width:])[:5].astype(F32)
    gain_one, bias_q, gain_two = small[0:1], small[1:2], small[2:3]

    def bias_of(row):
        return row.reshape(-1, shard_rows)[:, :kv_bias_rows].reshape(1, -1)

    bias_k, bias_v = bias_of(small[3]), bias_of(small[4])
    out_low = cotangent[0]
    group_out = spread_tokens(links, out_low)

    stream = tokens[0].astype(F32)
    scale_one = rms_scale(stream)
    unit_one = stream * scale_one
    normed_one = (unit_one * gain_one).astype(BF16)
    cosine, sine = angle_tables(positions[0])
    linear = nn(normed_one, weight_qkv)
    query = rotate(linear[:, :width] + bias_q, cosine, sine).astype(BF16)
    key = rotate(linear[:, width : width + KV_WIDTH] + bias_k, cosine, sine).astype(BF16)
    value = (linear[:, width + KV_WIDTH :] + bias_v).astype(BF16)
    pairs = jnp.concatenate([key, value], axis=1)
    row_pairs = jnp.concatenate(
        [pairs] + [links.shift(pairs, step) for step in range(1, ctx_size)]
    )
    keys = row_pairs[:, :KV_WIDTH].reshape(-1, KEY_VALUE_HEADS, HEAD_SIZE)
    values = row_pairs[:, KV_WIDTH:].reshape(-1, KEY_VALUE_HEADS, HEAD_SIZE)
    local_index = jnp.arange(count)
    key_index = jnp.concatenate(
        [(ctx - step) * count + local_index for step in range(ctx_size)]
    )
    query_index = ctx * count + local_index
    doc_start = query_index - positions[0]
    allowed = (key_index[None, :] >= doc_start[:, None]) & (
        key_index[None, :] <= query_index[:, None]
    )
    query_heads = query.reshape(count, KEY_VALUE_HEADS, GROUP, HEAD_SIZE)
    scores = jnp.einsum("qkgd,rkd->kgqr", query_heads, keys, preferred_element_type=F32) * scale
    scores = jnp.where(allowed, scores, -1e30)
    top = jnp.max(scores, axis=-1, keepdims=True)
    weights = jnp.where(allowed, jnp.exp(scores - top), 0.0)
    probs = weights / jnp.sum(weights, axis=-1, keepdims=True)
    probs_low = probs.astype(BF16)
    mixed = jnp.einsum("kgqr,rkd->qkgd", probs_low, values, preferred_element_type=F32)
    mixed_low = mixed.reshape(count, -1).astype(BF16)
    hidden_one = stream + nn(mixed_low, weight_o)

    scale_two = rms_scale(hidden_one)
    unit_two = hidden_one * scale_two
    normed_two = (unit_two * gain_two).astype(BF16)
    group_normed = spread_tokens(links, normed_two)
    gate_pre = nn(group_normed, weight_gate)
    up_pre = nn(group_normed, weight_up)
    grad_act = nn(group_out, weight_down)
    sigmoid_gate = jax.nn.sigmoid(gate_pre)
    activated = (gate_pre * sigmoid_gate * up_pre).astype(BF16)
    grad_gate_low = (
        grad_act * up_pre * sigmoid_gate * (1.0 + gate_pre * (1.0 - sigmoid_gate))
    ).astype(BF16)
    grad_up_low = (grad_act * gate_pre * sigmoid_gate).astype(BF16)
    grad_normed_two = collect_tokens(
        links, nt(grad_gate_low, weight_gate) + nt(grad_up_low, weight_up)
    )
    layer_out = hidden_one + collect_tokens(links, nt(activated, weight_down))

    planes = [
        [c * fsdp_size + 2 * p + k for p in range(fsdp_size // 2)]
        for c in range(ctx_size)
        for k in range(2)
    ]

    def ff_grad(left, right):
        term = tn(left, right).astype(BF16)
        part = lax.psum_scatter(
            term, BOTH, scatter_dimension=0, tiled=True, axis_index_groups=planes
        )
        part = part.reshape(2, -1, part.shape[1])
        mine, got = pick(part, core), links.core(pick(part, 1 - core))
        return jnp.concatenate(
            [jnp.where(even, mine, got), jnp.where(even, got, mine)], axis=1
        ).astype(F32)

    grad_gate = ff_grad(group_normed, grad_gate_low)
    grad_up = ff_grad(group_normed, grad_up_low)
    grad_down = jnp.transpose(ff_grad(group_out, activated))

    grad_gain_two = jnp.sum(grad_normed_two * unit_two, axis=0)
    weighted_two = grad_normed_two * gain_two
    grad_hidden = out_low.astype(F32) + scale_two * (
        weighted_two - unit_two * jnp.mean(weighted_two * unit_two, axis=-1, keepdims=True)
    )

    grad_hidden_low = grad_hidden.astype(BF16)
    grad_mixed = nt(grad_hidden_low, weight_o).astype(BF16)
    grad_mixed = grad_mixed.reshape(count, KEY_VALUE_HEADS, GROUP, HEAD_SIZE)
    grad_probs = jnp.einsum("qkgd,rkd->kgqr", grad_mixed, values, preferred_element_type=F32)
    delta = jnp.sum(probs * grad_probs, axis=-1, keepdims=True)
    grad_scores = (probs * (grad_probs - delta)).astype(BF16)
    grad_query = jnp.einsum("kgqr,rkd->qkgd", grad_scores, keys, preferred_element_type=F32)
    grad_key = (
        jnp.einsum("kgqr,qkgd->rkd", grad_scores, query_heads, preferred_element_type=F32) * scale
    )
    grad_value = jnp.einsum("kgqr,qkgd->rkd", probs_low, grad_mixed, preferred_element_type=F32)
    pair_terms = jnp.concatenate(
        [grad_key.reshape(-1, KV_WIDTH), grad_value.reshape(-1, KV_WIDTH)], axis=1
    ).reshape(ctx_size, count, -1)
    pair_grads = pair_terms[0]
    for step in range(1, ctx_size):
        pair_grads = pair_grads + links.shift(pair_terms[step].astype(BF16), -step).astype(F32)
    grad_q_low = rotate(grad_query.reshape(count, -1) * scale, cosine, -sine).astype(BF16)
    grad_k_low = rotate(pair_grads[:, :KV_WIDTH], cosine, -sine).astype(BF16)
    grad_v_low = pair_grads[:, KV_WIDTH:].astype(BF16)
    grad_qkv = jnp.concatenate([grad_q_low, grad_k_low, grad_v_low], axis=1)
    grad_normed_one = nt(grad_qkv, weight_qkv)
    grad_gain_one = jnp.sum(grad_normed_one * unit_one, axis=0)
    weighted_one = grad_normed_one * gain_one
    grad_stream = grad_hidden + scale_one * (
        weighted_one - unit_one * jnp.mean(weighted_one * unit_one, axis=-1, keepdims=True)
    )

    def columns_over_ctx(arrays):
        parts = jnp.concatenate([x.reshape(count, ctx_size, -1) for x in arrays], axis=2)
        parts = jnp.transpose(parts, (1, 0, 2))
        whole = jnp.zeros_like(parts)
        whole = lax.dynamic_update_index_in_dim(whole, pick(parts, ctx), ctx, 0)
        for step in range(1, ctx_size):
            piece = links.turn(pick(parts, (ctx + step) % ctx_size), step)
            whole = lax.dynamic_update_index_in_dim(whole, piece, (ctx - step) % ctx_size, 0)
        return whole.reshape(ctx_size * count, -1)

    def attention_grad(rows, arrays):
        left = lax.all_gather(rows, "ctx", axis=0, tiled=True)
        term = tn(left, columns_over_ctx(arrays)).astype(BF16)
        return lax.psum_scatter(term, "fsdp", scatter_dimension=0, tiled=True).astype(F32)

    grad_o = attention_grad(mixed_low, [grad_hidden_low])
    grad_packed = attention_grad(normed_one, [grad_q_low, grad_k_low, grad_v_low])
    q_columns, kv_columns = width // ctx_size, KV_WIDTH // ctx_size

    sums = jnp.concatenate(
        [grad_gain_one, grad_gain_two, jnp.sum(grad_qkv.astype(F32), axis=0)]
    )
    sums = lax.psum(sums, BOTH)
    device = ctx * fsdp_size + row_index

    def own(start, size):
        part = size // (ctx_size * fsdp_size)
        return lax.dynamic_slice_in_dim(sums, start + device * part, part)

    return (
        layer_out[None],
        grad_stream[None],
        own(0, width),
        grad_packed[:, :q_columns],
        own(2 * width, width),
        grad_packed[:, q_columns : q_columns + kv_columns],
        own(3 * width, KV_WIDTH),
        grad_packed[:, q_columns + kv_columns :],
        own(3 * width + KV_WIDTH, KV_WIDTH),
        grad_o,
        own(width, width),
        grad_gate,
        grad_up,
        grad_down,
    )


def after(x, *others):
    return lax.optimization_barrier((x, *others))[0]


def phase(*groups):
    flat = lax.optimization_barrier(tuple(x for group in groups for x in group))
    out = []
    for group in groups:
        out.append(list(flat[: len(group)]))
        flat = flat[len(group) :]
    return out


def plane_start(links, shard):
    return links.plane(shard, 2), links.plane(shard, 4)


def plane_end(links, shard, a, b):
    half = shard.shape[0] // 2
    return shard, a, b, links.plane(b[:half], 2), links.plane(a[half:], 4)


def load_pieces(layout, sizes, place, pieces, which, weight, semaphore):
    ctx_size, chips, rows = sizes
    for (entries, mask, _), piece in zip(layout, pieces):
        for i, (step, core) in enumerate(entries):
            source = lax.rem(place[0] - step + ctx_size, ctx_size)
            start = ((source * chips + (place[1] ^ mask)) * 2 + core) * rows
            pltpu.make_async_copy(
                piece.at[i, which],
                weight.at[pl.ds(pl.multiple_of(start, rows), rows)],
                semaphore,
            ).start()


def ff_kernel(layout, sizes, place, normed, out_grad, *refs):
    pieces, refs = refs[: len(layout)], refs[len(layout) :]
    act_ref, gate_ref, up_ref, down_ref, weights, semaphores = refs

    @pl.when(pl.program_id(0) == 0)
    def _():
        for which in range(3):
            load_pieces(
                layout, sizes, place, pieces, which, weights.at[which], semaphores.at[which]
            )

    def arrived(which):
        @pl.when(pl.program_id(0) == 0)
        def _():
            wait_all(weights.at[which], semaphores.at[which])

    x, gy = normed[...], out_grad[...]
    arrived(0)
    gate = nn(x, weights[0])
    arrived(1)
    up = nn(x, weights[1])
    arrived(2)
    grad = nn(gy, weights[2])
    sigmoid = 1.0 / (1.0 + jnp.exp(-gate))
    silu = gate * sigmoid
    grad_gate = (grad * up * sigmoid * (1.0 + gate * (1.0 - sigmoid))).astype(BF16)
    grad_up = (grad * silu).astype(BF16)
    act_ref[...] = (silu * up).astype(BF16)
    gate_ref[...] = grad_gate
    up_ref[...] = grad_up
    down_ref[...] = (nt(grad_gate, weights[0]) + nt(grad_up, weights[1])).astype(BF16)


def y_kernel(layout, sizes, place, act_a, act_b, *refs):
    pieces, (y_a, y_b, weight, semaphore) = refs[: len(layout)], refs[len(layout) :]

    @pl.when(pl.program_id(0) == 0)
    def _():
        load_pieces(layout, sizes, place, pieces, 2, weight, semaphore)
        wait_all(weight, semaphore)

    y_a[...] = nt(act_a[...], weight[...]).astype(BF16)
    y_b[...] = nt(act_b[...], weight[...]).astype(BF16)


def ff_call(links, kernel, layout, place, arrays, widths, matrices):
    tokens = arrays[0].shape[0]
    rows, block = layout[0][2].shape[2:]
    sizes = (links.ctx_size, links.fsdp_size // 2, rows)
    depth = 2 * sizes[0] * sizes[1] * rows
    tile = 256

    def spec(size):
        return pl.BlockSpec((tile, size), lambda i, place: (i, 0))

    def body(*refs):
        kernel(layout, sizes, *refs)

    if matrices == 1:
        scratch = [pltpu.VMEM((depth, block), BF16), pltpu.SemaphoreType.DMA]
    else:
        scratch = [
            pltpu.VMEM((matrices, depth, block), BF16),
            pltpu.SemaphoreType.DMA((matrices,)),
        ]
    return pl.pallas_call(
        body,
        grid_spec=pltpu.PrefetchScalarGridSpec(
            num_scalar_prefetch=1,
            grid=(tokens // tile,),
            in_specs=[spec(x.shape[1]) for x in arrays]
            + [pl.BlockSpec(memory_space=pl.ANY)] * len(layout),
            out_specs=[spec(x) for x in widths],
            scratch_shapes=scratch,
        ),
        out_shape=[jax.ShapeDtypeStruct((tokens, x), BF16) for x in widths],
        compiler_params=pltpu.CompilerParams(vmem_limit_bytes=56 * 2**20),
        cost_estimate=pl.CostEstimate(flops=0, bytes_accessed=0, transcendentals=0),
    )(place, *arrays, *[piece for _, _, piece in layout])


def grad_kernel(place, *refs):
    lefts, rights, outs = refs[:8], refs[8:14], refs[14:]
    low, high = outs[: len(outs) // 2], outs[len(outs) // 2 :]
    for which in range(3):
        first = 4 * (which // 2)
        for parts, (left_a, left_b), core in (
            (low, lefts[first : first + 2], 0),
            (high, lefts[first + 2 : first + 4], 1),
        ):
            out, at = (parts[0], which) if len(parts) == 1 else (parts[which > 0], max(which - 1, 0))
            half = left_a.shape[1] // 2
            rows = slice(core * half, (core + 1) * half)
            right_a, right_b = rights[2 * which : 2 * which + 2]
            term = tn(left_a[:, rows], right_a[...]) + tn(left_b[:, rows], right_b[...])
            out[0, at] = term.astype(BF16)


def ff_grad_terms(place, lefts, rights, low_at, high_at, parts):
    tokens, width = lefts[0].shape
    block = rights[0].shape[1]
    part = width // 4

    def left(at):
        return pl.BlockSpec((tokens, part), lambda j, place: (0, place[1] ^ at(j)))

    right = pl.BlockSpec((tokens, block), lambda j, place: (0, 0))
    outs = [pl.BlockSpec((1, n, part // 2, block), lambda j, place: (j, 0, 0, 0)) for n in parts]
    low, high = left(low_at), left(high_at)
    x_a, x_b, y_a, y_b = lefts
    return pl.pallas_call(
        grad_kernel,
        grid_spec=pltpu.PrefetchScalarGridSpec(
            num_scalar_prefetch=1,
            grid=(2,),
            in_specs=[low, low, high, high] * 2 + [right] * 6,
            out_specs=outs * 2,
        ),
        out_shape=[jax.ShapeDtypeStruct((2, n, part // 2, block), BF16) for n in parts] * 2,
        compiler_params=pltpu.CompilerParams(vmem_limit_bytes=56 * 2**20),
        cost_estimate=pl.CostEstimate(flops=0, bytes_accessed=0, transcendentals=0),
    )(place, x_a, x_b, x_a, x_b, y_a, y_b, y_a, y_b, *rights)


def added(a, b):
    return (a.astype(F32) + b.astype(F32)).astype(BF16)


def reduce_start(links, terms):
    return [links.plane(x, mask) for x, mask in zip(terms, (4, 4, 2, 2))]


def add_pairs_kernel(*refs):
    for i, out in enumerate(refs[6:]):
        keep, one, rest = refs[3 * i : 3 * i + 3]
        out[:1] = (keep[0, :1].astype(F32) + one[0].astype(F32)).astype(BF16)
        out[1:] = (keep[0, 1:].astype(F32) + rest[0].astype(F32)).astype(BF16)


def first_specs(index):
    def spec(x):
        return pl.BlockSpec((1, *x.shape[1:]), lambda i, *place: (index, 0, 0, 0))

    return spec


def reduce_next(links, terms, first):
    shape = terms[0].shape
    arrays = (terms[0], first[0], first[1], terms[1], first[2], first[3])
    spec = first_specs(1)
    whole = pl.BlockSpec(shape[1:], lambda i: (0, 0, 0))
    low, high = pl.pallas_call(
        add_pairs_kernel,
        grid=(1,),
        in_specs=[spec(x) for x in arrays],
        out_specs=[whole] * 2,
        out_shape=[jax.ShapeDtypeStruct(shape[1:], BF16)] * 2,
        compiler_params=pltpu.CompilerParams(vmem_limit_bytes=56 * 2**20),
        cost_estimate=pl.CostEstimate(flops=0, bytes_accessed=0, transcendentals=0),
    )(*arrays)
    return links.plane(low, 2), links.plane(high, 4)


def reduce_end_kernel(turned, place, *refs):
    low, high, (out,) = refs[:4], refs[4:8], refs[8:]

    def write(ref, parts):
        keep, one, rest, last = parts
        total = keep[0, :1].astype(F32) + one[0].astype(F32) + last[:1].astype(F32)
        ref[:1] = total.astype(ref.dtype)
        total = keep[0, 1:].astype(F32) + rest[0].astype(F32) + last[1:].astype(F32)
        ref[1:] = total.astype(ref.dtype)

    @pl.when(place[2] == turned)
    def _():
        write(out, low)

    @pl.when(place[2] != turned)
    def _():
        write(out, high)


def reduce_end(place, terms, first, second, turned, dtype, cost):
    shape = terms[0].shape[1:]
    spec = first_specs(0)
    whole = pl.BlockSpec(shape, lambda i, place: (0, 0, 0))
    low = (terms[0], first[0], first[1])
    high = (terms[1], first[2], first[3])
    def body(*refs):
        reduce_end_kernel(turned, *refs)

    return pl.pallas_call(
        body,
        grid_spec=pltpu.PrefetchScalarGridSpec(
            num_scalar_prefetch=1,
            grid=(1,),
            in_specs=[*map(spec, low), whole, *map(spec, high), whole],
            out_specs=whole,
        ),
        out_shape=jax.ShapeDtypeStruct(shape, dtype),
        compiler_params=pltpu.CompilerParams(vmem_limit_bytes=56 * 2**20),
        cost_estimate=pl.CostEstimate(flops=cost, bytes_accessed=0, transcendentals=0),
    )(place, *low, second[0], *high, second[1])


def join_cores_kernel(place, mine, got, gate, up, down):
    def write(even, odd):
        for which, ref in enumerate((gate, up, down)):
            ref[...] = jnp.concatenate([even(which), odd(which)], axis=1)

    def own(which):
        return mine[which]

    def others(which):
        return got[which].astype(F32)

    @pl.when(place[2] == 0)
    def _():
        write(own, others)

    @pl.when(place[2] != 0)
    def _():
        write(others, own)


def split_kernel(place, gate, up, down, mine, other):
    block = mine.shape[3]

    def write(core):
        for which, ref in enumerate((gate, up, down)):
            for target in range(mine.shape[0]):
                start = (2 * target + core) * block
                mine[target, which] = ref[:, start : start + block]
                start = (2 * target + 1 - core) * block
                other[target, which] = ref[:, start : start + block]

    @pl.when(place[2] == 0)
    def _():
        write(0)

    @pl.when(place[2] != 0)
    def _():
        write(1)


def split_hidden(links, place, shards):
    rows, hidden = shards[0].shape
    whole = pl.BlockSpec((rows, hidden), lambda i, place: (0, 0))
    shape = (links.ctx_size, 3, rows, hidden // (2 * links.ctx_size))
    out = pl.BlockSpec(shape, lambda i, place: (0, 0, 0, 0))
    return pl.pallas_call(
        split_kernel,
        grid_spec=pltpu.PrefetchScalarGridSpec(
            num_scalar_prefetch=1, grid=(1,), in_specs=[whole] * 3, out_specs=[out] * 2
        ),
        out_shape=[jax.ShapeDtypeStruct(shape, BF16)] * 2,
        compiler_params=pltpu.CompilerParams(vmem_limit_bytes=32 * 2**20),
    )(place, *shards)


class Rows:
    def __init__(self, sizes, pieces, layout, first, columns):
        self.sizes, self.pieces, self.layout = sizes, pieces, layout
        self.first, self.columns = first, columns
        self.rows = pieces[0].shape[-2]
        self.shape = (2 * sizes[0] * sizes[1] * self.rows, columns)

    def start(self, place, refs, weight, semaphore):
        ctx_size, chips = self.sizes
        for piece, index, step, mask, turned in self.layout:
            source = lax.rem(place[0] - step + ctx_size, ctx_size)
            start = ((source * chips + (place[1] ^ mask)) * 2 + (place[2] ^ turned)) * self.rows
            pltpu.make_async_copy(
                refs[piece].at[(*index, slice(None), pl.ds(self.first, self.columns))],
                weight.at[pl.ds(pl.multiple_of(start, self.rows), self.rows)],
                semaphore,
            ).start()


def rows_layout(ctx_size):
    half = ctx_size // 2
    layout = []
    for step in range(ctx_size):
        layout += [(mask, (step,), step, mask, 0) for mask in range(3)]
        layout.append((3, (step,), step, 3, 0) if step < half else (4, (step - half,), step, 3, 0))
        layout.append((5, (step,), step, 0, 1))
        layout += [(6, (i * ctx_size + step,), step, i + 1, 1) for i in range(3)]
    return layout


def wait_all(weight, semaphore):
    pltpu.make_async_copy(weight, weight, semaphore).wait()


def call(body, place, arrays, weight, out_shapes, cost, scratch=()):
    any_spec = pl.BlockSpec(memory_space=pl.ANY)
    vmem = pl.BlockSpec(memory_space=pltpu.VMEM)
    count, pieces = len(arrays), len(weight.pieces)

    def kernel(place, *refs):
        ins, parts, outs = refs[:count], refs[count : count + pieces], refs[count + pieces : -2]
        whole, semaphore = refs[-2:]
        weight.start(place, parts, whole, semaphore)
        body(place, ins, outs, whole, lambda: wait_all(whole, semaphore))

    return pl.pallas_call(
        kernel,
        in_specs=[pl.BlockSpec(memory_space=pltpu.SMEM)] + [vmem] * count + [any_spec] * pieces,
        out_specs=[vmem] * len(out_shapes),
        out_shape=[jax.ShapeDtypeStruct(shape, dtype) for shape, dtype in out_shapes],
        scratch_shapes=[*scratch, pltpu.VMEM(weight.shape, BF16), pltpu.SemaphoreType.DMA],
        compiler_params=pltpu.CompilerParams(vmem_limit_bytes=56 * 2**20),
        cost_estimate=pl.CostEstimate(flops=cost, bytes_accessed=0, transcendentals=0),
    )(place, *arrays, *weight.pieces)


def turn_halves(x, cosine, sine):
    return x * cosine + pltpu.roll(x, HEAD_SIZE // 2, 1) * sine


def turned_heads(x, cosine, sine):
    heads = [x[:, i : i + HEAD_SIZE] for i in range(0, x.shape[1], HEAD_SIZE)]
    return jnp.concatenate([turn_halves(x, cosine, sine) for x in heads], axis=1)


def qkv_body(shard_rows, place, ins, outs, weight, wait):
    tokens, cosine, sine = ins
    normed_ref, query_ref, pairs_ref, small_ref = outs
    width = tokens.shape[1]
    qkv_width = width + 2 * KV_WIDTH
    x = tokens[...].astype(F32)
    unit = x * rms_scale(x)
    wait()
    small = jnp.transpose(weight[:, qkv_width:].astype(F32))[:8]
    bias_rows = KV_WIDTH * shard_rows // width
    row = lax.broadcasted_iota(jnp.int32, (width, KV_WIDTH), 0)
    at = lax.broadcasted_iota(jnp.int32, (width, KV_WIDTH), 1)
    chosen = row == (at // bias_rows) * shard_rows + at % bias_rows
    kv_bias = nn(small.astype(BF16), chosen.astype(BF16))
    normed = (unit * small[0:1]).astype(BF16)
    normed_ref[...] = normed
    small_ref[...] = small
    linear = nn(normed, weight[:, :qkv_width])
    query = linear[:, :width] + small[1:2]
    key = linear[:, width : width + KV_WIDTH] + kv_bias[3:4]
    query_ref[...] = turned_heads(query, cosine[...], sine[...]).astype(BF16)
    pairs_ref[:, :KV_WIDTH] = turned_heads(key, cosine[...], sine[...]).astype(BF16)
    pairs_ref[:, KV_WIDTH:] = (linear[:, width + KV_WIDTH :] + kv_bias[4:5]).astype(BF16)


def allowed_keys(ctx, positions, blocks):
    count = positions.shape[0]
    shape = (count, blocks * count)
    column = lax.broadcasted_iota(jnp.int32, shape, 1)
    query = ctx * count + lax.broadcasted_iota(jnp.int32, shape, 0)
    key = (ctx - column // count) * count + column % count
    return (key >= query - positions) & (key <= query)


def heads_of(x, group):
    first = group * GROUP
    return jnp.concatenate(
        [x[:, i * HEAD_SIZE : (i + 1) * HEAD_SIZE] for i in range(first, first + GROUP)], axis=0
    )


def softmax_of(query, keys, allowed):
    scores = nt(query, keys) * HEAD_SIZE ** (-0.5)
    scores = jnp.where(allowed, scores, -1e30)
    weights = jnp.exp(scores - jnp.max(scores, axis=-1, keepdims=True))
    weights = jnp.where(allowed, weights, 0.0)
    return weights / jnp.sum(weights, axis=-1, keepdims=True)


def group_pairs(blocks, group):
    def columns(start):
        return jnp.concatenate([b[:, start : start + HEAD_SIZE] for b in blocks], axis=0)

    return columns(group * HEAD_SIZE), columns(KV_WIDTH + group * HEAD_SIZE)


def mix_body(place, ins, outs, weight, wait):
    tokens, small, positions, query, *blocks = ins
    mixed_ref, hidden_ref, normed_ref = outs
    count = tokens.shape[0]
    allowed = allowed_keys(place[0], positions[...], len(blocks))
    allowed = jnp.concatenate([allowed.astype(F32)] * GROUP, axis=0) > 0
    for group in range(KEY_VALUE_HEADS):
        keys, values = group_pairs(blocks, group)
        probs = softmax_of(heads_of(query, group), keys, allowed)
        mixed = nn(probs.astype(BF16), values).astype(BF16)
        for h in range(GROUP):
            start = (group * GROUP + h) * HEAD_SIZE
            mixed_ref[:, start : start + HEAD_SIZE] = mixed[h * count : (h + 1) * count]
    wait()
    hidden = tokens[...].astype(F32) + nn(mixed_ref[...], weight[...])
    hidden_ref[...] = hidden
    normed_ref[...] = (hidden * rms_scale(hidden) * small[2:3]).astype(BF16)


def norm_back(unit, scale, grad, gain):
    weighted = grad * gain
    return scale * (weighted - unit * jnp.mean(weighted * unit, axis=-1, keepdims=True))


def mix_back_body(steps, place, ins, outs, weight, wait):
    terms, ins = ins[:steps], ins[steps:]
    hidden_ref, small, out_grad, positions, query, cosine, sine, *blocks = ins
    grad_hidden_ref, low_ref, grad_query_ref, gain_ref, *pair_refs = outs
    count = hidden_ref.shape[0]
    hidden = hidden_ref[...]
    scale = rms_scale(hidden)
    unit = hidden * scale
    grad = terms[0][...].astype(F32)
    for term in terms[1:]:
        grad = grad + term[...].astype(F32)
    gain_ref[...] = jnp.sum(grad * unit, axis=0, keepdims=True)
    grad_hidden = out_grad[...].astype(F32) + norm_back(unit, scale, grad, small[2:3])
    grad_hidden_ref[...] = grad_hidden
    low = grad_hidden.astype(BF16)
    low_ref[...] = low
    wait()
    grad_mixed = nt(low, weight[...]).astype(BF16)
    allowed = allowed_keys(place[0], positions[...], len(blocks))
    allowed = jnp.concatenate([allowed.astype(F32)] * GROUP, axis=0) > 0
    score_scale = HEAD_SIZE ** (-0.5)
    for group in range(KEY_VALUE_HEADS):
        keys, values = group_pairs(blocks, group)
        queries, grads = heads_of(query, group), heads_of(grad_mixed, group)
        probs = softmax_of(queries, keys, allowed)
        grad_probs = nt(grads, values)
        delta = jnp.sum(probs * grad_probs, axis=-1, keepdims=True)
        grad_scores = (probs * (grad_probs - delta)).astype(BF16)
        grad_query = nn(grad_scores, keys) * score_scale
        for h in range(GROUP):
            start = (group * GROUP + h) * HEAD_SIZE
            grad_query_ref[:, start : start + HEAD_SIZE] = turn_halves(
                grad_query[h * count : (h + 1) * count], cosine[...], -sine[...]
            ).astype(BF16)
        grad_key = (tn(grad_scores, queries) * score_scale).astype(BF16)
        grad_value = tn(probs.astype(BF16), grads).astype(BF16)
        start = group * HEAD_SIZE
        for block, ref in enumerate(pair_refs):
            rows = slice(block * count, (block + 1) * count)
            ref[:, start : start + HEAD_SIZE] = grad_key[rows]
            ref[:, KV_WIDTH + start : KV_WIDTH + start + HEAD_SIZE] = grad_value[rows]


def qkv_back_body(steps, place, ins, outs, weight, wait):
    terms, ins = ins[:steps], ins[steps:]
    tokens, small, cosine, sine, grad_query, grad_hidden, grad_hidden_low, gain_two = ins
    stream_ref, *share_refs, share_ref = outs
    count, width = tokens.shape
    pairs = terms[0][...].astype(F32)
    for term in terms[1:]:
        pairs = pairs + term[...].astype(F32)
    grad_key = turned_heads(pairs[:, :KV_WIDTH], cosine[...], -sine[...]).astype(BF16)
    grad_value = pairs[:, KV_WIDTH:].astype(BF16)
    wait()
    kv_end = width + KV_WIDTH
    grad = (
        nt(grad_query[...], weight[:, :width])
        + nt(grad_key, weight[:, width:kv_end])
        + nt(grad_value, weight[:, kv_end : kv_end + KV_WIDTH])
    )
    x = tokens[...].astype(F32)
    scale = rms_scale(x)
    unit = x * scale
    stream_ref[...] = grad_hidden[...] + norm_back(unit, scale, grad, small[0:1])
    gains = jnp.concatenate([jnp.sum(grad * unit, axis=0, keepdims=True), gain_two[...]], axis=0)
    gains = jnp.concatenate([gains, jnp.zeros((14, width), F32)], axis=0).astype(BF16)
    targets = share_ref.shape[0]
    q_columns, kv_columns = width // targets, KV_WIDTH // targets
    for target in range(targets):
        q, kv = target * q_columns, target * kv_columns
        share_ref[target, :count, :q_columns] = grad_query[:, q : q + q_columns]
        kv_end = q_columns + 2 * kv_columns
        share_ref[target, :count, q_columns:kv_end] = jnp.concatenate(
            [grad_key[:, kv : kv + kv_columns], grad_value[:, kv : kv + kv_columns]], axis=1
        )
        share_ref[target, :count, kv_end:] = grad_hidden_low[:, q : q + q_columns]
        share_ref[target, count:, :q_columns] = gains[:, q : q + q_columns]
        share_ref[target, count:, q_columns:] = jnp.zeros(
            (16, share_ref.shape[2] - q_columns), BF16
        )
    for step, ref in enumerate(share_refs):
        ref[...] = share_ref[lax.rem(place[0] + step, targets)]


def term_kernel(place, *refs):
    *shares, normed_rows, mixed_rows, mine, other, share, terms, vectors = refs
    ctx_size, width = len(shares), normed_rows.shape[1]
    count = normed_rows.shape[0] // ctx_size
    chips, height = mine.shape[0], mine.shape[1] - 16
    devices = 2 * chips
    q_columns, kv_columns = width // ctx_size, KV_WIDTH // ctx_size
    kv_end = q_columns + 2 * kv_columns
    gains = jnp.zeros((16, q_columns), F32)
    for step, ref in enumerate(shares):
        source = lax.rem(place[0] - step + ctx_size, ctx_size)
        share[pl.ds(pl.multiple_of(source * count, count), count)] = ref[:count]
        gains = gains + ref[count:, :q_columns].astype(F32)
    terms[:, :kv_end] = tn(normed_rows[...], share[:, :kv_end])
    terms[:, kv_end:] = tn(mixed_rows[...], share[:, kv_end:])
    biases = jnp.sum(share[:, :kv_end].astype(F32), axis=0, keepdims=True)
    vectors[...] = jnp.zeros_like(vectors)
    parts = (gains[0:1], gains[1:2], biases[:, :q_columns])
    parts += (biases[:, q_columns : q_columns + kv_columns], biases[:, q_columns + kv_columns :])
    for f in range(devices):
        start = 0
        for part in parts:
            size = part.shape[1] // devices
            vectors[f : f + 1, start : start + size] = part[:, f * size : (f + 1) * size]
            start += size
    first = lax.broadcasted_iota(jnp.int32, (16, terms.shape[1]), 0) == 0
    for ref, core in ((mine, place[2]), (other, 1 - place[2])):
        for mask in range(chips):
            f = (place[1] ^ mask) * 2 + core
            start = pl.multiple_of(f * height, 64)
            ref[mask, :height] = terms[pl.ds(start, height)].astype(BF16)
            row = jnp.broadcast_to(vectors[pl.ds(f, 1)], first.shape)
            ref[mask, height:] = jnp.where(first, row, 0.0).astype(BF16)


def sum_cores_kernel(mine, got, keep, *sends):
    keep[...] = mine[0].astype(F32) + got[0].astype(F32)
    for mask, ref in enumerate(sends, 1):
        ref[...] = (mine[mask].astype(F32) + got[mask].astype(F32)).astype(BF16)


def sum_plane_kernel(keep, *refs):
    got, outs = refs[:3], refs[3:]
    total = keep[...] + got[0][...].astype(F32) + got[1][...].astype(F32) + got[2][...].astype(F32)
    height = total.shape[0] - 16
    start = 0
    for ref, turned in zip(outs[:4], (False, True, True, False)):
        size = ref.shape[0] if turned else ref.shape[1]
        part = total[:height, start : start + size]
        ref[...] = jnp.transpose(part) if turned else part
        start += size
    start = 0
    for ref in outs[4:]:
        ref[...] = total[height : height + 1, start : start + ref.shape[1]]
        start += ref.shape[1]


def small_call(body, arrays, out_shapes, scratch=(), place=None, cost=0):
    vmem = pl.BlockSpec(memory_space=pltpu.VMEM)
    smem = [] if place is None else [place]
    return pl.pallas_call(
        body,
        in_specs=[pl.BlockSpec(memory_space=pltpu.SMEM)] * len(smem) + [vmem] * len(arrays),
        out_specs=[vmem] * len(out_shapes),
        out_shape=[jax.ShapeDtypeStruct(shape, dtype) for shape, dtype in out_shapes],
        scratch_shapes=list(scratch),
        compiler_params=pltpu.CompilerParams(vmem_limit_bytes=56 * 2**20),
        cost_estimate=pl.CostEstimate(flops=cost, bytes_accessed=0, transcendentals=0),
    )(*smem, *arrays)


def per_device_plane_of_four(
    tokens,
    positions,
    norm1_gain,
    q_weight,
    q_bias,
    key_projection,
    key_bias_vector,
    value_projection,
    value_bias_vector,
    o_weight,
    norm2_gain,
    gate_weight,
    up_weight,
    down_weight,
    cotangent,
    *,
    links,
):
    ctx_size, fsdp_size = links.ctx_size, links.fsdp_size
    ctx, row_index = lax.axis_index("ctx"), lax.axis_index("fsdp")
    chip, core = row_index // 2, row_index % 2
    place = jnp.stack([ctx, chip, core])
    count, width = tokens.shape[1:]
    shard_rows = q_weight.shape[0]
    even = core == 0
    steps = range(1, ctx_size)

    def column(x):
        return jnp.pad(x, (0, shard_rows - x.shape[0]))[:, None]

    extra = jnp.concatenate(
        [
            column(x)
            for x in (norm1_gain, q_bias, norm2_gain, key_bias_vector, value_bias_vector)
        ],
        axis=1,
    )
    extra = jnp.pad(extra, ((0, 0), (0, 128 - extra.shape[1])))
    packed = jnp.concatenate([q_weight, key_projection, value_projection, extra, o_weight], axis=1)
    links.label = "qkvo_ctx"
    packed_got = [links.turn(packed, step) for step in steps]

    mine, other = split_hidden(
        links, place, (gate_weight, up_weight, jnp.transpose(down_weight))
    )
    links.label = "ff_core"
    got = links.core(other)

    def for_ctx(step):
        target = (ctx + step) % ctx_size
        a, b = pick(mine, target), pick(got, target)
        return jnp.stack([jnp.where(even, a, b), jnp.where(even, b, a)])

    packed_got, (mine, got) = phase(packed_got, (mine, got))
    packed_mine = jnp.stack([packed] + packed_got)
    links.label = "qkvo_plane1"
    packed_stage = plane_start(links, packed_mine)
    links.label = "ff_ctx_a"
    near_steps, far_steps = (1, ctx_size - 1), tuple(range(2, ctx_size - 1))
    near = [links.turn(for_ctx(step), step) for step in near_steps]
    far = [for_ctx(step) for step in far_steps]
    links.label = "qkvo_core"
    packed_stage, near, far, (own_piece, early) = phase(
        packed_stage, near, far, (for_ctx(0), links.core(packed_mine))
    )
    links.label = "ff_ctx_b"
    far = [links.turn(piece, step) for step, piece in zip(far_steps, far)]
    links.label = "qkvo_plane2"
    packed_parts = plane_end(links, packed_mine, *packed_stage)
    links.label = "ff_own1"
    own_stage = plane_start(links, own_piece)
    near, far, late, own_stage = phase(near, far, packed_parts[3:], own_stage)
    links.label = "qkvo_core"
    pieces = [*packed_parts[:3], *late, early]
    pieces.append(links.core(jnp.concatenate([*packed_parts[1:3], *late])))
    sizes, qkv_columns = (ctx_size, fsdp_size // 2), packed.shape[1] - width
    weight_qkv = Rows(sizes, pieces, rows_layout(ctx_size), 0, qkv_columns)
    weight_o = Rows(sizes, pieces, rows_layout(ctx_size), qkv_columns, width)
    links.label = "ff_plane1"
    moved = dict(zip(near_steps + far_steps, near + far))
    moved_piece = jnp.concatenate([moved[step] for step in steps])
    moved_stage = plane_start(links, moved_piece)

    low_tokens, out_low = tokens[0], cotangent[0]
    cosine, sine = (x[:, 0] for x in angle_tables(positions[0]))
    cosine = jnp.concatenate([cosine, cosine], axis=1)
    sine = jnp.concatenate([-sine, sine], axis=1)
    place_column = positions[0][:, None]
    wide, narrow = (count, width), (count, 2 * KV_WIDTH)

    def qkv(*refs):
        qkv_body(shard_rows, *refs)

    normed_one, query, pairs, small = call(
        qkv,
        place,
        (low_tokens, cosine, sine),
        weight_qkv,
        [(wide, BF16), (wide, BF16), (narrow, BF16), ((8, width), F32)],
        0,
    )
    links.label = "kv"
    blocks = [pairs] + [links.shift(pairs, step) for step in steps]
    mixed_low, hidden_one, normed_two = call(
        mix_body,
        place,
        (low_tokens, small, place_column, query, *blocks),
        weight_o,
        [(wide, BF16), (wide, F32), (wide, BF16)],
        0,
    )

    out_row = lax.all_gather(after(out_low, *far), "ctx", axis=0, tiled=True)
    normed_row = lax.all_gather(normed_two, "ctx", axis=0, tiled=True)
    links.label = "gy_core"
    out_other = links.core(out_row)
    links.label = "ff_plane2"
    half = ctx_size - 1
    last = [
        links.plane(jnp.concatenate([moved_stage[1][:half], own_stage[1][:1]]), 2),
        links.plane(jnp.concatenate([moved_stage[0][half:], own_stage[0][1:]]), 4),
    ]
    own_entries = [(0, 0), (0, 1)]
    entries = [(step, core) for step in steps for core in range(2)]
    layout = [(own_entries, mask, x) for mask, x in enumerate((own_piece, *own_stage))]
    layout += [(entries, mask, x) for mask, x in enumerate((moved_piece, *moved_stage))]
    layout += [
        (entries[:half] + own_entries[:1], 3, last[0]),
        (entries[half:] + own_entries[1:], 3, last[1]),
    ]
    links.label = "n2_core"
    normed_other = links.core(after(normed_row, *last, out_other))
    block = own_piece.shape[3]
    ff_widths = (block, block, block, width)
    act_a, gate_a, up_a, down_a = ff_call(
        links, ff_kernel, layout, place, (normed_row, out_row), ff_widths, 3
    )
    normed_other = after(normed_other, act_a)
    act_b, gate_b, up_b, down_b = ff_call(
        links, ff_kernel, layout, place, (normed_other, out_other), ff_widths, 3
    )
    links.label = "gn2_core"
    down_got = links.core(down_b)
    normed_rows = lax.all_gather(after(normed_one, normed_row), "ctx", axis=0, tiled=True)
    grad_normed_two = lax.psum_scatter(
        after(added(down_a, down_got), normed_rows), "ctx", scatter_dimension=0, tiled=True
    )

    rights = (gate_a, gate_b, up_a, up_b, act_a, act_b)
    lefts = (after(normed_row, down_got), normed_other, out_row, out_other)
    send_terms = ff_grad_terms(place, lefts, rights, lambda j: 2 + j, lambda j: 1 + 2 * j, (1, 2))
    links.label = "ff_sum1"
    ff_first = reduce_start(links, send_terms)
    links.label = "y_core"
    y_a, y_b = ff_call(
        links, y_kernel, layout, place, (after(act_a, *send_terms), act_b), (width, width), 1
    )
    y_got = links.core(y_b)
    grad_normed_two = after(grad_normed_two, y_b, *ff_first[::2])

    def mix_back(*refs):
        mix_back_body(1, *refs)

    grad_hidden, grad_hidden_low, grad_query, gain_two, *pair_terms = call(
        mix_back,
        place,
        (grad_normed_two, hidden_one, small, out_low, place_column, query, cosine, sine, *blocks),
        weight_o,
        [(wide, F32), (wide, BF16), (wide, BF16), ((1, width), F32)] + [(narrow, BF16)] * ctx_size,
        BACK_COST,
    )
    links.label = "y_core"
    mixed_rows = lax.all_gather(
        after(mixed_low, grad_normed_two), "ctx", axis=0, tiled=True
    )
    lefts = (after(normed_row, grad_hidden_low, y_got), *lefts[1:])
    ff_terms = ff_grad_terms(place, lefts, rights, lambda j: j, lambda j: 2 * j, (3,))
    links.label = "gkv"
    pair_terms = [pair_terms[0]] + [links.shift(pair_terms[step], -step) for step in steps]
    pair_terms[0] = after(pair_terms[0], ff_terms[0])
    def columns_over_ctx(parts):
        whole = jnp.zeros_like(parts)
        whole = lax.dynamic_update_index_in_dim(whole, pick(parts, ctx), ctx, 0)
        for step in steps:
            piece = links.turn(pick(parts, (ctx + step) % ctx_size), step)
            whole = lax.dynamic_update_index_in_dim(whole, piece, (ctx - step) % ctx_size, 0)
        return whole

    def qkv_back(*refs):
        qkv_back_body(ctx_size, *refs)

    columns = (width + 2 * KV_WIDTH) // ctx_size
    share_shape = (count + 16, columns + width // ctx_size)
    grad_stream, *shares = call(
        qkv_back,
        place,
        (*pair_terms, low_tokens, small, cosine, sine, grad_query, grad_hidden, grad_hidden_low, gain_two),
        weight_qkv,
        [(wide, F32)] + [(share_shape, BF16)] * ctx_size,
        0,
        [pltpu.VMEM((ctx_size, *share_shape), BF16)],
    )

    links.label = "gqkv_ctx"
    first_share = shares[0]
    shares = [first_share] + [links.turn(shares[step], step) for step in steps]
    shares[0] = after(shares[0], *ff_first)
    y_both = after(added(y_a, y_got), *shares[1:])
    y_sum = lax.psum_scatter(y_both, "ctx", scatter_dimension=0, tiled=True)
    layer_out = hidden_one + y_sum.astype(F32)
    links.label = "ff_sum2"
    ff_second = reduce_next(links, ff_terms, phase(ff_first, (first_share,))[0])
    chips = fsdp_size // 2
    term_shape = (chips, width // fsdp_size + 16, share_shape[1])
    term_mine, term_other = small_call(
        term_kernel,
        (*shares, normed_rows, mixed_rows),
        [(term_shape, BF16)] * 2,
        [
            pltpu.VMEM((ctx_size * count, share_shape[1]), BF16),
            pltpu.VMEM((width, share_shape[1]), F32),
            pltpu.VMEM((fsdp_size, share_shape[1]), F32),
        ],
        place,
    )
    links.label = "term_core"
    ff_send = reduce_end(place, ff_terms, ff_first, ff_second, 1, BF16, 12 * 10**9)
    term_mine = after(term_mine, ff_send)
    keep, *sends = small_call(
        sum_cores_kernel,
        (term_mine, links.core(term_other)),
        [(term_shape[1:], F32)] + [(term_shape[1:], BF16)] * (chips - 1),
    )
    links.label = "term_plane"
    q_columns, kv_columns = width // ctx_size, KV_WIDTH // ctx_size
    height, devices = width // fsdp_size, ctx_size * fsdp_size
    plane_got = [links.plane(x, 2 * mask) for mask, x in enumerate(sends, 1)]
    grad_q, grad_k, grad_v, grad_o, *vectors = small_call(
        sum_plane_kernel,
        (keep, *plane_got),
        [((height, q_columns), F32)]
        + [((kv_columns, height), F32)] * 2
        + [((height, q_columns), F32)]
        + [((1, x // devices), F32) for x in (width, width, width, KV_WIDTH, KV_WIDTH)],
        cost=0,
    )
    vectors = [x[0] for x in vectors]

    links.label = "final_core"
    ff_second = phase(ff_second, sends)[0]
    ff_mine = reduce_end(place, ff_terms, ff_first, ff_second, 0, F32, 0)
    hidden = 2 * ff_mine.shape[2]
    grad_gate, grad_up, grad_down = small_call(
        join_cores_kernel,
        (ff_mine, after(links.core(ff_send), *sends)),
        [((height, hidden), F32)] * 3,
        place=place,
        cost=2*10**9,
    )

    return (
        layer_out[None],
        grad_stream[None],
        vectors[0],
        grad_q,
        vectors[2],
        jnp.transpose(grad_k),
        vectors[3],
        jnp.transpose(grad_v),
        vectors[4],
        grad_o,
        vectors[1],
        grad_gate,
        grad_up,
        jnp.transpose(grad_down),
    )


def solution(mesh):
    links = Links(mesh.shape["ctx"], mesh.shape["fsdp"])
    vector, matrix, stream = P(BOTH), P(BOTH, None), P("fsdp", "ctx", None)
    grid = P("fsdp", "ctx")
    in_specs = (
        stream,
        grid,
        vector,
        matrix,
        vector,
        matrix,
        vector,
        matrix,
        vector,
        matrix,
        vector,
        matrix,
        matrix,
        P(None, BOTH),
        stream,
    )
    out_specs = (
        stream,
        stream,
        vector,
        grid,
        vector,
        grid,
        vector,
        grid,
        vector,
        grid,
        vector,
        grid,
        grid,
        P("ctx", "fsdp"),
    )

    def run(*arrays):
        plane_of_four = mesh.shape["fsdp"] == 8 and arrays[3].shape[0] % 16 == 0
        form = per_device_plane_of_four if plane_of_four else per_device_any_mesh
        return form(*arrays, links=links)

    return jax.shard_map(run, mesh=mesh, in_specs=in_specs, out_specs=out_specs, check_vma=False)
```

```python
import jax
import jax.numpy as jnp
from jax import lax
from jax.experimental import pallas as pl
from jax.experimental.pallas import tpu as pltpu
from jax.sharding import PartitionSpec as P

QUERY_HEADS = 12
KEY_VALUE_HEADS = 2
HEAD_SIZE = 128
GROUP = QUERY_HEADS // KEY_VALUE_HEADS
KV_WIDTH = KEY_VALUE_HEADS * HEAD_SIZE
EPSILON = 1e-06
BACK_COST = 8 * 10**9
BOTH = ("ctx", "fsdp")
F32 = jnp.float32
BF16 = jnp.bfloat16


def dot(a, b, dims):
    return lax.dot_general(a, b, ((dims[:1], dims[1:]), ((), ())), preferred_element_type=F32)


def nn(a, b):
    return dot(a, b, (1, 0))


def nt(a, b):
    return dot(a, b, (1, 1))


def tn(a, b):
    return dot(a, b, (0, 0))


def rms_scale(matrix):
    return lax.rsqrt(jnp.mean(matrix * matrix, axis=-1, keepdims=True) + EPSILON)


def angle_tables(positions):
    step_index = jnp.arange(HEAD_SIZE // 2, dtype=F32) * 2.0
    frequency = 10000.0 ** (-step_index / HEAD_SIZE)
    angles = positions.astype(F32)[:, None] * frequency[None, :]
    return jnp.cos(angles)[:, None, :], jnp.sin(angles)[:, None, :]


def rotate(matrix, cosine, sine):
    rows = matrix.shape[0]
    heads = matrix.reshape(rows, -1, HEAD_SIZE)
    a, b = heads[..., : HEAD_SIZE // 2], heads[..., HEAD_SIZE // 2 :]
    turned = jnp.concatenate([a * cosine - b * sine, b * cosine + a * sine], axis=-1)
    return turned.reshape(rows, -1)


def pick(stacked, index):
    return lax.dynamic_index_in_dim(stacked, index, 0, keepdims=False)


class Links:
    def __init__(self, ctx_size, fsdp_size):
        self.ctx_size, self.fsdp_size = ctx_size, fsdp_size
        self.label = "move"
        self.planes = [m for m in (2, 4, 8, 16, 32, 64) if m < fsdp_size]

    def send(self, x, target):
        pairs = []
        for c in range(self.ctx_size):
            for f in range(self.fsdp_size):
                to = target(c, f)
                if to is not None:
                    pairs.append((c * self.fsdp_size + f, to[0] * self.fsdp_size + to[1]))
        with jax.named_scope(self.label):
            return lax.ppermute(x, BOTH, pairs)

    def core(self, x):
        return self.send(x, lambda c, f: (c, f ^ 1))

    def plane(self, x, mask):
        return self.send(x, lambda c, f: (c, f ^ mask))

    def turn(self, x, step):
        return self.send(x, lambda c, f: ((c + step) % self.ctx_size, f))

    def shift(self, x, step):
        return self.send(
            x, lambda c, f: (c + step, f) if 0 <= c + step < self.ctx_size else None
        )


def plane_gather(links, shard):
    first, second, *rest = links.planes
    half = shard.shape[0] // 2
    a = links.plane(shard, first)
    b = links.plane(shard, second)
    low = links.plane(b[:half], first)
    high = links.plane(a[half:], second)
    pieces = {0: shard, first: a, second: b, first | second: jnp.concatenate([low, high])}
    for mask in rest:
        pieces.update({had | mask: links.plane(piece, mask) for had, piece in pieces.items()})
    return pieces


def ff_weight(links, ctx, chip, core, shard):
    ctx_size = links.ctx_size
    rows, hidden = shard.shape
    block = hidden // (2 * ctx_size)
    parts = jnp.transpose(shard.reshape(rows, ctx_size, 2, block), (2, 1, 0, 3))
    mine, other = pick(parts, core), pick(parts, 1 - core)
    got = links.core(other)
    even = core == 0
    pairs = jnp.stack([jnp.where(even, mine, got), jnp.where(even, got, mine)], axis=1)
    by_source = jnp.zeros_like(pairs)
    by_source = lax.dynamic_update_index_in_dim(by_source, pick(pairs, ctx), ctx, 0)
    for step in range(1, ctx_size):
        piece = links.turn(pick(pairs, (ctx + step) % ctx_size), step)
        by_source = lax.dynamic_update_index_in_dim(by_source, piece, (ctx - step) % ctx_size, 0)
    pieces = plane_gather(links, by_source)
    whole = jnp.zeros((ctx_size, links.fsdp_size // 2, 2, rows, block), shard.dtype)
    for mask, piece in pieces.items():
        whole = lax.dynamic_update_index_in_dim(whole, piece, chip ^ (mask // 2), 1)
    return whole.reshape(-1, block)


def spread_tokens(links, x):
    row = jnp.concatenate([x] + [links.turn(x, step) for step in range(1, links.ctx_size)])
    return jnp.concatenate([row, links.core(row)])


def collect_tokens(links, partial):
    rows = partial.shape[0] // 2
    got = links.core(partial[rows:].astype(BF16))
    count = rows // links.ctx_size
    row = (partial[:rows].astype(F32) + got.astype(F32)).reshape(links.ctx_size, count, -1)
    total = row[0]
    for step in range(1, links.ctx_size):
        total = total + links.turn(row[step].astype(BF16), -step).astype(F32)
    return total


def per_device_any_mesh(
    tokens,
    positions,
    norm1_gain,
    q_weight,
    q_bias,
    key_projection,
    key_bias_vector,
    value_projection,
    value_bias_vector,
    o_weight,
    norm2_gain,
    gate_weight,
    up_weight,
    down_weight,
    cotangent,
    *,
    links,
):
    ctx_size, fsdp_size = links.ctx_size, links.fsdp_size
    ctx, row_index = lax.axis_index("ctx"), lax.axis_index("fsdp")
    chip, core = row_index // 2, row_index % 2
    count, width = tokens.shape[1:]
    scale = HEAD_SIZE ** (-0.5)
    even = core == 0

    shard_rows = q_weight.shape[0]

    def column(x):
        return jnp.pad(x, (0, shard_rows - x.shape[0]))[:, None]

    kv_bias_rows = key_bias_vector.shape[0]
    extra = jnp.concatenate(
        [
            column(x)
            for x in (norm1_gain, q_bias, norm2_gain, key_bias_vector, value_bias_vector)
        ],
        axis=1,
    )
    extra = jnp.pad(extra, ((0, 0), (0, 128 - extra.shape[1])))
    packed = jnp.concatenate([q_weight, key_projection, value_projection, extra], axis=1)
    packed = lax.all_gather(packed, BOTH, axis=0, tiled=True)
    weight_o = lax.all_gather(o_weight, BOTH, axis=0, tiled=True)

    weight_gate = ff_weight(links, ctx, chip, core, gate_weight)
    weight_up = ff_weight(links, ctx, chip, core, up_weight)
    weight_down = ff_weight(links, ctx, chip, core, jnp.transpose(down_weight))

    qkv_width = width + 2 * KV_WIDTH
    weight_qkv = packed[:, :qkv_width]
    small = jnp.transpose(packed[:, qkv_width:])[:5].astype(F32)
    gain_one, bias_q, gain_two = small[0:1], small[1:2], small[2:3]

    def bias_of(row):
        return row.reshape(-1, shard_rows)[:, :kv_bias_rows].reshape(1, -1)

    bias_k, bias_v = bias_of(small[3]), bias_of(small[4])
    out_low = cotangent[0]
    group_out = spread_tokens(links, out_low)

    stream = tokens[0].astype(F32)
    scale_one = rms_scale(stream)
    unit_one = stream * scale_one
    normed_one = (unit_one * gain_one).astype(BF16)
    cosine, sine = angle_tables(positions[0])
    linear = nn(normed_one, weight_qkv)
    query = rotate(linear[:, :width] + bias_q, cosine, sine).astype(BF16)
    key = rotate(linear[:, width : width + KV_WIDTH] + bias_k, cosine, sine).astype(BF16)
    value = (linear[:, width + KV_WIDTH :] + bias_v).astype(BF16)
    pairs = jnp.concatenate([key, value], axis=1)
    row_pairs = jnp.concatenate(
        [pairs] + [links.shift(pairs, step) for step in range(1, ctx_size)]
    )
    keys = row_pairs[:, :KV_WIDTH].reshape(-1, KEY_VALUE_HEADS, HEAD_SIZE)
    values = row_pairs[:, KV_WIDTH:].reshape(-1, KEY_VALUE_HEADS, HEAD_SIZE)
    local_index = jnp.arange(count)
    key_index = jnp.concatenate(
        [(ctx - step) * count + local_index for step in range(ctx_size)]
    )
    query_index = ctx * count + local_index
    doc_start = query_index - positions[0]
    allowed = (key_index[None, :] >= doc_start[:, None]) & (
        key_index[None, :] <= query_index[:, None]
    )
    query_heads = query.reshape(count, KEY_VALUE_HEADS, GROUP, HEAD_SIZE)
    scores = jnp.einsum("qkgd,rkd->kgqr", query_heads, keys, preferred_element_type=F32) * scale
    scores = jnp.where(allowed, scores, -1e30)
    top = jnp.max(scores, axis=-1, keepdims=True)
    weights = jnp.where(allowed, jnp.exp(scores - top), 0.0)
    probs = weights / jnp.sum(weights, axis=-1, keepdims=True)
    probs_low = probs.astype(BF16)
    mixed = jnp.einsum("kgqr,rkd->qkgd", probs_low, values, preferred_element_type=F32)
    mixed_low = mixed.reshape(count, -1).astype(BF16)
    hidden_one = stream + nn(mixed_low, weight_o)

    scale_two = rms_scale(hidden_one)
    unit_two = hidden_one * scale_two
    normed_two = (unit_two * gain_two).astype(BF16)
    group_normed = spread_tokens(links, normed_two)
    gate_pre = nn(group_normed, weight_gate)
    up_pre = nn(group_normed, weight_up)
    grad_act = nn(group_out, weight_down)
    sigmoid_gate = jax.nn.sigmoid(gate_pre)
    activated = (gate_pre * sigmoid_gate * up_pre).astype(BF16)
    grad_gate_low = (
        grad_act * up_pre * sigmoid_gate * (1.0 + gate_pre * (1.0 - sigmoid_gate))
    ).astype(BF16)
    grad_up_low = (grad_act * gate_pre * sigmoid_gate).astype(BF16)
    grad_normed_two = collect_tokens(
        links, nt(grad_gate_low, weight_gate) + nt(grad_up_low, weight_up)
    )
    layer_out = hidden_one + collect_tokens(links, nt(activated, weight_down))

    planes = [
        [c * fsdp_size + 2 * p + k for p in range(fsdp_size // 2)]
        for c in range(ctx_size)
        for k in range(2)
    ]

    def ff_grad(left, right):
        term = tn(left, right).astype(BF16)
        part = lax.psum_scatter(
            term, BOTH, scatter_dimension=0, tiled=True, axis_index_groups=planes
        )
        part = part.reshape(2, -1, part.shape[1])
        mine, got = pick(part, core), links.core(pick(part, 1 - core))
        return jnp.concatenate(
            [jnp.where(even, mine, got), jnp.where(even, got, mine)], axis=1
        ).astype(F32)

    grad_gate = ff_grad(group_normed, grad_gate_low)
    grad_up = ff_grad(group_normed, grad_up_low)
    grad_down = jnp.transpose(ff_grad(group_out, activated))

    grad_gain_two = jnp.sum(grad_normed_two * unit_two, axis=0)
    weighted_two = grad_normed_two * gain_two
    grad_hidden = out_low.astype(F32) + scale_two * (
        weighted_two - unit_two * jnp.mean(weighted_two * unit_two, axis=-1, keepdims=True)
    )

    grad_hidden_low = grad_hidden.astype(BF16)
    grad_mixed = nt(grad_hidden_low, weight_o).astype(BF16)
    grad_mixed = grad_mixed.reshape(count, KEY_VALUE_HEADS, GROUP, HEAD_SIZE)
    grad_probs = jnp.einsum("qkgd,rkd->kgqr", grad_mixed, values, preferred_element_type=F32)
    delta = jnp.sum(probs * grad_probs, axis=-1, keepdims=True)
    grad_scores = (probs * (grad_probs - delta)).astype(BF16)
    grad_query = jnp.einsum("kgqr,rkd->qkgd", grad_scores, keys, preferred_element_type=F32)
    grad_key = (
        jnp.einsum("kgqr,qkgd->rkd", grad_scores, query_heads, preferred_element_type=F32) * scale
    )
    grad_value = jnp.einsum("kgqr,qkgd->rkd", probs_low, grad_mixed, preferred_element_type=F32)
    pair_terms = jnp.concatenate(
        [grad_key.reshape(-1, KV_WIDTH), grad_value.reshape(-1, KV_WIDTH)], axis=1
    ).reshape(ctx_size, count, -1)
    pair_grads = pair_terms[0]
    for step in range(1, ctx_size):
        pair_grads = pair_grads + links.shift(pair_terms[step].astype(BF16), -step).astype(F32)
    grad_q_low = rotate(grad_query.reshape(count, -1) * scale, cosine, -sine).astype(BF16)
    grad_k_low = rotate(pair_grads[:, :KV_WIDTH], cosine, -sine).astype(BF16)
    grad_v_low = pair_grads[:, KV_WIDTH:].astype(BF16)
    grad_qkv = jnp.concatenate([grad_q_low, grad_k_low, grad_v_low], axis=1)
    grad_normed_one = nt(grad_qkv, weight_qkv)
    grad_gain_one = jnp.sum(grad_normed_one * unit_one, axis=0)
    weighted_one = grad_normed_one * gain_one
    grad_stream = grad_hidden + scale_one * (
        weighted_one - unit_one * jnp.mean(weighted_one * unit_one, axis=-1, keepdims=True)
    )

    def columns_over_ctx(arrays):
        parts = jnp.concatenate([x.reshape(count, ctx_size, -1) for x in arrays], axis=2)
        parts = jnp.transpose(parts, (1, 0, 2))
        whole = jnp.zeros_like(parts)
        whole = lax.dynamic_update_index_in_dim(whole, pick(parts, ctx), ctx, 0)
        for step in range(1, ctx_size):
            piece = links.turn(pick(parts, (ctx + step) % ctx_size), step)
            whole = lax.dynamic_update_index_in_dim(whole, piece, (ctx - step) % ctx_size, 0)
        return whole.reshape(ctx_size * count, -1)

    def attention_grad(rows, arrays):
        left = lax.all_gather(rows, "ctx", axis=0, tiled=True)
        term = tn(left, columns_over_ctx(arrays)).astype(BF16)
        return lax.psum_scatter(term, "fsdp", scatter_dimension=0, tiled=True).astype(F32)

    grad_o = attention_grad(mixed_low, [grad_hidden_low])
    grad_packed = attention_grad(normed_one, [grad_q_low, grad_k_low, grad_v_low])
    q_columns, kv_columns = width // ctx_size, KV_WIDTH // ctx_size

    sums = jnp.concatenate(
        [grad_gain_one, grad_gain_two, jnp.sum(grad_qkv.astype(F32), axis=0)]
    )
    sums = lax.psum(sums, BOTH)
    device = ctx * fsdp_size + row_index

    def own(start, size):
        part = size // (ctx_size * fsdp_size)
        return lax.dynamic_slice_in_dim(sums, start + device * part, part)

    return (
        layer_out[None],
        grad_stream[None],
        own(0, width),
        grad_packed[:, :q_columns],
        own(2 * width, width),
        grad_packed[:, q_columns : q_columns + kv_columns],
        own(3 * width, KV_WIDTH),
        grad_packed[:, q_columns + kv_columns :],
        own(3 * width + KV_WIDTH, KV_WIDTH),
        grad_o,
        own(width, width),
        grad_gate,
        grad_up,
        grad_down,
    )


def after(x, *others):
    return lax.optimization_barrier((x, *others))[0]


def phase(*groups):
    flat = lax.optimization_barrier(tuple(x for group in groups for x in group))
    out = []
    for group in groups:
        out.append(list(flat[: len(group)]))
        flat = flat[len(group) :]
    return out


def plane_start(links, shard):
    return links.plane(shard, 2), links.plane(shard, 4)


def plane_end(links, shard, a, b):
    half = shard.shape[0] // 2
    return shard, a, b, links.plane(b[:half], 2), links.plane(a[half:], 4)


def load_pieces(layout, sizes, place, pieces, which, weight, semaphore):
    ctx_size, chips, rows = sizes
    for (entries, mask, _), piece in zip(layout, pieces):
        for i, (step, core) in enumerate(entries):
            source = lax.rem(place[0] - step + ctx_size, ctx_size)
            start = ((source * chips + (place[1] ^ mask)) * 2 + core) * rows
            pltpu.make_async_copy(
                piece.at[i, which],
                weight.at[pl.ds(pl.multiple_of(start, rows), rows)],
                semaphore,
            ).start()


def ff_kernel(layout, sizes, place, normed, out_grad, *refs):
    pieces, refs = refs[: len(layout)], refs[len(layout) :]
    act_ref, gate_ref, up_ref, down_ref, weights, semaphores = refs

    @pl.when(pl.program_id(0) == 0)
    def _():
        for which in range(3):
            load_pieces(
                layout, sizes, place, pieces, which, weights.at[which], semaphores.at[which]
            )

    def arrived(which):
        @pl.when(pl.program_id(0) == 0)
        def _():
            wait_all(weights.at[which], semaphores.at[which])

    x, gy = normed[...], out_grad[...]
    arrived(0)
    gate = nn(x, weights[0])
    arrived(1)
    up = nn(x, weights[1])
    arrived(2)
    grad = nn(gy, weights[2])
    sigmoid = 1.0 / (1.0 + jnp.exp(-gate))
    silu = gate * sigmoid
    grad_gate = (grad * up * sigmoid * (1.0 + gate * (1.0 - sigmoid))).astype(BF16)
    grad_up = (grad * silu).astype(BF16)
    act_ref[...] = (silu * up).astype(BF16)
    gate_ref[...] = grad_gate
    up_ref[...] = grad_up
    down_ref[...] = (nt(grad_gate, weights[0]) + nt(grad_up, weights[1])).astype(BF16)


def y_kernel(layout, sizes, place, act_a, act_b, *refs):
    pieces, (y_a, y_b, weight, semaphore) = refs[: len(layout)], refs[len(layout) :]

    @pl.when(pl.program_id(0) == 0)
    def _():
        load_pieces(layout, sizes, place, pieces, 2, weight, semaphore)
        wait_all(weight, semaphore)

    y_a[...] = nt(act_a[...], weight[...]).astype(BF16)
    y_b[...] = nt(act_b[...], weight[...]).astype(BF16)


def ff_call(links, kernel, layout, place, arrays, widths, matrices):
    tokens = arrays[0].shape[0]
    rows, block = layout[0][2].shape[2:]
    sizes = (links.ctx_size, links.fsdp_size // 2, rows)
    depth = 2 * sizes[0] * sizes[1] * rows
    tile = 256

    def spec(size):
        return pl.BlockSpec((tile, size), lambda i, place: (i, 0))

    def body(*refs):
        kernel(layout, sizes, *refs)

    if matrices == 1:
        scratch = [pltpu.VMEM((depth, block), BF16), pltpu.SemaphoreType.DMA]
    else:
        scratch = [
            pltpu.VMEM((matrices, depth, block), BF16),
            pltpu.SemaphoreType.DMA((matrices,)),
        ]
    return pl.pallas_call(
        body,
        grid_spec=pltpu.PrefetchScalarGridSpec(
            num_scalar_prefetch=1,
            grid=(tokens // tile,),
            in_specs=[spec(x.shape[1]) for x in arrays]
            + [pl.BlockSpec(memory_space=pl.ANY)] * len(layout),
            out_specs=[spec(x) for x in widths],
            scratch_shapes=scratch,
        ),
        out_shape=[jax.ShapeDtypeStruct((tokens, x), BF16) for x in widths],
        compiler_params=pltpu.CompilerParams(vmem_limit_bytes=56 * 2**20),
        cost_estimate=pl.CostEstimate(flops=0, bytes_accessed=0, transcendentals=0),
    )(place, *arrays, *[piece for _, _, piece in layout])


def grad_kernel(place, *refs):
    lefts, rights, outs = refs[:8], refs[8:14], refs[14:]
    low, high = outs[: len(outs) // 2], outs[len(outs) // 2 :]
    for which in range(3):
        first = 4 * (which // 2)
        for parts, (left_a, left_b), core in (
            (low, lefts[first : first + 2], 0),
            (high, lefts[first + 2 : first + 4], 1),
        ):
            out, at = (parts[0], which) if len(parts) == 1 else (parts[which > 0], max(which - 1, 0))
            half = left_a.shape[1] // 2
            rows = slice(core * half, (core + 1) * half)
            right_a, right_b = rights[2 * which : 2 * which + 2]
            term = tn(left_a[:, rows], right_a[...]) + tn(left_b[:, rows], right_b[...])
            out[0, at] = term.astype(BF16)


def ff_grad_terms(place, lefts, rights, low_at, high_at, parts):
    tokens, width = lefts[0].shape
    block = rights[0].shape[1]
    part = width // 4

    def left(at):
        return pl.BlockSpec((tokens, part), lambda j, place: (0, place[1] ^ at(j)))

    right = pl.BlockSpec((tokens, block), lambda j, place: (0, 0))
    outs = [pl.BlockSpec((1, n, part // 2, block), lambda j, place: (j, 0, 0, 0)) for n in parts]
    low, high = left(low_at), left(high_at)
    x_a, x_b, y_a, y_b = lefts
    return pl.pallas_call(
        grad_kernel,
        grid_spec=pltpu.PrefetchScalarGridSpec(
            num_scalar_prefetch=1,
            grid=(2,),
            in_specs=[low, low, high, high] * 2 + [right] * 6,
            out_specs=outs * 2,
        ),
        out_shape=[jax.ShapeDtypeStruct((2, n, part // 2, block), BF16) for n in parts] * 2,
        compiler_params=pltpu.CompilerParams(vmem_limit_bytes=56 * 2**20),
        cost_estimate=pl.CostEstimate(flops=0, bytes_accessed=0, transcendentals=0),
    )(place, x_a, x_b, x_a, x_b, y_a, y_b, y_a, y_b, *rights)


def added(a, b):
    return (a.astype(F32) + b.astype(F32)).astype(BF16)


def reduce_start(links, terms):
    return [links.plane(x, mask) for x, mask in zip(terms, (4, 4, 2, 2))]


def add_pairs_kernel(*refs):
    for i, out in enumerate(refs[6:]):
        keep, one, rest = refs[3 * i : 3 * i + 3]
        out[:1] = (keep[0, :1].astype(F32) + one[0].astype(F32)).astype(BF16)
        out[1:] = (keep[0, 1:].astype(F32) + rest[0].astype(F32)).astype(BF16)


def first_specs(index):
    def spec(x):
        return pl.BlockSpec((1, *x.shape[1:]), lambda i, *place: (index, 0, 0, 0))

    return spec


def reduce_next(links, terms, first):
    shape = terms[0].shape
    arrays = (terms[0], first[0], first[1], terms[1], first[2], first[3])
    spec = first_specs(1)
    whole = pl.BlockSpec(shape[1:], lambda i: (0, 0, 0))
    low, high = pl.pallas_call(
        add_pairs_kernel,
        grid=(1,),
        in_specs=[spec(x) for x in arrays],
        out_specs=[whole] * 2,
        out_shape=[jax.ShapeDtypeStruct(shape[1:], BF16)] * 2,
        compiler_params=pltpu.CompilerParams(vmem_limit_bytes=56 * 2**20),
        cost_estimate=pl.CostEstimate(flops=0, bytes_accessed=0, transcendentals=0),
    )(*arrays)
    return links.plane(low, 2), links.plane(high, 4)


def reduce_end_kernel(turned, place, *refs):
    low, high, (out,) = refs[:4], refs[4:8], refs[8:]

    def write(ref, parts):
        keep, one, rest, last = parts
        total = keep[0, :1].astype(F32) + one[0].astype(F32) + last[:1].astype(F32)
        ref[:1] = total.astype(ref.dtype)
        total = keep[0, 1:].astype(F32) + rest[0].astype(F32) + last[1:].astype(F32)
        ref[1:] = total.astype(ref.dtype)

    @pl.when(place[2] == turned)
    def _():
        write(out, low)

    @pl.when(place[2] != turned)
    def _():
        write(out, high)


def reduce_end(place, terms, first, second, turned, dtype, cost):
    shape = terms[0].shape[1:]
    spec = first_specs(0)
    whole = pl.BlockSpec(shape, lambda i, place: (0, 0, 0))
    low = (terms[0], first[0], first[1])
    high = (terms[1], first[2], first[3])
    def body(*refs):
        reduce_end_kernel(turned, *refs)

    return pl.pallas_call(
        body,
        grid_spec=pltpu.PrefetchScalarGridSpec(
            num_scalar_prefetch=1,
            grid=(1,),
            in_specs=[*map(spec, low), whole, *map(spec, high), whole],
            out_specs=whole,
        ),
        out_shape=jax.ShapeDtypeStruct(shape, dtype),
        compiler_params=pltpu.CompilerParams(vmem_limit_bytes=56 * 2**20),
        cost_estimate=pl.CostEstimate(flops=cost, bytes_accessed=0, transcendentals=0),
    )(place, *low, second[0], *high, second[1])


def join_cores_kernel(place, mine, got, gate, up, down):
    def write(even, odd):
        for which, ref in enumerate((gate, up, down)):
            ref[...] = jnp.concatenate([even(which), odd(which)], axis=1)

    def own(which):
        return mine[which]

    def others(which):
        return got[which].astype(F32)

    @pl.when(place[2] == 0)
    def _():
        write(own, others)

    @pl.when(place[2] != 0)
    def _():
        write(others, own)


def split_kernel(place, gate, up, down, mine, other):
    block = mine.shape[3]

    def write(core):
        for which, ref in enumerate((gate, up, down)):
            for target in range(mine.shape[0]):
                start = (2 * target + core) * block
                mine[target, which] = ref[:, start : start + block]
                start = (2 * target + 1 - core) * block
                other[target, which] = ref[:, start : start + block]

    @pl.when(place[2] == 0)
    def _():
        write(0)

    @pl.when(place[2] != 0)
    def _():
        write(1)


def split_hidden(links, place, shards):
    rows, hidden = shards[0].shape
    whole = pl.BlockSpec((rows, hidden), lambda i, place: (0, 0))
    shape = (links.ctx_size, 3, rows, hidden // (2 * links.ctx_size))
    out = pl.BlockSpec(shape, lambda i, place: (0, 0, 0, 0))
    return pl.pallas_call(
        split_kernel,
        grid_spec=pltpu.PrefetchScalarGridSpec(
            num_scalar_prefetch=1, grid=(1,), in_specs=[whole] * 3, out_specs=[out] * 2
        ),
        out_shape=[jax.ShapeDtypeStruct(shape, BF16)] * 2,
        compiler_params=pltpu.CompilerParams(vmem_limit_bytes=32 * 2**20),
    )(place, *shards)


class Rows:
    def __init__(self, sizes, pieces, layout, first, columns):
        self.sizes, self.pieces, self.layout = sizes, pieces, layout
        self.first, self.columns = first, columns
        self.rows = pieces[0].shape[-2]
        self.shape = (2 * sizes[0] * sizes[1] * self.rows, columns)

    def start(self, place, refs, weight, semaphore):
        ctx_size, chips = self.sizes
        for piece, index, step, mask, turned in self.layout:
            source = lax.rem(place[0] - step + ctx_size, ctx_size)
            start = ((source * chips + (place[1] ^ mask)) * 2 + (place[2] ^ turned)) * self.rows
            pltpu.make_async_copy(
                refs[piece].at[(*index, slice(None), pl.ds(self.first, self.columns))],
                weight.at[pl.ds(pl.multiple_of(start, self.rows), self.rows)],
                semaphore,
            ).start()


def rows_layout(ctx_size):
    half = ctx_size // 2
    layout = []
    for step in range(ctx_size):
        layout += [(mask, (step,), step, mask, 0) for mask in range(3)]
        layout.append((3, (step,), step, 3, 0) if step < half else (4, (step - half,), step, 3, 0))
        layout.append((5, (step,), step, 0, 1))
        layout += [(6, (i * ctx_size + step,), step, i + 1, 1) for i in range(3)]
    return layout


def wait_all(weight, semaphore):
    pltpu.make_async_copy(weight, weight, semaphore).wait()


def call(body, place, arrays, weight, out_shapes, cost, scratch=()):
    any_spec = pl.BlockSpec(memory_space=pl.ANY)
    vmem = pl.BlockSpec(memory_space=pltpu.VMEM)
    count, pieces = len(arrays), len(weight.pieces)

    def kernel(place, *refs):
        ins, parts, outs = refs[:count], refs[count : count + pieces], refs[count + pieces : -2]
        whole, semaphore = refs[-2:]
        weight.start(place, parts, whole, semaphore)
        body(place, ins, outs, whole, lambda: wait_all(whole, semaphore))

    return pl.pallas_call(
        kernel,
        in_specs=[pl.BlockSpec(memory_space=pltpu.SMEM)] + [vmem] * count + [any_spec] * pieces,
        out_specs=[vmem] * len(out_shapes),
        out_shape=[jax.ShapeDtypeStruct(shape, dtype) for shape, dtype in out_shapes],
        scratch_shapes=[*scratch, pltpu.VMEM(weight.shape, BF16), pltpu.SemaphoreType.DMA],
        compiler_params=pltpu.CompilerParams(vmem_limit_bytes=56 * 2**20),
        cost_estimate=pl.CostEstimate(flops=cost, bytes_accessed=0, transcendentals=0),
    )(place, *arrays, *weight.pieces)


def turn_halves(x, cosine, sine):
    return x * cosine + pltpu.roll(x, HEAD_SIZE // 2, 1) * sine


def turned_heads(x, cosine, sine):
    heads = [x[:, i : i + HEAD_SIZE] for i in range(0, x.shape[1], HEAD_SIZE)]
    return jnp.concatenate([turn_halves(x, cosine, sine) for x in heads], axis=1)


def qkv_body(shard_rows, place, ins, outs, weight, wait):
    tokens, cosine, sine = ins
    normed_ref, query_ref, pairs_ref, small_ref = outs
    width = tokens.shape[1]
    qkv_width = width + 2 * KV_WIDTH
    x = tokens[...].astype(F32)
    unit = x * rms_scale(x)
    wait()
    small = jnp.transpose(weight[:, qkv_width:].astype(F32))[:8]
    bias_rows = KV_WIDTH * shard_rows // width
    row = lax.broadcasted_iota(jnp.int32, (width, KV_WIDTH), 0)
    at = lax.broadcasted_iota(jnp.int32, (width, KV_WIDTH), 1)
    chosen = row == (at // bias_rows) * shard_rows + at % bias_rows
    kv_bias = nn(small.astype(BF16), chosen.astype(BF16))
    normed = (unit * small[0:1]).astype(BF16)
    normed_ref[...] = normed
    small_ref[...] = small
    linear = nn(normed, weight[:, :qkv_width])
    query = linear[:, :width] + small[1:2]
    key = linear[:, width : width + KV_WIDTH] + kv_bias[3:4]
    query_ref[...] = turned_heads(query, cosine[...], sine[...]).astype(BF16)
    pairs_ref[:, :KV_WIDTH] = turned_heads(key, cosine[...], sine[...]).astype(BF16)
    pairs_ref[:, KV_WIDTH:] = (linear[:, width + KV_WIDTH :] + kv_bias[4:5]).astype(BF16)


def allowed_keys(ctx, positions, blocks):
    count = positions.shape[0]
    shape = (count, blocks * count)
    column = lax.broadcasted_iota(jnp.int32, shape, 1)
    query = ctx * count + lax.broadcasted_iota(jnp.int32, shape, 0)
    key = (ctx - column // count) * count + column % count
    return (key >= query - positions) & (key <= query)


def heads_of(x, group):
    first = group * GROUP
    return jnp.concatenate(
        [x[:, i * HEAD_SIZE : (i + 1) * HEAD_SIZE] for i in range(first, first + GROUP)], axis=0
    )


def softmax_of(query, keys, allowed):
    scores = nt(query, keys) * HEAD_SIZE ** (-0.5)
    scores = jnp.where(allowed, scores, -1e30)
    weights = jnp.exp(scores - jnp.max(scores, axis=-1, keepdims=True))
    weights = jnp.where(allowed, weights, 0.0)
    return weights / jnp.sum(weights, axis=-1, keepdims=True)


def group_pairs(blocks, group):
    def columns(start):
        return jnp.concatenate([b[:, start : start + HEAD_SIZE] for b in blocks], axis=0)

    return columns(group * HEAD_SIZE), columns(KV_WIDTH + group * HEAD_SIZE)


def mix_body(place, ins, outs, weight, wait):
    tokens, small, positions, query, *blocks = ins
    mixed_ref, hidden_ref, normed_ref = outs
    count = tokens.shape[0]
    allowed = allowed_keys(place[0], positions[...], len(blocks))
    allowed = jnp.concatenate([allowed.astype(F32)] * GROUP, axis=0) > 0
    for group in range(KEY_VALUE_HEADS):
        keys, values = group_pairs(blocks, group)
        probs = softmax_of(heads_of(query, group), keys, allowed)
        mixed = nn(probs.astype(BF16), values).astype(BF16)
        for h in range(GROUP):
            start = (group * GROUP + h) * HEAD_SIZE
            mixed_ref[:, start : start + HEAD_SIZE] = mixed[h * count : (h + 1) * count]
    wait()
    hidden = tokens[...].astype(F32) + nn(mixed_ref[...], weight[...])
    hidden_ref[...] = hidden
    normed_ref[...] = (hidden * rms_scale(hidden) * small[2:3]).astype(BF16)


def norm_back(unit, scale, grad, gain):
    weighted = grad * gain
    return scale * (weighted - unit * jnp.mean(weighted * unit, axis=-1, keepdims=True))


def mix_back_body(steps, place, ins, outs, weight, wait):
    terms, ins = ins[:steps], ins[steps:]
    hidden_ref, small, out_grad, positions, query, cosine, sine, *blocks = ins
    grad_hidden_ref, low_ref, grad_query_ref, gain_ref, *pair_refs = outs
    count = hidden_ref.shape[0]
    hidden = hidden_ref[...]
    scale = rms_scale(hidden)
    unit = hidden * scale
    grad = terms[0][...].astype(F32)
    for term in terms[1:]:
        grad = grad + term[...].astype(F32)
    gain_ref[...] = jnp.sum(grad * unit, axis=0, keepdims=True)
    grad_hidden = out_grad[...].astype(F32) + norm_back(unit, scale, grad, small[2:3])
    grad_hidden_ref[...] = grad_hidden
    low = grad_hidden.astype(BF16)
    low_ref[...] = low
    wait()
    grad_mixed = nt(low, weight[...]).astype(BF16)
    allowed = allowed_keys(place[0], positions[...], len(blocks))
    allowed = jnp.concatenate([allowed.astype(F32)] * GROUP, axis=0) > 0
    score_scale = HEAD_SIZE ** (-0.5)
    for group in range(KEY_VALUE_HEADS):
        keys, values = group_pairs(blocks, group)
        queries, grads = heads_of(query, group), heads_of(grad_mixed, group)
        probs = softmax_of(queries, keys, allowed)
        grad_probs = nt(grads, values)
        delta = jnp.sum(probs * grad_probs, axis=-1, keepdims=True)
        grad_scores = (probs * (grad_probs - delta)).astype(BF16)
        grad_query = nn(grad_scores, keys) * score_scale
        for h in range(GROUP):
            start = (group * GROUP + h) * HEAD_SIZE
            grad_query_ref[:, start : start + HEAD_SIZE] = turn_halves(
                grad_query[h * count : (h + 1) * count], cosine[...], -sine[...]
            ).astype(BF16)
        grad_key = (tn(grad_scores, queries) * score_scale).astype(BF16)
        grad_value = tn(probs.astype(BF16), grads).astype(BF16)
        start = group * HEAD_SIZE
        for block, ref in enumerate(pair_refs):
            rows = slice(block * count, (block + 1) * count)
            ref[:, start : start + HEAD_SIZE] = grad_key[rows]
            ref[:, KV_WIDTH + start : KV_WIDTH + start + HEAD_SIZE] = grad_value[rows]


def qkv_back_body(steps, place, ins, outs, weight, wait):
    terms, ins = ins[:steps], ins[steps:]
    tokens, small, cosine, sine, grad_query, grad_hidden, grad_hidden_low, gain_two = ins
    stream_ref, *share_refs, share_ref = outs
    count, width = tokens.shape
    pairs = terms[0][...].astype(F32)
    for term in terms[1:]:
        pairs = pairs + term[...].astype(F32)
    grad_key = turned_heads(pairs[:, :KV_WIDTH], cosine[...], -sine[...]).astype(BF16)
    grad_value = pairs[:, KV_WIDTH:].astype(BF16)
    wait()
    kv_end = width + KV_WIDTH
    grad = (
        nt(grad_query[...], weight[:, :width])
        + nt(grad_key, weight[:, width:kv_end])
        + nt(grad_value, weight[:, kv_end : kv_end + KV_WIDTH])
    )
    x = tokens[...].astype(F32)
    scale = rms_scale(x)
    unit = x * scale
    stream_ref[...] = grad_hidden[...] + norm_back(unit, scale, grad, small[0:1])
    gains = jnp.concatenate([jnp.sum(grad * unit, axis=0, keepdims=True), gain_two[...]], axis=0)
    gains = jnp.concatenate([gains, jnp.zeros((14, width), F32)], axis=0).astype(BF16)
    targets = share_ref.shape[0]
    q_columns, kv_columns = width // targets, KV_WIDTH // targets
    for target in range(targets):
        q, kv = target * q_columns, target * kv_columns
        share_ref[target, :count, :q_columns] = grad_query[:, q : q + q_columns]
        kv_end = q_columns + 2 * kv_columns
        share_ref[target, :count, q_columns:kv_end] = jnp.concatenate(
            [grad_key[:, kv : kv + kv_columns], grad_value[:, kv : kv + kv_columns]], axis=1
        )
        share_ref[target, :count, kv_end:] = grad_hidden_low[:, q : q + q_columns]
        share_ref[target, count:, :q_columns] = gains[:, q : q + q_columns]
        share_ref[target, count:, q_columns:] = jnp.zeros(
            (16, share_ref.shape[2] - q_columns), BF16
        )
    for step, ref in enumerate(share_refs):
        ref[...] = share_ref[lax.rem(place[0] + step, targets)]


def term_kernel(place, *refs):
    *shares, normed_rows, mixed_rows, mine, other, share, terms, vectors = refs
    ctx_size, width = len(shares), normed_rows.shape[1]
    count = normed_rows.shape[0] // ctx_size
    chips, height = mine.shape[0], mine.shape[1] - 16
    devices = 2 * chips
    q_columns, kv_columns = width // ctx_size, KV_WIDTH // ctx_size
    kv_end = q_columns + 2 * kv_columns
    gains = jnp.zeros((16, q_columns), F32)
    for step, ref in enumerate(shares):
        source = lax.rem(place[0] - step + ctx_size, ctx_size)
        share[pl.ds(pl.multiple_of(source * count, count), count)] = ref[:count]
        gains = gains + ref[count:, :q_columns].astype(F32)
    terms[:, :kv_end] = tn(normed_rows[...], share[:, :kv_end])
    terms[:, kv_end:] = tn(mixed_rows[...], share[:, kv_end:])
    biases = jnp.sum(share[:, :kv_end].astype(F32), axis=0, keepdims=True)
    vectors[...] = jnp.zeros_like(vectors)
    parts = (gains[0:1], gains[1:2], biases[:, :q_columns])
    parts += (biases[:, q_columns : q_columns + kv_columns], biases[:, q_columns + kv_columns :])
    for f in range(devices):
        start = 0
        for part in parts:
            size = part.shape[1] // devices
            vectors[f : f + 1, start : start + size] = part[:, f * size : (f + 1) * size]
            start += size
    first = lax.broadcasted_iota(jnp.int32, (16, terms.shape[1]), 0) == 0
    for ref, core in ((mine, place[2]), (other, 1 - place[2])):
        for mask in range(chips):
            f = (place[1] ^ mask) * 2 + core
            start = pl.multiple_of(f * height, 64)
            ref[mask, :height] = terms[pl.ds(start, height)].astype(BF16)
            row = jnp.broadcast_to(vectors[pl.ds(f, 1)], first.shape)
            ref[mask, height:] = jnp.where(first, row, 0.0).astype(BF16)


def sum_cores_kernel(mine, got, keep, *sends):
    keep[...] = mine[0].astype(F32) + got[0].astype(F32)
    for mask, ref in enumerate(sends, 1):
        ref[...] = (mine[mask].astype(F32) + got[mask].astype(F32)).astype(BF16)


def sum_plane_kernel(keep, *refs):
    got, outs = refs[:3], refs[3:]
    total = keep[...] + got[0][...].astype(F32) + got[1][...].astype(F32) + got[2][...].astype(F32)
    height = total.shape[0] - 16
    start = 0
    for ref, turned in zip(outs[:4], (False, True, True, False)):
        size = ref.shape[0] if turned else ref.shape[1]
        part = total[:height, start : start + size]
        ref[...] = jnp.transpose(part) if turned else part
        start += size
    start = 0
    for ref in outs[4:]:
        ref[...] = total[height : height + 1, start : start + ref.shape[1]]
        start += ref.shape[1]


def small_call(body, arrays, out_shapes, scratch=(), place=None, cost=0):
    vmem = pl.BlockSpec(memory_space=pltpu.VMEM)
    smem = [] if place is None else [place]
    return pl.pallas_call(
        body,
        in_specs=[pl.BlockSpec(memory_space=pltpu.SMEM)] * len(smem) + [vmem] * len(arrays),
        out_specs=[vmem] * len(out_shapes),
        out_shape=[jax.ShapeDtypeStruct(shape, dtype) for shape, dtype in out_shapes],
        scratch_shapes=list(scratch),
        compiler_params=pltpu.CompilerParams(vmem_limit_bytes=56 * 2**20),
        cost_estimate=pl.CostEstimate(flops=cost, bytes_accessed=0, transcendentals=0),
    )(*smem, *arrays)


def per_device_plane_of_four(
    tokens,
    positions,
    norm1_gain,
    q_weight,
    q_bias,
    key_projection,
    key_bias_vector,
    value_projection,
    value_bias_vector,
    o_weight,
    norm2_gain,
    gate_weight,
    up_weight,
    down_weight,
    cotangent,
    *,
    links,
):
    ctx_size, fsdp_size = links.ctx_size, links.fsdp_size
    ctx, row_index = lax.axis_index("ctx"), lax.axis_index("fsdp")
    chip, core = row_index // 2, row_index % 2
    place = jnp.stack([ctx, chip, core])
    count, width = tokens.shape[1:]
    shard_rows = q_weight.shape[0]
    even = core == 0
    steps = range(1, ctx_size)

    def column(x):
        return jnp.pad(x, (0, shard_rows - x.shape[0]))[:, None]

    extra = jnp.concatenate(
        [
            column(x)
            for x in (norm1_gain, q_bias, norm2_gain, key_bias_vector, value_bias_vector)
        ],
        axis=1,
    )
    extra = jnp.pad(extra, ((0, 0), (0, 128 - extra.shape[1])))
    packed = jnp.concatenate([q_weight, key_projection, value_projection, extra, o_weight], axis=1)
    links.label = "qkvo_ctx"
    packed_got = [links.turn(packed, step) for step in steps]

    mine, other = split_hidden(
        links, place, (gate_weight, up_weight, jnp.transpose(down_weight))
    )
    links.label = "ff_core"
    got = links.core(other)

    def for_ctx(step):
        target = (ctx + step) % ctx_size
        a, b = pick(mine, target), pick(got, target)
        return jnp.stack([jnp.where(even, a, b), jnp.where(even, b, a)])

    packed_got, (mine, got) = phase(packed_got, (mine, got))
    packed_mine = jnp.stack([packed] + packed_got)
    links.label = "qkvo_plane1"
    packed_stage = plane_start(links, packed_mine)
    links.label = "ff_ctx_a"
    near_steps, far_steps = (1, ctx_size - 1), tuple(range(2, ctx_size - 1))
    near = [links.turn(for_ctx(step), step) for step in near_steps]
    far = [for_ctx(step) for step in far_steps]
    links.label = "qkvo_core"
    packed_stage, near, far, (own_piece, early) = phase(
        packed_stage, near, far, (for_ctx(0), links.core(packed_mine))
    )
    links.label = "ff_ctx_b"
    far = [links.turn(piece, step) for step, piece in zip(far_steps, far)]
    links.label = "qkvo_plane2"
    packed_parts = plane_end(links, packed_mine, *packed_stage)
    links.label = "ff_own1"
    own_stage = plane_start(links, own_piece)
    near, far, late, own_stage = phase(near, far, packed_parts[3:], own_stage)
    links.label = "qkvo_core"
    pieces = [*packed_parts[:3], *late, early]
    pieces.append(links.core(jnp.concatenate([*packed_parts[1:3], *late])))
    sizes, qkv_columns = (ctx_size, fsdp_size // 2), packed.shape[1] - width
    weight_qkv = Rows(sizes, pieces, rows_layout(ctx_size), 0, qkv_columns)
    weight_o = Rows(sizes, pieces, rows_layout(ctx_size), qkv_columns, width)
    links.label = "ff_plane1"
    moved = dict(zip(near_steps + far_steps, near + far))
    moved_piece = jnp.concatenate([moved[step] for step in steps])
    moved_stage = plane_start(links, moved_piece)

    low_tokens, out_low = tokens[0], cotangent[0]
    cosine, sine = (x[:, 0] for x in angle_tables(positions[0]))
    cosine = jnp.concatenate([cosine, cosine], axis=1)
    sine = jnp.concatenate([-sine, sine], axis=1)
    place_column = positions[0][:, None]
    wide, narrow = (count, width), (count, 2 * KV_WIDTH)

    def qkv(*refs):
        qkv_body(shard_rows, *refs)

    normed_one, query, pairs, small = call(
        qkv,
        place,
        (low_tokens, cosine, sine),
        weight_qkv,
        [(wide, BF16), (wide, BF16), (narrow, BF16), ((8, width), F32)],
        0,
    )
    links.label = "kv"
    blocks = [pairs] + [links.shift(pairs, step) for step in steps]
    mixed_low, hidden_one, normed_two = call(
        mix_body,
        place,
        (low_tokens, small, place_column, query, *blocks),
        weight_o,
        [(wide, BF16), (wide, F32), (wide, BF16)],
        0,
    )

    out_row = lax.all_gather(after(out_low, *far), "ctx", axis=0, tiled=True)
    normed_row = lax.all_gather(normed_two, "ctx", axis=0, tiled=True)
    links.label = "gy_core"
    out_other = links.core(out_row)
    links.label = "ff_plane2"
    half = ctx_size - 1
    last = [
        links.plane(jnp.concatenate([moved_stage[1][:half], own_stage[1][:1]]), 2),
        links.plane(jnp.concatenate([moved_stage[0][half:], own_stage[0][1:]]), 4),
    ]
    own_entries = [(0, 0), (0, 1)]
    entries = [(step, core) for step in steps for core in range(2)]
    layout = [(own_entries, mask, x) for mask, x in enumerate((own_piece, *own_stage))]
    layout += [(entries, mask, x) for mask, x in enumerate((moved_piece, *moved_stage))]
    layout += [
        (entries[:half] + own_entries[:1], 3, last[0]),
        (entries[half:] + own_entries[1:], 3, last[1]),
    ]
    links.label = "n2_core"
    normed_other = links.core(after(normed_row, *last, out_other))
    block = own_piece.shape[3]
    ff_widths = (block, block, block, width)
    act_a, gate_a, up_a, down_a = ff_call(
        links, ff_kernel, layout, place, (normed_row, out_row), ff_widths, 3
    )
    normed_other = after(normed_other, act_a)
    act_b, gate_b, up_b, down_b = ff_call(
        links, ff_kernel, layout, place, (normed_other, out_other), ff_widths, 3
    )
    links.label = "gn2_core"
    down_got = links.core(down_b)
    normed_rows = lax.all_gather(after(normed_one, normed_row), "ctx", axis=0, tiled=True)
    grad_normed_two = lax.psum_scatter(
        after(added(down_a, down_got), normed_rows), "ctx", scatter_dimension=0, tiled=True
    )

    rights = (gate_a, gate_b, up_a, up_b, act_a, act_b)
    lefts = (after(normed_row, down_got), normed_other, out_row, out_other)
    send_terms = ff_grad_terms(place, lefts, rights, lambda j: 2 + j, lambda j: 1 + 2 * j, (1, 2))
    links.label = "ff_sum1"
    ff_first = reduce_start(links, send_terms)
    links.label = "y_core"
    y_a, y_b = ff_call(
        links, y_kernel, layout, place, (after(act_a, *send_terms), act_b), (width, width), 1
    )
    y_got = links.core(y_b)
    grad_normed_two = after(grad_normed_two, y_b, *ff_first[::2])

    def mix_back(*refs):
        mix_back_body(1, *refs)

    grad_hidden, grad_hidden_low, grad_query, gain_two, *pair_terms = call(
        mix_back,
        place,
        (grad_normed_two, hidden_one, small, out_low, place_column, query, cosine, sine, *blocks),
        weight_o,
        [(wide, F32), (wide, BF16), (wide, BF16), ((1, width), F32)] + [(narrow, BF16)] * ctx_size,
        BACK_COST,
    )
    links.label = "y_core"
    mixed_rows = lax.all_gather(
        after(mixed_low, grad_normed_two), "ctx", axis=0, tiled=True
    )
    lefts = (after(normed_row, grad_hidden_low, y_got), *lefts[1:])
    ff_terms = ff_grad_terms(place, lefts, rights, lambda j: j, lambda j: 2 * j, (3,))
    links.label = "gkv"
    pair_terms = [pair_terms[0]] + [links.shift(pair_terms[step], -step) for step in steps]
    pair_terms[0] = after(pair_terms[0], ff_terms[0])
    def columns_over_ctx(parts):
        whole = jnp.zeros_like(parts)
        whole = lax.dynamic_update_index_in_dim(whole, pick(parts, ctx), ctx, 0)
        for step in steps:
            piece = links.turn(pick(parts, (ctx + step) % ctx_size), step)
            whole = lax.dynamic_update_index_in_dim(whole, piece, (ctx - step) % ctx_size, 0)
        return whole

    def qkv_back(*refs):
        qkv_back_body(ctx_size, *refs)

    columns = (width + 2 * KV_WIDTH) // ctx_size
    share_shape = (count + 16, columns + width // ctx_size)
    grad_stream, *shares = call(
        qkv_back,
        place,
        (*pair_terms, low_tokens, small, cosine, sine, grad_query, grad_hidden, grad_hidden_low, gain_two),
        weight_qkv,
        [(wide, F32)] + [(share_shape, BF16)] * ctx_size,
        0,
        [pltpu.VMEM((ctx_size, *share_shape), BF16)],
    )

    links.label = "gqkv_ctx"
    first_share = shares[0]
    shares = [first_share] + [links.turn(shares[step], step) for step in steps]
    shares[0] = after(shares[0], *ff_first)
    y_both = after(added(y_a, y_got), *shares[1:])
    y_sum = lax.psum_scatter(y_both, "ctx", scatter_dimension=0, tiled=True)
    links.label = "ff_sum2"
    ff_second = reduce_next(links, ff_terms, phase(ff_first, (first_share,))[0])
    chips = fsdp_size // 2
    term_shape = (chips, width // fsdp_size + 16, share_shape[1])
    term_mine, term_other = small_call(
        term_kernel,
        (*shares, normed_rows, mixed_rows),
        [(term_shape, BF16)] * 2,
        [
            pltpu.VMEM((ctx_size * count, share_shape[1]), BF16),
            pltpu.VMEM((width, share_shape[1]), F32),
            pltpu.VMEM((fsdp_size, share_shape[1]), F32),
        ],
        place,
    )
    links.label = "term_core"
    ff_send = reduce_end(place, ff_terms, ff_first, ff_second, 1, BF16, 12 * 10**9)
    term_mine = after(term_mine, ff_send)
    keep, *sends = small_call(
        sum_cores_kernel,
        (term_mine, links.core(term_other)),
        [(term_shape[1:], F32)] + [(term_shape[1:], BF16)] * (chips - 1),
    )
    links.label = "term_plane"
    q_columns, kv_columns = width // ctx_size, KV_WIDTH // ctx_size
    height, devices = width // fsdp_size, ctx_size * fsdp_size
    plane_got = [links.plane(x, 2 * mask) for mask, x in enumerate(sends, 1)]
    grad_q, grad_k, grad_v, grad_o, *vectors = small_call(
        sum_plane_kernel,
        (keep, *plane_got),
        [((height, q_columns), F32)]
        + [((kv_columns, height), F32)] * 2
        + [((height, q_columns), F32)]
        + [((1, x // devices), F32) for x in (width, width, width, KV_WIDTH, KV_WIDTH)],
        cost=0,
    )
    vectors = [x[0] for x in vectors]

    links.label = "final_core"
    ff_second = phase(ff_second, sends)[0]
    ff_mine = reduce_end(place, ff_terms, ff_first, ff_second, 0, F32, 0)
    hidden = 2 * ff_mine.shape[2]
    grad_gate, grad_up, grad_down = small_call(
        join_cores_kernel,
        (ff_mine, after(links.core(ff_send), *sends)),
        [((height, hidden), F32)] * 3,
        place=place,
        cost=2*10**9,
    )

    layer_out = hidden_one + after(y_sum, grad_gate).astype(F32)

    return (
        layer_out[None],
        grad_stream[None],
        vectors[0],
        grad_q,
        vectors[2],
        jnp.transpose(grad_k),
        vectors[3],
        jnp.transpose(grad_v),
        vectors[4],
        grad_o,
        vectors[1],
        grad_gate,
        grad_up,
        jnp.transpose(grad_down),
    )


def solution(mesh):
    links = Links(mesh.shape["ctx"], mesh.shape["fsdp"])
    vector, matrix, stream = P(BOTH), P(BOTH, None), P("fsdp", "ctx", None)
    grid = P("fsdp", "ctx")
    in_specs = (
        stream,
        grid,
        vector,
        matrix,
        vector,
        matrix,
        vector,
        matrix,
        vector,
        matrix,
        vector,
        matrix,
        matrix,
        P(None, BOTH),
        stream,
    )
    out_specs = (
        stream,
        stream,
        vector,
        grid,
        vector,
        grid,
        vector,
        grid,
        vector,
        grid,
        vector,
        grid,
        grid,
        P("ctx", "fsdp"),
    )

    def run(*arrays):
        plane_of_four = mesh.shape["fsdp"] == 8 and arrays[3].shape[0] % 16 == 0
        form = per_device_plane_of_four if plane_of_four else per_device_any_mesh
        return form(*arrays, links=links)

    return jax.shard_map(run, mesh=mesh, in_specs=in_specs, out_specs=out_specs, check_vma=False)
```
